32 devices in a mesh: dp: 32 (over z, y, x, core).
Axes of the slice: x: 2, y: 2, z: 4, core: 2. Of those that a mesh axis runs over, the one named last changes fastest.
Arguments:
- tokens: bfloat16 [512, 128, 512], P('dp'), may hold values from -6 to 6
- memory: bfloat16 [512, 32, 512], P(None, 'dp'), may hold values from -6 to 6
- target_lengths: int32 [512], P('dp'), may hold values from 16 to 128, as said below
- memory_lengths: int32 [512], P('dp'), may hold values from 16 to 32, as said below
- grad_output: bfloat16 [512, 128, 512], P('dp'), may hold values from -6 to 6
- gain_self: float32 [512], replicated, may hold values from 0.5 to 1.5
- w_qkv: bfloat16 [512, 1536], replicated, may hold values from -0.25 to 0.25
- w_self_out: bfloat16 [512, 512], replicated, may hold values from -1.5 to 1.5
- gain_cross: float32 [512], replicated, may hold values from 0.5 to 1.5
- w_cross_query: bfloat16 [512, 512], replicated, may hold values from -0.25 to 0.25
- w_cross_kv: bfloat16 [512, 1024], replicated, may hold values from -0.25 to 0.25
- w_cross_out: bfloat16 [512, 512], replicated, may hold values from -1.5 to 1.5
- gain_ffn: float32 [512], replicated, may hold values from 0.5 to 1.5
- w_expand: bfloat16 [512, 2048], replicated, may hold values from -0.25 to 0.25
- w_contract: bfloat16 [2048, 512], replicated, may hold values from -0.125 to 0.125
Outputs:
- output: bfloat16 [512, 128, 512], P('dp')
- grad_tokens: bfloat16 [512, 128, 512], P('dp')
- grad_memory: bfloat16 [512, 32, 512], P(None, 'dp')
- grad_gain_self: float32 [512], replicated
- grad_w_qkv: float32 [512, 1536], replicated
- grad_w_self_out: float32 [512, 512], replicated
- grad_gain_cross: float32 [512], replicated
- grad_w_cross_query: float32 [512, 512], replicated
- grad_w_cross_kv: float32 [512, 1024], replicated
- grad_w_cross_out: float32 [512, 512], replicated
- grad_gain_ffn: float32 [512], replicated
- grad_w_expand: float32 [512, 2048], replicated
- grad_w_contract: float32 [2048, 512], replicated
The draws below stay inside these ranges and needn't reach their ends.
Inputs may be any that keep to these rules, and one draw needn't show every extreme that they name: `target_lengths`: the 16 sequences of one device lie in one length bucket: from c // 2 to c with c = k * 32 for a k of 1 to 4, and one of them has exactly c tokens; some device has c = 128. `memory_lengths`: among the 16 sequences of each device one has exactly 32 memory tokens.
All inputs are finite; a program needn't handle non-finite values.
Results may differ from the reference program's by a relative error of at most 0.017.
Values may be sent and summed in bfloat16 or wider, within the bound.
No kernel may reach another device: no remote copies, remote signals or barrier semaphores. Data moves between devices by JAX's collectives and lax.ppermute only.
A program may use at most 256 MiB of HBM per device.

```python
import jax
import jax.numpy as jnp
from jax import lax

D = 512
HEADS = 8
HEAD = 64
FF = 2048
SEQ_DEV = 16
L = 128
SEQS = 512
LM = 32


def draw_target_lengths(key, part):
    key = jax.random.fold_in(key, 11)
    devices = SEQS // SEQ_DEV
    bucket = jax.random.randint(jax.random.fold_in(key, 1), (devices,), 0, 4)
    chosen = jax.random.randint(jax.random.fold_in(key, 2), (), 0, devices)
    bucket = jnp.where(jnp.arange(devices) == chosen, 3, bucket)
    ceiling = L * (bucket + 1) // 4
    floor_len = ceiling // 2
    ceiling_each = jnp.repeat(ceiling, SEQ_DEV)
    floor_each = jnp.repeat(floor_len, SEQ_DEV)
    random_bits = jax.random.randint(jax.random.fold_in(key, 3), (SEQS,), 0, 1 << 20)
    drawn = floor_each + random_bits % (ceiling_each - floor_each + 1)
    slot_pick = jax.random.randint(jax.random.fold_in(key, 4), (devices,), 0, SEQ_DEV)
    longest = jnp.arange(SEQS) % SEQ_DEV == jnp.repeat(slot_pick, SEQ_DEV)
    return jnp.where(longest, ceiling_each, drawn).astype(jnp.int32)


def draw_memory_lengths(key, part):
    key = jax.random.fold_in(key, 23)
    devices = SEQS // SEQ_DEV
    drawn = jax.random.randint(jax.random.fold_in(key, 1), (SEQS,), LM // 2, LM + 1)
    slot_pick = jax.random.randint(jax.random.fold_in(key, 2), (devices,), 0, SEQ_DEV)
    longest = jnp.arange(SEQS) % SEQ_DEV == jnp.repeat(slot_pick, SEQ_DEV)
    return jnp.where(longest, LM, drawn).astype(jnp.int32)


def block_levels(stream_key, dims, cuts, least, high):
    level = 1.0
    for dim, blocks in cuts:
        heights = jax.random.uniform(jax.random.fold_in(jax.random.fold_in(stream_key, 6), dim), (blocks,), jnp.float32, least / len(cuts), high / len(cuts))
        level = level * jnp.repeat(jnp.exp(heights), dims[dim] // blocks).reshape((-1,) + (1,) * (len(dims) - 1 - dim))
    return level


def gaussian(own_key, dims, scale, reach, shards=(), kind=jnp.bfloat16):
    loudness = block_levels(own_key, dims, shards, -0.22, 0.18) if shards else 1.0
    values = jax.random.normal(own_key, dims, jnp.float32) * scale * loudness
    return jnp.minimum(jnp.maximum(values, -reach), reach).astype(kind)


def setup_inputs(seed: int = 0) -> dict:
    key_of = jax.random.split(jax.random.key(seed), 16)
    tokens = gaussian(key_of[0], (SEQS, L, D), 1.0, 6.0, ((0, 32),))
    memory = gaussian(key_of[1], (SEQS, LM, D), 1.0, 6.0, ((1, 32),))
    target_lengths = draw_target_lengths(jax.random.fold_in(key_of[15], 71), 0)
    memory_lengths = draw_memory_lengths(jax.random.fold_in(key_of[15], 71), 0)
    grad_output = gaussian(key_of[4], (SEQS, L, D), 1.0, 6.0, ((0, 32),))
    gain_self = jnp.clip(1.0 + 0.1 * jax.random.normal(key_of[5], (D,), jnp.float32), 0.5, 1.5)
    w_qkv = gaussian(key_of[6], (D, 3 * D), D ** -0.5, 0.25)
    w_self_out = gaussian(key_of[7], (D, D), (D // 32) ** -0.5, 1.5)
    gain_cross = jnp.clip(1.0 + 0.1 * jax.random.normal(key_of[8], (D,), jnp.float32), 0.5, 1.5)
    w_cross_query = gaussian(key_of[9], (D, D), D ** -0.5, 0.25)
    w_cross_kv = gaussian(key_of[10], (D, 2 * D), D ** -0.5, 0.25)
    w_cross_out = gaussian(key_of[11], (D, D), (D // 32) ** -0.5, 1.5)
    gain_ffn = jnp.clip(1.0 + 0.1 * jax.random.normal(key_of[12], (D,), jnp.float32), 0.5, 1.5)
    w_expand = gaussian(key_of[13], (D, FF), D ** -0.5, 0.25)
    w_contract = gaussian(key_of[14], (FF, D), FF ** -0.5, 0.125)
    return {"tokens": tokens, "memory": memory, "target_lengths": target_lengths, "memory_lengths": memory_lengths, "grad_output": grad_output, "gain_self": gain_self, "w_qkv": w_qkv, "w_self_out": w_self_out, "gain_cross": gain_cross, "w_cross_query": w_cross_query, "w_cross_kv": w_cross_kv, "w_cross_out": w_cross_out, "gain_ffn": gain_ffn, "w_expand": w_expand, "w_contract": w_contract}


epsilon = 1e-05
big_negative = -1e+30
exact = lax.Precision.HIGHEST

@jax.custom_vjp
def low(v):
    return lax.optimization_barrier(v.astype(jnp.bfloat16)).astype(jnp.float32)

@jax.custom_vjp
def low_back(v):
    return v

def low_keep(v):
    return (low(v), None)

def low_pass(kept, grad):
    return (grad,)

def back_keep(v):
    return (v, None)

def back_low(kept, grad):
    return (low(grad),)
low.defvjp(low_keep, low_pass)
low_back.defvjp(back_keep, back_low)

def rounded_both(values):
    return low(low_back(values))

def product_exact(left_side, right_side):
    return jnp.dot(left_side, right_side, precision=exact)

def layer_norm(hidden, gain_vector):
    centred = hidden - lax.optimization_barrier(jnp.mean(hidden, axis=-1, keepdims=True))
    return centred * lax.rsqrt(lax.optimization_barrier(jnp.mean(centred * centred, axis=-1, keepdims=True)) + epsilon) * gain_vector

def attention(queries, keys, values, allowed):
    scores = jnp.einsum('sqhe,skhe->shqk', queries, keys, precision=exact) * HEAD ** (-0.5)
    scores = low_back(scores)
    scores = jnp.where(allowed[:, None], scores, big_negative)
    row_max = lax.optimization_barrier(jnp.max(scores, axis=-1, keepdims=True))
    exponentials = jnp.exp(scores - row_max)
    soft_weights = low(exponentials / lax.optimization_barrier(jnp.sum(exponentials, axis=-1, keepdims=True)))
    return jnp.einsum('shqk,skhe->sqhe', soft_weights, values, precision=exact)

def forward(inputs_now, memory_now, target_now, memory_len_now, weights_now):
    gain_self, w_qkv, w_self_out, gain_cross, w_cross_query, w_cross_kv, w_cross_out, gain_ffn, w_expand, w_contract = weights_now
    seq_count = inputs_now.shape[0]
    mem_total = memory_now.shape[1]
    row_count = seq_count * L
    position = jnp.arange(L)
    self_allowed = (position[None, :, None] >= position[None, None, :]) & (position[None, None, :] < target_now[:, None, None])
    cross_allowed = jnp.arange(mem_total)[None, None, :] < memory_len_now[:, None, None]
    residual = inputs_now.reshape(row_count, D)
    act_one = low(layer_norm(residual, gain_self))
    triple = rounded_both(product_exact(act_one, w_qkv))
    queries = triple[:, :D].reshape(seq_count, L, HEADS, HEAD)
    keys = triple[:, D:2 * D].reshape(seq_count, L, HEADS, HEAD)
    values = triple[:, 2 * D:].reshape(seq_count, L, HEADS, HEAD)
    attended = rounded_both(attention(queries, keys, values, self_allowed).reshape(row_count, D))
    residual = residual + low_back(product_exact(attended, w_self_out))
    act_two = low(layer_norm(residual, gain_cross))
    cross_queries = rounded_both(product_exact(act_two, w_cross_query)).reshape(seq_count, L, HEADS, HEAD)
    pairs = rounded_both(product_exact(memory_now.reshape(seq_count * mem_total, D), w_cross_kv))
    cross_keys = pairs[:, :D].reshape(seq_count, mem_total, HEADS, HEAD)
    cross_values = pairs[:, D:].reshape(seq_count, mem_total, HEADS, HEAD)
    cross_out = rounded_both(attention(cross_queries, cross_keys, cross_values, cross_allowed).reshape(row_count, D))
    residual = residual + low_back(product_exact(cross_out, w_cross_out))
    act_three = low(layer_norm(residual, gain_ffn))
    expanded = low_back(product_exact(act_three, w_expand))
    activated = low(jax.nn.gelu(expanded, approximate=False))
    residual = residual + low_back(product_exact(activated, w_contract))
    return residual.reshape(seq_count, L, D)

def reference(tokens, memory, target_lengths, memory_lengths, grad_output, gain_self, w_qkv, w_self_out, gain_cross, w_cross_query, w_cross_kv, w_cross_out, gain_ffn, w_expand, w_contract):
    weights_all = tuple((matrix.astype(jnp.float32) for matrix in (gain_self, w_qkv, w_self_out, gain_cross, w_cross_query, w_cross_kv, w_cross_out, gain_ffn, w_expand, w_contract)))
    group_size = 32 if SEQS % 32 == 0 else SEQS
    group_count = SEQS // group_size

    def by_group(array_in):
        return array_in.reshape((group_count, group_size) + array_in.shape[1:])
    position = jnp.arange(L)
    in_sequence = (position[None, :] < target_lengths[:, None]).astype(jnp.float32)
    cotangent = grad_output.astype(jnp.float32) * in_sequence[:, :, None]

    def one_group(summed, block_args):
        inputs_now, memory_now, target_now, memory_len_now, cotangent_now = block_args

        def apply_layer(inputs_here, memory_here, weights_here):
            return forward(inputs_here, memory_here, target_now, memory_len_now, weights_here)
        result, pullback = jax.vjp(apply_layer, inputs_now.astype(jnp.float32), memory_now.astype(jnp.float32), weights_all)
        grad_inputs, grad_mem, grad_weights = pullback(cotangent_now)
        summed = jax.tree.map(lambda first_term, second_term: first_term + second_term, summed, grad_weights)
        return (summed, (result.astype(jnp.bfloat16), grad_inputs.astype(jnp.bfloat16), grad_mem.astype(jnp.bfloat16)))
    starting = jax.tree.map(jnp.zeros_like, weights_all)
    totals, (results, grad_inputs, grad_mem) = lax.scan(one_group, starting, (by_group(tokens), by_group(memory), by_group(target_lengths), by_group(memory_lengths), by_group(cotangent)))
    output = results.reshape(SEQS, L, D)
    grad_tokens = grad_inputs.reshape(SEQS, L, D)
    grad_memory = grad_mem.reshape(SEQS, LM, D)
    return (output, grad_tokens, grad_memory, totals[0], totals[1], totals[2], totals[3], totals[4], totals[5], totals[6], totals[7], totals[8], totals[9])
```

```python
import functools
import jax
import jax.numpy as jnp
from jax import lax
from jax.experimental import pallas as pl
from jax.experimental.pallas import tpu as pltpu
from jax.sharding import PartitionSpec as P

HEAD = 64
PAIR = 128
epsilon = 1e-05
big_negative = -1e30
f32 = jnp.float32
bf16 = jnp.bfloat16
VMEM_LIMIT = 24
HBM = pltpu.HBM
VMEM = pltpu.VMEM


def dot(left, right, left_dim=1, right_dim=0):
    return lax.dot_general(
        left, right, (((left_dim,), (right_dim,)), ((), ())), preferred_element_type=f32
    )


def normalize(hidden):
    centred = hidden - jnp.mean(hidden, axis=-1, keepdims=True)
    spread = lax.rsqrt(jnp.mean(centred * centred, axis=-1, keepdims=True) + epsilon)
    return centred * spread, spread


def norm_backward(gradient, gain, normalized, spread):
    scaled = gradient * gain
    first = jnp.mean(scaled, axis=-1, keepdims=True)
    second = jnp.mean(scaled * normalized, axis=-1, keepdims=True)
    return spread * (scaled - first - normalized * second)


def head_masks(rows):
    lane = lax.broadcasted_iota(jnp.int32, (rows, PAIR), 1)
    first = jnp.where(lane < HEAD, 1.0, 0.0).astype(bf16)
    second = jnp.where(lane >= HEAD, 1.0, 0.0).astype(bf16)
    return first, second


def spread_pair(block, first, second):
    return jnp.concatenate([block * first, block * second], axis=0)


def stack_pair(block):
    half = block.shape[1] // 2
    return jnp.concatenate([block[:, :half], block[:, half:]], axis=0)


def wide_mask(mem_total, width):
    lane = lax.broadcasted_iota(jnp.int32, (mem_total, width), 1)
    parts = [
        jnp.where((lane >= h * HEAD) & (lane < (h + 1) * HEAD), 1.0, 0.0)
        for h in range(width // HEAD)
    ]
    return parts


PARTS = 1
LAG = 1


def stagger(parts):
    waiting = [LAG * n for n in range(len(parts))]
    while parts:
        left = []
        for n, part in enumerate(parts):
            if waiting[n]:
                waiting[n] -= 1
                left.append(n)
            elif next(part, part) is not part:
                left.append(n)
        parts, waiting = [parts[n] for n in left], [waiting[n] for n in left]


def self_forward_kernel(
    seqs, length, width,
    bits, lengths, tokens, gain_self, w_qkv, w_out, gain_cross, w_query,
    act, triple, weights, attended, mid, queries,
):
    step = pl.program_id(0)
    first, second = head_masks(length)
    key_at = lax.broadcasted_iota(jnp.int32, (length, 2 * length), 0)
    query_at = lax.broadcasted_iota(jnp.int32, (length, 2 * length), 1)
    query_at = jnp.where(query_at >= length, query_at - length, query_at)
    causal = key_at <= query_at
    count = seqs // PARTS

    def part(n):
        span = slice(n * count * length, (n + 1) * count * length)
        residual = tokens[span, :].astype(f32)
        normal, _ = normalize(residual)
        low = (normal * gain_self[...]).astype(bf16)
        yield
        both = dot(low, w_qkv[...]).astype(bf16)
        yield
        heads = [(s, p) for s in range(count) for p in range(width // PAIR)]
        scores = []
        for s, p in heads:
            rows = slice(s * length, (s + 1) * length)
            q = both[rows, p * PAIR : (p + 1) * PAIR] * 0.125
            k = both[rows, width + p * PAIR : width + (p + 1) * PAIR]
            scores.append(dot(k, spread_pair(q, first, second), 1, 1))
        yield
        softs = []
        for (s, p), score in zip(heads, scores):
            allowed = causal & (key_at < lengths[step * seqs + n * count + s])
            score = jnp.where(allowed, score, big_negative)
            raised = jnp.exp(score - jnp.max(score, axis=0, keepdims=True))
            softs.append((raised * (1.0 / jnp.sum(raised, axis=0, keepdims=True))).astype(bf16))
        yield
        joined = {}
        for (s, p), soft in zip(heads, softs):
            rows = slice(s * length, (s + 1) * length)
            v = both[rows, 2 * width + p * PAIR : 2 * width + (p + 1) * PAIR]
            joined[s, p] = dot(stack_pair(soft), spread_pair(v, first, second), 0, 0).astype(bf16)
        yield
        out = jnp.concatenate(
            [
                jnp.concatenate([joined[s, p] for p in range(width // PAIR)], axis=1)
                for s in range(count)
            ],
            axis=0,
        )
        residual = residual + dot(out, w_out[...])
        yield
        normal, _ = normalize(residual)
        after = (normal * gain_cross[...]).astype(bf16)
        yield
        found = dot(after, w_query[...]).astype(bf16)
        yield
        act[span, :] = low
        triple[span, :] = both
        attended[span, :] = out
        mid[span, :] = residual.astype(bf16)
        queries[span, :] = found
        for (s, p), soft in zip(heads, softs):
            weights[n * count + s, p] = soft

    stagger([part(n) for n in range(PARTS)])


def cross_forward_kernel(
    seqs, length, width, mem_total,
    bits, lengths, memory_lengths, raw, queries, mid, grad_output, w_kv, w_out, gain_ffn,
    arrived, pairs, weights, cross, late, grad_low, late_near, grad_low_near, act,
):
    step = pl.program_id(0)
    total = raw.shape[0] // mem_total
    at = lax.broadcasted_iota(jnp.int32, (mem_total, raw.shape[0]), 0) * total
    column = lax.broadcasted_iota(jnp.int32, (mem_total, raw.shape[0]), 1)
    own_rows = jnp.concatenate(
        [jnp.where(column == at + (step * seqs + s), 1.0, 0.0).astype(bf16) for s in range(seqs)],
        axis=0,
    )
    own_rows = dot(own_rows, raw[...]).astype(bf16)
    arrived[...] = own_rows
    both = dot(own_rows, w_kv[...]).astype(bf16)
    pairs[...] = both
    mask = jnp.concatenate(wide_mask(mem_total, width), axis=0).astype(bf16)
    heads = width // HEAD
    key_at = lax.broadcasted_iota(jnp.int32, (mem_total, length), 0)
    row_at = lax.broadcasted_iota(jnp.int32, (length, width), 0)

    def spread(s, at):
        return jnp.concatenate([both[s * mem_total : (s + 1) * mem_total, at]] * heads, axis=0) * mask

    scores = []
    for s in range(seqs):
        q = queries[s * length : (s + 1) * length, :] * 0.125
        scores.append(dot(spread(s, slice(0, width)), q, 1, 1).reshape(heads, mem_total, length))
    softs = []
    for s in range(seqs):
        allowed = (key_at < memory_lengths[step * seqs + s])[None]
        score = jnp.where(allowed, scores[s], big_negative)
        raised = jnp.exp(score - jnp.max(score, axis=1, keepdims=True))
        soft = raised * (1.0 / jnp.sum(raised, axis=1, keepdims=True))
        softs.append(soft.reshape(heads * mem_total, length).astype(bf16))
    joined = [dot(softs[s], spread(s, slice(width, 2 * width)), 0, 0).astype(bf16) for s in range(seqs)]
    low = jnp.concatenate(joined, axis=0)
    cross[...] = low
    for s in range(seqs):
        rows = slice(s * length, (s + 1) * length)
        weights[s] = softs[s]
        live = row_at < lengths[step * seqs + s]
        masked = jnp.where(live, grad_output[rows, :].astype(f32), 0.0).astype(bf16)
        grad_low[rows, :] = masked
        grad_low_near[rows, :] = masked
    residual = mid[...].astype(f32) + dot(low, w_out[...])
    late[...] = residual.astype(bf16)
    late_near[...] = residual.astype(bf16)
    normal, _ = normalize(residual)
    act[...] = (normal * gain_ffn[...]).astype(bf16)


def gelu_parts(value):
    half = 0.5 + 0.5 * lax.erf(value * 0.7071067811865476)
    bell = value * jnp.exp2(value * value * (-0.5 * 1.4426950408889634))
    return value * half, half + 0.3989422804014327 * bell


def ffn_kernel(
    row_block,
    bits, act, grad_low, start, w_expand, w_contract,
    result, grad_normed, send, keep,
    activated, grad_expanded, total, change,
):
    step = pl.program_id(0)
    rows = act.shape[0]
    chunk = w_expand.shape[1]

    @pl.when(step == 0)
    def _():
        total[...] = start[...].astype(f32)
        change[...] = jnp.zeros_like(change)

    for b in range(rows // row_block):
        r = slice(b * row_block, (b + 1) * row_block)
        expanded = dot(act[r, :], w_expand[...])
        grad_activated = dot(grad_low[r, :], w_contract[...], 1, 1)
        value, slope = gelu_parts(expanded)
        value = value.astype(bf16)
        slope = (grad_activated * slope).astype(bf16)
        activated[r, :] = value
        grad_expanded[r, :] = slope
        total[r, :] += dot(value, w_contract[...])
        change[r, :] += dot(slope, w_expand[...], 1, 1)

    def fill(grads):
        grads[:chunk, :] = dot(activated[...], grad_low[...], 0, 0).astype(bf16)
        grads[chunk:, :] = dot(act[...], grad_expanded[...], 0, 0).astype(bf16)

    @pl.when(step < pl.num_programs(0) // 2)
    def _():
        fill(send)

    @pl.when(step >= pl.num_programs(0) // 2)
    def _():
        fill(keep)

    @pl.when(step == pl.num_programs(0) - 1)
    def _():
        result[...] = total[...].astype(bf16)
        grad_normed[...] = change[...].astype(bf16)


def give_halves(core, total, send, keep, height):
    half = height // 2
    for n in range(total.shape[0] // height):
        at = pl.ds(pl.multiple_of(n * height + (1 - core) * half, half), half)
        send[n * half : (n + 1) * half, :] = total[at, :].astype(bf16)
        at = pl.ds(pl.multiple_of(n * height + core * half, half), half)
        keep[n * half : (n + 1) * half, :] = total[at, :].astype(bf16)


def cross_backward_kernel(
    seqs, length, width, mem_total,
    bits, grad_normed, late, grad_low, cross, weights, pairs, queries, mid, arrived, attended,
    w_out, w_query, w_kv, gain_ffn, gain_cross,
    gradient, grad_arrived, send, keep,
    total, grad_rows,
):
    step = pl.program_id(0)

    @pl.when(step == 0)
    def _():
        total[...] = jnp.zeros_like(total)

    normal, spread = normalize(late[...].astype(f32))
    change = norm_backward(
        grad_normed[...].astype(f32), gain_ffn[...], normal, spread
    )
    running = grad_low[...].astype(f32) + change
    low = running.astype(bf16)
    total[:width, :] += dot(cross[...], low, 0, 0)
    grad_cross = dot(low, w_out[...], 1, 1).astype(bf16)
    masks = wide_mask(mem_total, width)
    mask = jnp.concatenate(masks, axis=0).astype(bf16)
    heads = width // HEAD

    def widen(s, at):
        return jnp.concatenate([pairs[s * mem_total : (s + 1) * mem_total, at]] * heads, axis=0) * mask

    def narrow(block):
        return sum(block[h * mem_total : (h + 1) * mem_total, :] * masks[h] for h in range(heads))

    softs = [weights[s] for s in range(seqs)]
    grads = [grad_cross[s * length : (s + 1) * length, :] for s in range(seqs)]
    values = [dot(softs[s], grads[s]) for s in range(seqs)]
    changes = [
        dot(widen(s, slice(width, 2 * width)), grads[s], 1, 1).reshape(heads, mem_total, length)
        for s in range(seqs)
    ]
    scores = []
    for s in range(seqs):
        soft = softs[s].astype(f32).reshape(heads, mem_total, length)
        product = soft * changes[s]
        score = product - soft * jnp.sum(product, axis=1, keepdims=True)
        scores.append(score.reshape(heads * mem_total, length).astype(bf16))
    low_q = [
        (dot(scores[s], widen(s, slice(0, width)), 0, 0) * 0.125).astype(bf16) for s in range(seqs)
    ]
    keys = [dot(scores[s], queries[s * length : (s + 1) * length, :]) for s in range(seqs)]
    low_q = jnp.concatenate(low_q, axis=0)
    low_pairs = jnp.concatenate(
        [
            jnp.concatenate(
                [(narrow(keys[s]) * 0.125).astype(bf16), narrow(values[s]).astype(bf16)], axis=1
            )
            for s in range(seqs)
        ],
        axis=0,
    )
    at = pl.ds(pl.multiple_of(step * seqs * mem_total, seqs * mem_total), seqs * mem_total)
    grad_rows[at, :] = dot(low_pairs, w_kv[...], 1, 1).astype(bf16)
    normal, spread = normalize(mid[...].astype(f32))
    act = (normal * gain_cross[...]).astype(bf16)
    total[width : 2 * width, :] += dot(act, low_q, 0, 0)
    total[2 * width : 3 * width, :] += dot(arrived[...], low_pairs[:, :width], 0, 0)
    total[3 * width : 4 * width, :] += dot(arrived[...], low_pairs[:, width:], 0, 0)
    change = norm_backward(
        dot(low_q, w_query[...], 1, 1), gain_cross[...], normal, spread
    )
    running = running + change
    gradient[...] = running.astype(bf16)
    total[4 * width :, :] += dot(attended[...], running.astype(bf16), 0, 0)

    @pl.when(step == pl.num_programs(0) - 1)
    def _():
        give_halves(bits[0], total, send, keep, width)
        rows = grad_rows.shape[0]
        block = min(rows, 512)
        count = rows // mem_total
        for start in range(0, rows, block):
            row = lax.broadcasted_iota(jnp.int32, (block, rows), 0) + start
            column = lax.broadcasted_iota(jnp.int32, (block, rows), 1)
            shift = count.bit_length() - 1
            source = (row & (count - 1)) * mem_total + (row >> shift)
            order = jnp.where(column == source, 1.0, 0.0).astype(bf16)
            grad_arrived[start : start + block, :] = dot(order, grad_rows[...]).astype(bf16)


def self_backward_kernel(
    seqs, length, width,
    bits, gradient, triple, weights, act, w_out,
    grad_triple, send, keep,
    total,
):
    step = pl.program_id(0)

    @pl.when(step == 0)
    def _():
        total[...] = jnp.zeros_like(total)

    low = dot(gradient[...], w_out[...], 1, 1).astype(bf16)
    first, second = head_masks(length)
    heads = [(s, p) for s in range(seqs) for p in range(width // PAIR)]
    for start in range(0, len(heads), GROUP):
        group = []
        for s, p in heads[start : start + GROUP]:
            rows = slice(s * length, (s + 1) * length)
            group.append((s, p, rows, [slice(j * width + p * PAIR, j * width + (p + 1) * PAIR) for j in range(3)]))
        grads = [spread_pair(low[rows, at[0]], first, second) for s, p, rows, at in group]
        softs = [weights[s, p] for s, p, rows, at in group]
        changes = [dot(triple[rows, at[2]], grad, 1, 1) for (s, p, rows, at), grad in zip(group, grads)]
        values = [dot(soft, grad).astype(bf16) for soft, grad in zip(softs, grads)]
        scores = []
        for soft, change in zip(softs, changes):
            soft = soft.astype(f32)
            product = soft * change
            scores.append((product - soft * jnp.sum(product, axis=0, keepdims=True)).astype(bf16))
        keys = [
            dot(score, spread_pair(triple[rows, at[0]] * 0.125, first, second)).astype(bf16)
            for (s, p, rows, at), score in zip(group, scores)
        ]
        queries = [
            (dot(stack_pair(score), spread_pair(triple[rows, at[1]], first, second), 0, 0) * 0.125).astype(bf16)
            for (s, p, rows, at), score in zip(group, scores)
        ]
        for n, (s, p, rows, at) in enumerate(group):
            grad_triple[rows, at[0]] = queries[n]
            grad_triple[rows, at[1]] = keys[n]
            grad_triple[rows, at[2]] = values[n]
    for j in range(3):
        total[j * width : (j + 1) * width, :] += dot(
            act[...], grad_triple[:, j * width : (j + 1) * width], 0, 0
        )

    @pl.when(step == pl.num_programs(0) - 1)
    def _():
        give_halves(bits[0], total, send, keep, width)


def grad_tokens_kernel(bits, gradient, grad_triple, tokens, w_qkv, gain_self, grad_tokens):
    normal, spread = normalize(tokens[...].astype(f32))
    change = norm_backward(dot(grad_triple[...], w_qkv[...], 1, 1), gain_self[...], normal, spread)
    grad_tokens[...] = (gradient[...].astype(f32) + change).astype(bf16)


def row_sums(weight, grad, gain):
    product = weight.astype(f32) * grad
    columns = sum(product[:, n : n + PAIR] for n in range(0, product.shape[1], PAIR))
    return jnp.sum(columns.T, axis=0, keepdims=True) / gain


def pick(core, own, got, fill):
    mine = pl.program_id(0) == core

    @pl.when(mine)
    def _():
        fill(own)

    @pl.when(jnp.logical_not(mine))
    def _():
        fill(got)


def ffn_final_kernel(bits, own, got, w_expand, gain, contract, expand, gain_grad):
    step = pl.program_id(0)
    chunk = expand.shape[1]

    def fill(source):
        contract[...] = source[:chunk, :].astype(f32)
        grad = source[chunk:, :].astype(f32)
        expand[...] = grad
        sums = row_sums(w_expand[...], grad, gain[...])

        @pl.when(step == 0)
        def _():
            gain_grad[...] = sums

        @pl.when(step > 0)
        def _():
            gain_grad[...] += sums

    mine = (step >= pl.num_programs(0) // 2) == (bits[0] == 1)

    @pl.when(mine)
    def _():
        fill(own)

    @pl.when(jnp.logical_not(mine))
    def _():
        fill(got)


def cross_final_kernel(bits, own, got, w_query, gain, cross_out, query, pair, self_out, gain_grad):
    half, width = query.shape

    def fill(source):
        cross_out[...] = source[:half, :].astype(f32)
        grad = source[half : 2 * half, :].astype(f32)
        query[...] = grad
        pair[:, :width] = source[2 * half : 3 * half, :].astype(f32)
        pair[:, width:] = source[3 * half : 4 * half, :].astype(f32)
        self_out[...] = source[4 * half :, :].astype(f32)
        gain_grad[...] = row_sums(w_query[...], grad, gain[...])

    pick(bits[0], own, got, fill)


def self_final_kernel(bits, own, got, w_qkv, gain, qkv, gain_grad):
    half = qkv.shape[0]
    width = own.shape[1]

    def fill(source):
        for j in range(3):
            qkv[:, j * width : (j + 1) * width] = source[j * half : (j + 1) * half, :].astype(f32)
        gain_grad[...] = row_sums(w_qkv[...], qkv[...], gain[...])

    pick(bits[0], own, got, fill)


def call(kernel, grid, bits, ins, outs, scratch=(), flops=0, deps=(), limit=VMEM_LIMIT):
    moved = sum(a.size * a.dtype.itemsize for a, *_ in ins)
    shapes = []
    for shape, dtype, _, *space in outs:
        size = 1
        for n in shape:
            size *= n
        moved += size * jnp.dtype(dtype).itemsize
        shapes.append(space[0](shape, dtype) if space else jax.ShapeDtypeStruct(shape, dtype))
    count = len(ins)
    arrays = [
        pltpu.with_memory_space_constraint(a, space[0]) if space else a for a, _, *space in ins
    ]

    def body(bits_ref, *refs):
        kernel(bits_ref, *refs[:count], *refs[count + len(deps) :])

    return pl.pallas_call(
        body,
        grid_spec=pltpu.PrefetchScalarGridSpec(
            num_scalar_prefetch=1,
            grid=grid,
            in_specs=[spec for _, spec, *_ in ins] + [pl.BlockSpec(memory_space=pl.ANY)] * len(deps),
            out_specs=[spec for _, _, spec, *_ in outs],
            scratch_shapes=list(scratch),
        ),
        out_shape=shapes,
        compiler_params=pltpu.CompilerParams(vmem_limit_bytes=limit * 1024 * 1024),
        cost_estimate=pl.CostEstimate(flops=flops, bytes_accessed=moved, transcendentals=0),
    )(bits, *arrays, *deps)


def by_step(*shape):
    return pl.BlockSpec(shape, lambda i, bits: (i,) + (0,) * (len(shape) - 1))


def whole(*shape):
    return pl.BlockSpec(shape, lambda i, bits: (0,) * len(shape))


def scalars():
    return pl.BlockSpec(memory_space=pltpu.SMEM)


SEQS = 4
GROUP = 16
MOST = 4


def self_forward(bits, tokens, lengths, gain_self, w_qkv, w_out, gain_cross, w_query, length):
    rows, width = tokens.shape
    n = rows // length
    block = SEQS * length
    row = by_step(block, width)
    return call(
        functools.partial(self_forward_kernel, SEQS, length, width),
        (n // SEQS,), bits,
        [
            (lengths, scalars()), (tokens, row, HBM),
            (gain_self, whole(1, width)), (w_qkv, whole(width, 3 * width), HBM),
            (w_out, whole(width, width), HBM), (gain_cross, whole(1, width)),
            (w_query, whole(width, width), HBM),
        ],
        [
            ((rows, width), bf16, row, HBM),
            ((rows, 3 * width), bf16, by_step(block, 3 * width), HBM),
            ((n, width // PAIR, length, 2 * length), bf16, by_step(SEQS, width // PAIR, length, 2 * length), HBM),
            ((rows, width), bf16, row, HBM),
            ((rows, width), bf16, row, HBM),
            ((rows, width), bf16, row, HBM),
        ],
        flops=12 * rows * width * width,
    )


def cross_forward(bits, lengths, memory_lengths, raw, queries, mid, grad_output, w_kv, w_out, gain_ffn, length, mem_total):
    rows, width = queries.shape
    n = rows // length
    block = SEQS * length
    mem = SEQS * mem_total
    heads = width // HEAD
    row = by_step(block, width)
    return call(
        functools.partial(cross_forward_kernel, SEQS, length, width, mem_total),
        (n // SEQS,), bits,
        [
            (lengths, scalars()), (memory_lengths, scalars()),
            (raw, whole(*raw.shape)), (queries, row, HBM),
            (mid, row, HBM), (grad_output, row, HBM),
            (w_kv, whole(width, 2 * width)), (w_out, whole(width, width)),
            (gain_ffn, whole(1, width)),
        ],
        [
            ((n * mem_total, width), bf16, by_step(mem, width), HBM),
            ((n * mem_total, 2 * width), bf16, by_step(mem, 2 * width), HBM),
            ((n, heads * mem_total, length), bf16, by_step(SEQS, heads * mem_total, length), HBM),
            ((rows, width), bf16, row, HBM),
            ((rows, width), bf16, row, HBM),
            ((rows, width), bf16, row, HBM),
            ((rows, width), bf16, row, VMEM),
            ((rows, width), bf16, row, VMEM),
            ((rows, width), bf16, row, VMEM),
        ],
        flops=6 * rows * width * width,
        limit=VMEM_LIMIT if mem_total <= 32 else 2 * VMEM_LIMIT,
    )


def feed_forward(bits, act, grad_low, start, w_expand, w_contract, chunk=512):
    rows, width = act.shape
    hidden = w_expand.shape[1]
    steps = hidden // chunk
    half = steps // 2

    def at(i, bits):
        return lax.rem(i + half * (1 - bits[0]), steps)

    def block(place):
        return pl.BlockSpec((2 * chunk, width), lambda i, bits: (place(i), 0))

    return call(
        functools.partial(ffn_kernel, min(rows, 512)),
        (steps,), bits,
        [
            (act, whole(rows, width)), (grad_low, whole(rows, width)), (start, whole(rows, width)),
            (w_expand, pl.BlockSpec((width, chunk), lambda i, bits: (0, at(i, bits)))),
            (w_contract, pl.BlockSpec((chunk, width), lambda i, bits: (at(i, bits), 0))),
        ],
        [
            ((rows, width), bf16, whole(rows, width), HBM),
            ((rows, width), bf16, whole(rows, width), HBM),
            ((hidden, width), bf16, block(lambda i: jnp.minimum(i, half - 1)), HBM),
            ((hidden, width), bf16, block(lambda i: jnp.maximum(i - half, 0)), HBM),
        ],
        [
            pltpu.VMEM((rows, chunk), bf16),
            pltpu.VMEM((rows, chunk), bf16),
            pltpu.VMEM((rows, width), f32),
            pltpu.VMEM((rows, width), f32),
        ],
        flops=12 * rows * width * hidden,
    )


def cross_backward(bits, grad_normed, late, grad_low, cross, weights, pairs, queries, mid, arrived, attended, w_out, w_query, w_kv, gain_ffn, gain_cross, length, mem_total, deps=()):
    rows, width = queries.shape
    n = rows // length
    block = SEQS * length
    mem = SEQS * mem_total
    heads = width // HEAD
    row = by_step(block, width)
    return call(
        functools.partial(cross_backward_kernel, SEQS, length, width, mem_total),
        (n // SEQS,), bits,
        [
            (grad_normed, row, HBM), (late, row, HBM), (grad_low, row, HBM), (cross, row, HBM),
            (weights, by_step(SEQS, heads * mem_total, length), HBM),
            (pairs, by_step(mem, 2 * width), HBM), (queries, row, HBM), (mid, row, HBM),
            (arrived, by_step(mem, width), HBM), (attended, row, HBM),
            (w_out, whole(width, width), HBM), (w_query, whole(width, width), HBM),
            (w_kv, whole(width, 2 * width), HBM),
            (gain_ffn, whole(1, width)), (gain_cross, whole(1, width)),
        ],
        [
            ((rows, width), bf16, row, HBM),
            ((n * mem_total, width), bf16, whole(n * mem_total, width), HBM),
            ((5 * width // 2, width), bf16, whole(5 * width // 2, width), HBM),
            ((5 * width // 2, width), bf16, whole(5 * width // 2, width), HBM),
        ],
        [
            pltpu.VMEM((5 * width, width), f32),
            pltpu.VMEM((n * mem_total, width), bf16),
        ],
        flops=14 * rows * width * width,
        deps=deps,
        limit=VMEM_LIMIT if mem_total <= 32 else 2 * VMEM_LIMIT,
    )


def self_backward(bits, gradient, triple, weights, act, w_out, length, deps=()):
    rows, width = gradient.shape
    n = rows // length
    block = SEQS * length
    return call(
        functools.partial(self_backward_kernel, SEQS, length, width),
        (n // SEQS,), bits,
        [
            (gradient, by_step(block, width), HBM), (triple, by_step(block, 3 * width), HBM),
            (weights, by_step(SEQS, width // PAIR, length, 2 * length), HBM),
            (act, by_step(block, width), HBM), (w_out, whole(width, width), HBM),
        ],
        [
            ((rows, 3 * width), bf16, by_step(block, 3 * width), HBM),
            ((3 * width // 2, width), bf16, whole(3 * width // 2, width), HBM),
            ((3 * width // 2, width), bf16, whole(3 * width // 2, width), HBM),
        ],
        [pltpu.VMEM((3 * width, width), f32)],
        flops=14 * rows * width * width,
        deps=deps,
    )


def token_gradient(bits, gradient, grad_triple, tokens, w_qkv, gain_self, deps=()):
    rows, width = tokens.shape
    block = 512
    row = by_step(block, width)
    return call(
        grad_tokens_kernel, (rows // block,), bits,
        [
            (gradient, row, HBM), (grad_triple, by_step(block, 3 * width), HBM), (tokens, row, HBM),
            (w_qkv, whole(width, 3 * width), HBM), (gain_self, whole(1, width)),
        ],
        [((rows, width), bf16, row)],
        flops=6 * rows * width * width,
        deps=deps,
    )[0]


def after(arrays, deps):
    if not deps:
        return arrays
    return lax.optimization_barrier((*arrays, *deps))[: len(arrays)]


def added(left, right):
    return (left.astype(f32) + right.astype(f32)).astype(bf16)


def split_sum(mine, keep, got):
    half = keep.shape[0] // 2

    def part(which):
        return added(
            lax.dynamic_slice_in_dim(keep, which * half, half),
            lax.dynamic_slice_in_dim(got, which * half, half),
        )

    return part(1 - mine), part(mine)


def join(mine, own, got):
    return jnp.where(mine == 0, jnp.concatenate([own, got]), jnp.concatenate([got, own]))


def exchange(block, bit, devices):
    return lax.ppermute(block, "dp", [(i, i ^ (1 << bit)) for i in range(devices)])


class Lane:
    def __init__(self, bits, devices, order, send, keep, most):
        halvings, rows = 1, keep.shape[0]
        while halvings < min(most, len(order)) and rows % 32 == 0:
            rows //= 2
            halvings += 1
        self.bits, self.devices = bits, devices
        self.own, self.token = keep, send
        self.got = exchange(send, order[0], devices)
        self.todo = [("split", b) for b in order[1:halvings]]
        self.todo += [("whole", b) for b in order[halvings:]]
        back = order[:halvings][::-1]
        self.todo += [("gather", back[0])] + list(zip(back[:-1], back[1:]))

    def advance(self, deps=()):
        if not self.todo:
            return
        kind, bit = self.todo.pop(0)
        own, got = after((self.own, self.got), deps)
        if kind == "split":
            send, self.own = split_sum(self.bits[bit], own, got)
        elif kind in ("whole", "gather"):
            send = self.own = added(own, got)
        else:
            send = self.own = join(self.bits[kind], own, got)
        self.token = send
        self.got = exchange(send, bit, self.devices)


def ffn_final(bits, own, got, w_expand, gain, deps=(), chunk=512):
    width, hidden = w_expand.shape
    steps = hidden // chunk

    def source(mine):
        def at(i, bits):
            first = (bits[0] == 0) == mine
            return (jnp.where(first, jnp.minimum(i, steps // 2 - 1), jnp.maximum(i - steps // 2, 0)), 0)

        return pl.BlockSpec((2 * chunk, width), at)

    return call(
        ffn_final_kernel, (steps,), bits,
        [
            (own, source(True), HBM), (got, source(False), HBM),
            (w_expand, pl.BlockSpec((width, chunk), lambda i, bits: (0, i))),
            (gain, whole(1, width)),
        ],
        [
            ((hidden, width), f32, by_step(chunk, width)),
            ((width, hidden), f32, pl.BlockSpec((width, chunk), lambda i, bits: (0, i))),
            ((1, width), f32, whole(1, width)),
        ],
        deps=deps,
    )


def cross_final(bits, own, got, w_query, gain, deps=()):
    width = w_query.shape[0]
    half = width // 2
    part = by_step(half, width)
    column = pl.BlockSpec((1, half), lambda i, bits: (0, i))
    return call(
        cross_final_kernel, (2,), bits,
        [
            (own, whole(*own.shape), HBM), (got, whole(*own.shape), HBM), (w_query, part), (gain, column),
        ],
        [
            ((width, width), f32, part), ((width, width), f32, part),
            ((width, 2 * width), f32, by_step(half, 2 * width)), ((width, width), f32, part),
            ((1, width), f32, column),
        ],
        deps=deps,
    )


def self_final(bits, own, got, w_qkv, gain, deps=()):
    width = w_qkv.shape[0]
    half = width // 2
    column = pl.BlockSpec((1, half), lambda i, bits: (0, i))
    return call(
        self_final_kernel, (2,), bits,
        [
            (own, whole(*own.shape), HBM), (got, whole(*own.shape), HBM),
            (w_qkv, by_step(half, 3 * width)), (gain, column),
        ],
        [((width, 3 * width), f32, by_step(half, 3 * width)), ((1, width), f32, column)],
        deps=deps,
    )


def local(
    devices, tokens, memory, target_lengths, memory_lengths, grad_output,
    gain_self, w_qkv, w_self_out, gain_cross, w_cross_query, w_cross_kv, w_cross_out,
    gain_ffn, w_expand, w_contract,
):
    seq_count, length, width = tokens.shape
    rows = seq_count * length
    gain_self, gain_cross, gain_ffn = gain_self[None], gain_cross[None], gain_ffn[None]
    flat_tokens = tokens.reshape(rows, width)
    order = tuple(range(devices.bit_length() - 1))
    turned = order[:1] + order[2:3] + order[1:2] + order[3:]
    me = lax.axis_index("dp")
    mine = [(me >> b) & 1 for b in order]
    bits = jnp.stack(mine).astype(jnp.int32)
    raw = lax.all_to_all(
        memory.reshape(devices, -1, width), "dp", split_axis=0, concat_axis=0, tiled=True
    ).reshape(-1, width)
    mem_total = raw.shape[0] // seq_count
    act_one, triple, self_weights, attended, mid, queries = self_forward(
        bits, flat_tokens, target_lengths, gain_self, w_qkv, w_self_out, gain_cross, w_cross_query, length
    )
    arrived, pairs, cross_weights, cross, late, grad_low, late_near, grad_low_near, act = cross_forward(
        bits, target_lengths, memory_lengths, raw, queries, mid, grad_output.reshape(rows, width),
        w_cross_kv, w_cross_out, gain_ffn, length, mem_total,
    )
    output, grad_normed, send, keep = feed_forward(
        bits, act, grad_low_near, late_near, w_expand, w_contract
    )
    ffn = Lane(mine, devices, order, send, keep, MOST)
    ffn.advance()
    gradient, grad_arrived, send, keep = cross_backward(
        bits, grad_normed, late, grad_low, cross, cross_weights, pairs, queries, mid, arrived,
        attended, w_cross_out, w_cross_query, w_cross_kv, gain_ffn, gain_cross, length, mem_total,
        deps=[ffn.token],
    )
    ffn.advance([send])
    crossed = Lane(mine, devices, order, after((send,), [ffn.token])[0], keep, MOST)
    crossed.advance()
    grad_triple, send, keep = self_backward(
        bits, gradient, triple, self_weights, act_one, w_self_out, length, deps=[ffn.token, crossed.token]
    )
    ffn.advance([send])
    crossed.advance([ffn.token])
    selfs = Lane(mine, devices, turned, after((send,), [crossed.token])[0], keep, MOST)
    selfs.advance()
    grad_memory = lax.all_to_all(
        after((grad_arrived,), [selfs.token])[0].reshape(devices, -1, width),
        "dp", split_axis=0, concat_axis=0, tiled=True,
    ).reshape(memory.shape)
    grad_tokens = token_gradient(
        bits, gradient, grad_triple, flat_tokens, w_qkv, gain_self,
        deps=[ffn.token, crossed.token, selfs.token],
    )
    deps = [grad_tokens, grad_memory]
    while selfs.todo or crossed.todo or ffn.todo:
        for lane in (ffn, crossed, selfs):
            lane.advance(deps)
            deps = [lane.token]
    grad_contract, grad_expand, grad_gain_ffn = ffn_final(bits, ffn.own, ffn.got, w_expand, gain_ffn)
    grad_cross_out, grad_cross_query, grad_cross_kv, grad_self_out, grad_gain_cross = cross_final(
        bits, crossed.own, crossed.got, w_cross_query, gain_cross
    )
    grad_qkv, grad_gain_self = self_final(bits, selfs.own, selfs.got, w_qkv, gain_self)
    return (
        output.reshape(tokens.shape),
        grad_tokens.reshape(tokens.shape),
        grad_memory,
        grad_gain_self[0],
        grad_qkv,
        grad_self_out,
        grad_gain_cross[0],
        grad_cross_query,
        grad_cross_kv,
        grad_cross_out,
        grad_gain_ffn[0],
        grad_expand,
        grad_contract,
    )


def solution(mesh):
    rows, columns, copied = P("dp", None, None), P(None, "dp", None), P()
    return jax.shard_map(
        functools.partial(local, mesh.shape["dp"]),
        mesh=mesh,
        in_specs=(rows, columns, P("dp"), P("dp"), rows) + (copied,) * 10,
        out_specs=(rows, rows, columns) + (copied,) * 10,
        check_vma=False,
    )
```

```python
import functools
import jax
import jax.numpy as jnp
from jax import lax
from jax.experimental import pallas as pl
from jax.experimental.pallas import tpu as pltpu
from jax.sharding import PartitionSpec as P

HEAD = 64
PAIR = 128
epsilon = 1e-05
big_negative = -1e30
f32 = jnp.float32
bf16 = jnp.bfloat16
VMEM_LIMIT = 24
HBM = pltpu.HBM
VMEM = pltpu.VMEM


def dot(left, right, left_dim=1, right_dim=0):
    return lax.dot_general(
        left, right, (((left_dim,), (right_dim,)), ((), ())), preferred_element_type=f32
    )


def normalize(hidden):
    centred = hidden - jnp.mean(hidden, axis=-1, keepdims=True)
    spread = lax.rsqrt(jnp.mean(centred * centred, axis=-1, keepdims=True) + epsilon)
    return centred * spread, spread


def norm_backward(gradient, gain, normalized, spread):
    scaled = gradient * gain
    first = jnp.mean(scaled, axis=-1, keepdims=True)
    second = jnp.mean(scaled * normalized, axis=-1, keepdims=True)
    return spread * (scaled - first - normalized * second)


def head_masks(rows):
    lane = lax.broadcasted_iota(jnp.int32, (rows, PAIR), 1)
    first = jnp.where(lane < HEAD, 1.0, 0.0).astype(bf16)
    second = jnp.where(lane >= HEAD, 1.0, 0.0).astype(bf16)
    return first, second


def spread_pair(block, first, second):
    return jnp.concatenate([block * first, block * second], axis=0)


def stack_pair(block):
    half = block.shape[1] // 2
    return jnp.concatenate([block[:, :half], block[:, half:]], axis=0)


def wide_mask(mem_total, width):
    lane = lax.broadcasted_iota(jnp.int32, (mem_total, width), 1)
    parts = [
        jnp.where((lane >= h * HEAD) & (lane < (h + 1) * HEAD), 1.0, 0.0)
        for h in range(width // HEAD)
    ]
    return parts


PARTS = 1
LAG = 1


def stagger(parts):
    waiting = [LAG * n for n in range(len(parts))]
    while parts:
        left = []
        for n, part in enumerate(parts):
            if waiting[n]:
                waiting[n] -= 1
                left.append(n)
            elif next(part, part) is not part:
                left.append(n)
        parts, waiting = [parts[n] for n in left], [waiting[n] for n in left]


def self_forward_kernel(
    seqs, length, width,
    bits, lengths, tokens, gain_self, w_qkv, w_out, gain_cross, w_query,
    act, triple, weights, attended, mid, queries,
):
    step = pl.program_id(0)
    first, second = head_masks(length)
    key_at = lax.broadcasted_iota(jnp.int32, (length, 2 * length), 0)
    query_at = lax.broadcasted_iota(jnp.int32, (length, 2 * length), 1)
    query_at = jnp.where(query_at >= length, query_at - length, query_at)
    causal = key_at <= query_at
    count = seqs // PARTS

    def part(n):
        span = slice(n * count * length, (n + 1) * count * length)
        residual = tokens[span, :].astype(f32)
        normal, _ = normalize(residual)
        low = (normal * gain_self[...]).astype(bf16)
        yield
        both = dot(low, w_qkv[...]).astype(bf16)
        yield
        heads = [(s, p) for s in range(count) for p in range(width // PAIR)]
        scores = []
        for s, p in heads:
            rows = slice(s * length, (s + 1) * length)
            q = both[rows, p * PAIR : (p + 1) * PAIR] * 0.125
            k = both[rows, width + p * PAIR : width + (p + 1) * PAIR]
            scores.append(dot(k, spread_pair(q, first, second), 1, 1))
        yield
        softs = []
        for (s, p), score in zip(heads, scores):
            allowed = causal & (key_at < lengths[step * seqs + n * count + s])
            score = jnp.where(allowed, score, big_negative)
            raised = jnp.exp(score - jnp.max(score, axis=0, keepdims=True))
            softs.append((raised * (1.0 / jnp.sum(raised, axis=0, keepdims=True))).astype(bf16))
        yield
        joined = {}
        for (s, p), soft in zip(heads, softs):
            rows = slice(s * length, (s + 1) * length)
            v = both[rows, 2 * width + p * PAIR : 2 * width + (p + 1) * PAIR]
            joined[s, p] = dot(stack_pair(soft), spread_pair(v, first, second), 0, 0).astype(bf16)
        yield
        out = jnp.concatenate(
            [
                jnp.concatenate([joined[s, p] for p in range(width // PAIR)], axis=1)
                for s in range(count)
            ],
            axis=0,
        )
        residual = residual + dot(out, w_out[...])
        yield
        normal, _ = normalize(residual)
        after = (normal * gain_cross[...]).astype(bf16)
        yield
        found = dot(after, w_query[...]).astype(bf16)
        yield
        act[span, :] = low
        triple[span, :] = both
        attended[span, :] = out
        mid[span, :] = residual.astype(bf16)
        queries[span, :] = found
        for (s, p), soft in zip(heads, softs):
            weights[n * count + s, p] = soft

    stagger([part(n) for n in range(PARTS)])


def cross_forward_kernel(
    seqs, length, width, mem_total,
    bits, lengths, memory_lengths, raw, queries, mid, grad_output, w_kv, w_out, gain_ffn,
    arrived, pairs, weights, cross, late, grad_low, late_near, grad_low_near, act,
):
    step = pl.program_id(0)
    total = raw.shape[0] // mem_total
    at = lax.broadcasted_iota(jnp.int32, (mem_total, raw.shape[0]), 0) * total
    column = lax.broadcasted_iota(jnp.int32, (mem_total, raw.shape[0]), 1)
    own_rows = jnp.concatenate(
        [jnp.where(column == at + (step * seqs + s), 1.0, 0.0).astype(bf16) for s in range(seqs)],
        axis=0,
    )
    own_rows = dot(own_rows, raw[...]).astype(bf16)
    arrived[...] = own_rows
    both = dot(own_rows, w_kv[...]).astype(bf16)
    pairs[...] = both
    mask = jnp.concatenate(wide_mask(mem_total, width), axis=0).astype(bf16)
    heads = width // HEAD
    key_at = lax.broadcasted_iota(jnp.int32, (mem_total, length), 0)
    row_at = lax.broadcasted_iota(jnp.int32, (length, width), 0)

    def spread(s, at):
        return jnp.concatenate([both[s * mem_total : (s + 1) * mem_total, at]] * heads, axis=0) * mask

    scores = []
    for s in range(seqs):
        q = queries[s * length : (s + 1) * length, :] * 0.125
        scores.append(dot(spread(s, slice(0, width)), q, 1, 1).reshape(heads, mem_total, length))
    softs = []
    for s in range(seqs):
        allowed = (key_at < memory_lengths[step * seqs + s])[None]
        score = jnp.where(allowed, scores[s], big_negative)
        raised = jnp.exp(score - jnp.max(score, axis=1, keepdims=True))
        soft = raised * (1.0 / jnp.sum(raised, axis=1, keepdims=True))
        softs.append(soft.reshape(heads * mem_total, length).astype(bf16))
    joined = [dot(softs[s], spread(s, slice(width, 2 * width)), 0, 0).astype(bf16) for s in range(seqs)]
    low = jnp.concatenate(joined, axis=0)
    cross[...] = low
    for s in range(seqs):
        rows = slice(s * length, (s + 1) * length)
        weights[s] = softs[s]
        live = row_at < lengths[step * seqs + s]
        masked = jnp.where(live, grad_output[rows, :].astype(f32), 0.0).astype(bf16)
        grad_low[rows, :] = masked
        grad_low_near[rows, :] = masked
    residual = mid[...].astype(f32) + dot(low, w_out[...])
    late[...] = residual.astype(bf16)
    late_near[...] = residual.astype(bf16)
    normal, _ = normalize(residual)
    act[...] = (normal * gain_ffn[...]).astype(bf16)


def gelu_parts(value):
    half = 0.5 + 0.5 * lax.erf(value * 0.7071067811865476)
    bell = value * jnp.exp2(value * value * (-0.5 * 1.4426950408889634))
    return value * half, half + 0.3989422804014327 * bell


def place(bits, n, turned=None):
    first, second = bits[1], bits[2]
    if turned is not None:
        first, second = jnp.where(turned, second, first), jnp.where(turned, first, second)
    mine = first * 4 + second * 2 + bits[3]
    return jnp.bitwise_xor(mine, 7 - n)


def ffn_kernel(
    row_block,
    bits, act, grad_low, start, w_expand, w_contract,
    result, grad_normed, send, keep,
    activated, grad_expanded, total, change,
):
    step = pl.program_id(0)
    rows = act.shape[0]
    chunk = w_expand.shape[1]

    @pl.when(step == 0)
    def _():
        total[...] = start[...].astype(f32)
        change[...] = jnp.zeros_like(change)

    for b in range(rows // row_block):
        r = slice(b * row_block, (b + 1) * row_block)
        expanded = dot(act[r, :], w_expand[...])
        grad_activated = dot(grad_low[r, :], w_contract[...], 1, 1)
        value, slope = gelu_parts(expanded)
        value = value.astype(bf16)
        slope = (grad_activated * slope).astype(bf16)
        activated[r, :] = value
        grad_expanded[r, :] = slope
        total[r, :] += dot(value, w_contract[...])
        change[r, :] += dot(slope, w_expand[...], 1, 1)

    def fill(grads):
        found = [dot(activated[...], grad_low[...], 0, 0), dot(act[...], grad_expanded[...], 0, 0)]
        size = chunk // 4
        turned = lax.rem(step, pl.num_programs(0) // 2) == 1
        for n in range(8):
            at = pl.ds(pl.multiple_of(place(bits, n, turned) * size, size), size)
            grads[at, :] = found[n // 4][n % 4 * size : (n % 4 + 1) * size, :].astype(bf16)

    @pl.when(step < pl.num_programs(0) // 2)
    def _():
        fill(send)

    @pl.when(step >= pl.num_programs(0) // 2)
    def _():
        fill(keep)

    @pl.when(step == pl.num_programs(0) - 1)
    def _():
        result[...] = total[...].astype(bf16)
        grad_normed[...] = change[...].astype(bf16)


def add_halves(total, n, value):
    half = value.shape[0] // 2
    rows = total.shape[0] // 2
    total[n * half : (n + 1) * half, :] += value[:half]
    total[rows + n * half : rows + (n + 1) * half, :] += value[half:]


def give_halves(bits, total, send, keep, turned):
    rows = send.shape[0]
    size = rows // 8
    for n in range(8):
        to = pl.ds(pl.multiple_of(place(bits, n, turned) * size, size), size)
        at = pl.ds(pl.multiple_of((1 - bits[0]) * rows + n * size, size), size)
        send[to, :] = total[at, :].astype(bf16)
        at = pl.ds(pl.multiple_of(bits[0] * rows + n * size, size), size)
        keep[to, :] = total[at, :].astype(bf16)


def cross_backward_kernel(
    seqs, length, width, mem_total,
    bits, grad_normed, late, grad_low, cross, weights, pairs, queries, mid, arrived, attended,
    w_out, w_query, w_kv, gain_ffn, gain_cross,
    gradient, grad_arrived, send, keep,
    total, grad_rows,
):
    step = pl.program_id(0)

    @pl.when(step == 0)
    def _():
        total[...] = jnp.zeros_like(total)

    normal, spread = normalize(late[...].astype(f32))
    change = norm_backward(
        grad_normed[...].astype(f32), gain_ffn[...], normal, spread
    )
    running = grad_low[...].astype(f32) + change
    low = running.astype(bf16)
    add_halves(total, 0, dot(cross[...], low, 0, 0))
    grad_cross = dot(low, w_out[...], 1, 1).astype(bf16)
    masks = wide_mask(mem_total, width)
    mask = jnp.concatenate(masks, axis=0).astype(bf16)
    heads = width // HEAD

    def widen(s, at):
        return jnp.concatenate([pairs[s * mem_total : (s + 1) * mem_total, at]] * heads, axis=0) * mask

    def narrow(block):
        return sum(block[h * mem_total : (h + 1) * mem_total, :] * masks[h] for h in range(heads))

    softs = [weights[s] for s in range(seqs)]
    grads = [grad_cross[s * length : (s + 1) * length, :] for s in range(seqs)]
    values = [dot(softs[s], grads[s]) for s in range(seqs)]
    changes = [
        dot(widen(s, slice(width, 2 * width)), grads[s], 1, 1).reshape(heads, mem_total, length)
        for s in range(seqs)
    ]
    scores = []
    for s in range(seqs):
        soft = softs[s].astype(f32).reshape(heads, mem_total, length)
        product = soft * changes[s]
        score = product - soft * jnp.sum(product, axis=1, keepdims=True)
        scores.append(score.reshape(heads * mem_total, length).astype(bf16))
    low_q = [
        (dot(scores[s], widen(s, slice(0, width)), 0, 0) * 0.125).astype(bf16) for s in range(seqs)
    ]
    keys = [dot(scores[s], queries[s * length : (s + 1) * length, :]) for s in range(seqs)]
    low_q = jnp.concatenate(low_q, axis=0)
    low_pairs = jnp.concatenate(
        [
            jnp.concatenate(
                [(narrow(keys[s]) * 0.125).astype(bf16), narrow(values[s]).astype(bf16)], axis=1
            )
            for s in range(seqs)
        ],
        axis=0,
    )
    at = pl.ds(pl.multiple_of(step * seqs * mem_total, seqs * mem_total), seqs * mem_total)
    grad_rows[at, :] = dot(low_pairs, w_kv[...], 1, 1).astype(bf16)
    normal, spread = normalize(mid[...].astype(f32))
    act = (normal * gain_cross[...]).astype(bf16)
    add_halves(total, 1, dot(act, low_q, 0, 0))
    add_halves(total, 2, dot(arrived[...], low_pairs[:, :width], 0, 0))
    add_halves(total, 3, dot(arrived[...], low_pairs[:, width:], 0, 0))
    change = norm_backward(
        dot(low_q, w_query[...], 1, 1), gain_cross[...], normal, spread
    )
    running = running + change
    gradient[...] = running.astype(bf16)
    add_halves(total, 4, dot(attended[...], running.astype(bf16), 0, 0))

    @pl.when(step == pl.num_programs(0) - 1)
    def _():
        give_halves(bits, total, send, keep, TURNED[0])
        rows = grad_rows.shape[0]
        block = min(rows, 512)
        count = rows // mem_total
        for start in range(0, rows, block):
            row = lax.broadcasted_iota(jnp.int32, (block, rows), 0) + start
            column = lax.broadcasted_iota(jnp.int32, (block, rows), 1)
            shift = count.bit_length() - 1
            source = (row & (count - 1)) * mem_total + (row >> shift)
            order = jnp.where(column == source, 1.0, 0.0).astype(bf16)
            grad_arrived[start : start + block, :] = dot(order, grad_rows[...]).astype(bf16)


def self_backward_kernel(
    seqs, length, width,
    bits, gradient, triple, weights, act, w_out,
    grad_triple, send, keep,
    total,
):
    step = pl.program_id(0)

    @pl.when(step == 0)
    def _():
        total[...] = jnp.zeros_like(total)

    low = dot(gradient[...], w_out[...], 1, 1).astype(bf16)
    first, second = head_masks(length)
    heads = [(s, p) for s in range(seqs) for p in range(width // PAIR)]
    for start in range(0, len(heads), GROUP):
        group = []
        for s, p in heads[start : start + GROUP]:
            rows = slice(s * length, (s + 1) * length)
            group.append((s, p, rows, [slice(j * width + p * PAIR, j * width + (p + 1) * PAIR) for j in range(3)]))
        grads = [spread_pair(low[rows, at[0]], first, second) for s, p, rows, at in group]
        softs = [weights[s, p] for s, p, rows, at in group]
        changes = [dot(triple[rows, at[2]], grad, 1, 1) for (s, p, rows, at), grad in zip(group, grads)]
        values = [dot(soft, grad).astype(bf16) for soft, grad in zip(softs, grads)]
        scores = []
        for soft, change in zip(softs, changes):
            soft = soft.astype(f32)
            product = soft * change
            scores.append((product - soft * jnp.sum(product, axis=0, keepdims=True)).astype(bf16))
        keys = [
            dot(score, spread_pair(triple[rows, at[0]] * 0.125, first, second)).astype(bf16)
            for (s, p, rows, at), score in zip(group, scores)
        ]
        queries = [
            (dot(stack_pair(score), spread_pair(triple[rows, at[1]], first, second), 0, 0) * 0.125).astype(bf16)
            for (s, p, rows, at), score in zip(group, scores)
        ]
        for n, (s, p, rows, at) in enumerate(group):
            grad_triple[rows, at[0]] = queries[n]
            grad_triple[rows, at[1]] = keys[n]
            grad_triple[rows, at[2]] = values[n]
    for j in range(3):
        add_halves(total, j, dot(act[...], grad_triple[:, j * width : (j + 1) * width], 0, 0))

    @pl.when(step == pl.num_programs(0) - 1)
    def _():
        give_halves(bits, total, send, keep, TURNED[1])


def grad_tokens_kernel(bits, gradient, grad_triple, tokens, w_qkv, gain_self, grad_tokens):
    normal, spread = normalize(tokens[...].astype(f32))
    change = norm_backward(dot(grad_triple[...], w_qkv[...], 1, 1), gain_self[...], normal, spread)
    grad_tokens[...] = (gradient[...].astype(f32) + change).astype(bf16)


def row_sums(weight, grad, gain):
    product = weight.astype(f32) * grad
    columns = sum(product[:, n : n + PAIR] for n in range(0, product.shape[1], PAIR))
    return jnp.sum(columns.T, axis=0, keepdims=True) / gain


def in_order(bits, mine, own, got, ordered, turned):
    size = ordered.shape[0] // 8

    def fill(source):
        for n in range(8):
            at = pl.ds(pl.multiple_of(place(bits, n, turned) * size, size), size)
            ordered[n * size : (n + 1) * size, :] = source[at, :]

    @pl.when(mine)
    def _():
        fill(own)

    @pl.when(jnp.logical_not(mine))
    def _():
        fill(got)


def ffn_final_kernel(bits, own, got, w_expand, gain, contract, expand, gain_grad, ordered):
    step = pl.program_id(0)
    chunk = expand.shape[1]
    half = pl.num_programs(0) // 2
    in_order(bits, (step >= half) == (bits[0] == 1), own, got, ordered, lax.rem(step, half) == 1)
    contract[...] = ordered[:chunk, :].astype(f32)
    grad = ordered[chunk:, :].astype(f32)
    expand[...] = grad
    sums = row_sums(w_expand[...], grad, gain[...])

    @pl.when(step == 0)
    def _():
        gain_grad[...] = sums

    @pl.when(step > 0)
    def _():
        gain_grad[...] += sums


def cross_final_kernel(bits, own, got, w_query, gain, cross_out, query, pair, self_out, gain_grad, ordered):
    half, width = query.shape
    in_order(bits, pl.program_id(0) == bits[0], own, got, ordered, TURNED[0])
    cross_out[...] = ordered[:half, :].astype(f32)
    grad = ordered[half : 2 * half, :].astype(f32)
    query[...] = grad
    pair[:, :width] = ordered[2 * half : 3 * half, :].astype(f32)
    pair[:, width:] = ordered[3 * half : 4 * half, :].astype(f32)
    self_out[...] = ordered[4 * half :, :].astype(f32)
    gain_grad[...] = row_sums(w_query[...], grad, gain[...])


def self_final_kernel(bits, own, got, w_qkv, gain, qkv, gain_grad, ordered):
    half = qkv.shape[0]
    width = own.shape[1]
    in_order(bits, pl.program_id(0) == bits[0], own, got, ordered, TURNED[1])
    for j in range(3):
        qkv[:, j * width : (j + 1) * width] = ordered[j * half : (j + 1) * half, :].astype(f32)
    gain_grad[...] = row_sums(w_qkv[...], qkv[...], gain[...])


def call(kernel, grid, bits, ins, outs, scratch=(), flops=0, deps=(), limit=VMEM_LIMIT):
    moved = sum(a.size * a.dtype.itemsize for a, *_ in ins)
    shapes = []
    for shape, dtype, _, *space in outs:
        size = 1
        for n in shape:
            size *= n
        moved += size * jnp.dtype(dtype).itemsize
        shapes.append(space[0](shape, dtype) if space else jax.ShapeDtypeStruct(shape, dtype))
    count = len(ins)
    arrays = [
        pltpu.with_memory_space_constraint(a, space[0]) if space else a for a, _, *space in ins
    ]

    def body(bits_ref, *refs):
        kernel(bits_ref, *refs[:count], *refs[count + len(deps) :])

    return pl.pallas_call(
        body,
        grid_spec=pltpu.PrefetchScalarGridSpec(
            num_scalar_prefetch=1,
            grid=grid,
            in_specs=[spec for _, spec, *_ in ins] + [pl.BlockSpec(memory_space=pl.ANY)] * len(deps),
            out_specs=[spec for _, _, spec, *_ in outs],
            scratch_shapes=list(scratch),
        ),
        out_shape=shapes,
        compiler_params=pltpu.CompilerParams(vmem_limit_bytes=limit * 1024 * 1024),
        cost_estimate=pl.CostEstimate(flops=flops, bytes_accessed=moved, transcendentals=0),
    )(bits, *arrays, *deps)


def by_step(*shape):
    return pl.BlockSpec(shape, lambda i, bits: (i,) + (0,) * (len(shape) - 1))


def whole(*shape):
    return pl.BlockSpec(shape, lambda i, bits: (0,) * len(shape))


def scalars():
    return pl.BlockSpec(memory_space=pltpu.SMEM)


SEQS = 4
GROUP = 16
TURNED = (True, None)
PLAN = (
    "do ffn",
    "cross",
    "do ffn",
    "start cross",
    "do cross",
    "memory",
    "self",
    "do ffn",
    "do cross",
    "start self",
    "do self",
    "do ffn",
    "do cross",
    "tokens",
    "do ffn",
    "do self",
    "do cross",
    "do ffn",
    "do self",
    "do cross",
    "do ffn",
    "do self",
    "do cross",
    "do self",
    "do self",
    "do ffn",
    "do cross",
    "do self",
    "end ffn",
    "do self",
    "do cross",
    "end self",
    "end cross",
)


def self_forward(bits, tokens, lengths, gain_self, w_qkv, w_out, gain_cross, w_query, length):
    rows, width = tokens.shape
    n = rows // length
    block = SEQS * length
    row = by_step(block, width)
    return call(
        functools.partial(self_forward_kernel, SEQS, length, width),
        (n // SEQS,), bits,
        [
            (lengths, scalars()), (tokens, row, HBM),
            (gain_self, whole(1, width)), (w_qkv, whole(width, 3 * width), HBM),
            (w_out, whole(width, width), HBM), (gain_cross, whole(1, width)),
            (w_query, whole(width, width), HBM),
        ],
        [
            ((rows, width), bf16, row, HBM),
            ((rows, 3 * width), bf16, by_step(block, 3 * width), HBM),
            ((n, width // PAIR, length, 2 * length), bf16, by_step(SEQS, width // PAIR, length, 2 * length), HBM),
            ((rows, width), bf16, row, HBM),
            ((rows, width), bf16, row, HBM),
            ((rows, width), bf16, row, HBM),
        ],
        flops=12 * rows * width * width,
        limit=36,
    )


def cross_forward(bits, lengths, memory_lengths, raw, queries, mid, grad_output, w_kv, w_out, gain_ffn, length, mem_total):
    rows, width = queries.shape
    n = rows // length
    block = SEQS * length
    mem = SEQS * mem_total
    heads = width // HEAD
    row = by_step(block, width)
    return call(
        functools.partial(cross_forward_kernel, SEQS, length, width, mem_total),
        (n // SEQS,), bits,
        [
            (lengths, scalars()), (memory_lengths, scalars()),
            (raw, whole(*raw.shape)), (queries, row, HBM),
            (mid, row, HBM), (grad_output, row, HBM),
            (w_kv, whole(width, 2 * width)), (w_out, whole(width, width)),
            (gain_ffn, whole(1, width)),
        ],
        [
            ((n * mem_total, width), bf16, by_step(mem, width), HBM),
            ((n * mem_total, 2 * width), bf16, by_step(mem, 2 * width), HBM),
            ((n, heads * mem_total, length), bf16, by_step(SEQS, heads * mem_total, length), HBM),
            ((rows, width), bf16, row, HBM),
            ((rows, width), bf16, row, HBM),
            ((rows, width), bf16, row, HBM),
            ((rows, width), bf16, row, VMEM),
            ((rows, width), bf16, row, VMEM),
            ((rows, width), bf16, row, VMEM),
        ],
        flops=6 * rows * width * width,
        limit=VMEM_LIMIT if mem_total <= 32 else 2 * VMEM_LIMIT,
    )


def feed_forward(bits, act, grad_low, start, w_expand, w_contract, chunk=512):
    rows, width = act.shape
    hidden = w_expand.shape[1]
    steps = hidden // chunk
    half = steps // 2

    def at(i, bits):
        return lax.rem(i + half * (1 - bits[0]), steps)

    def block(place):
        return pl.BlockSpec((2 * chunk, width), lambda i, bits: (place(i), 0))

    return call(
        functools.partial(ffn_kernel, min(rows, 512)),
        (steps,), bits,
        [
            (act, whole(rows, width)), (grad_low, whole(rows, width)), (start, whole(rows, width)),
            (w_expand, pl.BlockSpec((width, chunk), lambda i, bits: (0, at(i, bits)))),
            (w_contract, pl.BlockSpec((chunk, width), lambda i, bits: (at(i, bits), 0))),
        ],
        [
            ((rows, width), bf16, whole(rows, width), HBM),
            ((rows, width), bf16, whole(rows, width), HBM),
            ((hidden, width), bf16, block(lambda i: jnp.minimum(i, half - 1)), HBM),
            ((hidden, width), bf16, block(lambda i: jnp.maximum(i - half, 0)), HBM),
        ],
        [
            pltpu.VMEM((rows, chunk), bf16),
            pltpu.VMEM((rows, chunk), bf16),
            pltpu.VMEM((rows, width), f32),
            pltpu.VMEM((rows, width), f32),
        ],
        flops=12 * rows * width * hidden,
        limit=32,
    )


def cross_backward(bits, grad_normed, late, grad_low, cross, weights, pairs, queries, mid, arrived, attended, w_out, w_query, w_kv, gain_ffn, gain_cross, length, mem_total, deps=()):
    rows, width = queries.shape
    n = rows // length
    block = SEQS * length
    mem = SEQS * mem_total
    heads = width // HEAD
    row = by_step(block, width)
    return call(
        functools.partial(cross_backward_kernel, SEQS, length, width, mem_total),
        (n // SEQS,), bits,
        [
            (grad_normed, row, HBM), (late, row, HBM), (grad_low, row, HBM), (cross, row, HBM),
            (weights, by_step(SEQS, heads * mem_total, length), HBM),
            (pairs, by_step(mem, 2 * width), HBM), (queries, row, HBM), (mid, row, HBM),
            (arrived, by_step(mem, width), HBM), (attended, row, HBM),
            (w_out, whole(width, width), HBM), (w_query, whole(width, width), HBM),
            (w_kv, whole(width, 2 * width), HBM),
            (gain_ffn, whole(1, width)), (gain_cross, whole(1, width)),
        ],
        [
            ((rows, width), bf16, row, HBM),
            ((n * mem_total, width), bf16, whole(n * mem_total, width), HBM),
            ((5 * width // 2, width), bf16, whole(5 * width // 2, width), HBM),
            ((5 * width // 2, width), bf16, whole(5 * width // 2, width), HBM),
        ],
        [
            pltpu.VMEM((5 * width, width), f32),
            pltpu.VMEM((n * mem_total, width), bf16),
        ],
        flops=14 * rows * width * width,
        deps=deps,
        limit=40 if mem_total <= 32 else 56,
    )


def self_backward(bits, gradient, triple, weights, act, w_out, length, deps=()):
    rows, width = gradient.shape
    n = rows // length
    block = SEQS * length
    return call(
        functools.partial(self_backward_kernel, SEQS, length, width),
        (n // SEQS,), bits,
        [
            (gradient, by_step(block, width), HBM), (triple, by_step(block, 3 * width), HBM),
            (weights, by_step(SEQS, width // PAIR, length, 2 * length), HBM),
            (act, by_step(block, width), HBM), (w_out, whole(width, width), HBM),
        ],
        [
            ((rows, 3 * width), bf16, by_step(block, 3 * width), HBM),
            ((3 * width // 2, width), bf16, whole(3 * width // 2, width), HBM),
            ((3 * width // 2, width), bf16, whole(3 * width // 2, width), HBM),
        ],
        [pltpu.VMEM((3 * width, width), f32)],
        flops=14 * rows * width * width,
        limit=40,
        deps=deps,
    )


def token_gradient(bits, gradient, grad_triple, tokens, w_qkv, gain_self, deps=()):
    rows, width = tokens.shape
    block = 512
    row = by_step(block, width)
    return call(
        grad_tokens_kernel, (rows // block,), bits,
        [
            (gradient, row, HBM), (grad_triple, by_step(block, 3 * width), HBM), (tokens, row, HBM),
            (w_qkv, whole(width, 3 * width), HBM), (gain_self, whole(1, width)),
        ],
        [((rows, width), bf16, row)],
        flops=6 * rows * width * width,
        deps=deps,
    )[0]


def after(arrays, deps):
    if not deps:
        return arrays
    return lax.optimization_barrier((*arrays, *deps))[: len(arrays)]


def added(left, right):
    return (left.astype(f32) + right.astype(f32)).astype(bf16)


def exchange(block, bit, devices):
    return lax.ppermute(block, "dp", [(i, i ^ (1 << bit)) for i in range(devices)])


class Lane:
    def __init__(self, devices, orders, send, keep):
        self.devices, self.orders, self.count = devices, orders, len(orders)
        self.rest = list(range(4, devices.bit_length() - 1))
        self.level, self.state = 0, "halve"
        self.own = self.parted(keep)
        self.got = self.parted(exchange(send, 0, devices))
        self.token = send

    def parted(self, block):
        size = block.shape[0] // self.count
        return [block[n * size : (n + 1) * size] for n in range(self.count)]

    def send(self, blocks):
        self.token = blocks[0]
        if self.level in (1, 2):
            bits = [order[self.level - 1] for order in self.orders]
            self.got = [exchange(b, bit, self.devices) for b, bit in zip(blocks, bits)]
        else:
            bit = {0: 0, 3: 3}.get(self.level, self.level)
            whole_block = jnp.concatenate(blocks) if len(blocks) > 1 else blocks[0]
            self.token = whole_block
            self.got = self.parted(exchange(whole_block, bit, self.devices))

    def advance(self, deps=()):
        both = after((*self.own, *self.got), deps)
        own, got = both[: self.count], both[self.count :]
        if self.state == "halve":
            half = own[0].shape[0] // 2
            self.own = [added(a[half:], b[half:]) for a, b in zip(own, got)]
            self.level += 1
            self.send([added(a[:half], b[:half]) for a, b in zip(own, got)])
            if self.level == 3:
                self.state = "whole"
        elif self.state == "whole":
            self.own = [added(a, b) for a, b in zip(own, got)]
            if self.rest:
                self.level = self.rest.pop(0)
            else:
                self.level, self.state = 3, "join"
            self.send(self.own)
        else:
            self.own = [jnp.concatenate([b, a]) for a, b in zip(own, got)]
            self.level -= 1
            self.send(self.own)
            if self.level == 0:
                self.state = "done"

    def result(self):
        return [blocks[0] if self.count == 1 else jnp.concatenate(blocks) for blocks in (self.own, self.got)]


def ffn_final(bits, own, got, w_expand, gain, deps=(), chunk=512):
    width, hidden = w_expand.shape
    steps = hidden // chunk

    def source(mine):
        def at(i, bits):
            first = (bits[0] == 0) == mine
            return (jnp.where(first, jnp.minimum(i, steps // 2 - 1), jnp.maximum(i - steps // 2, 0)), 0)

        return pl.BlockSpec((2 * chunk, width), at)

    return call(
        ffn_final_kernel, (steps,), bits,
        [
            (own, source(True)), (got, source(False)),
            (w_expand, pl.BlockSpec((width, chunk), lambda i, bits: (0, i))),
            (gain, whole(1, width)),
        ],
        [
            ((hidden, width), f32, by_step(chunk, width)),
            ((width, hidden), f32, pl.BlockSpec((width, chunk), lambda i, bits: (0, i))),
            ((1, width), f32, whole(1, width)),
        ],
        [pltpu.VMEM((2 * chunk, width), bf16)],
        deps=deps,
    )


def cross_final(bits, own, got, w_query, gain, deps=()):
    width = w_query.shape[0]
    half = width // 2
    part = by_step(half, width)
    column = pl.BlockSpec((1, half), lambda i, bits: (0, i))
    return call(
        cross_final_kernel, (2,), bits,
        [
            (own, whole(*own.shape)), (got, whole(*own.shape)), (w_query, part), (gain, column),
        ],
        [
            ((width, width), f32, part), ((width, width), f32, part),
            ((width, 2 * width), f32, by_step(half, 2 * width)), ((width, width), f32, part),
            ((1, width), f32, column),
        ],
        [pltpu.VMEM(own.shape, bf16)],
        deps=deps,
    )


def self_final(bits, own, got, w_qkv, gain, deps=()):
    width = w_qkv.shape[0]
    half = width // 2
    column = pl.BlockSpec((1, half), lambda i, bits: (0, i))
    return call(
        self_final_kernel, (2,), bits,
        [
            (own, whole(*own.shape)), (got, whole(*own.shape)),
            (w_qkv, by_step(half, 3 * width)), (gain, column),
        ],
        [((width, 3 * width), f32, by_step(half, 3 * width)), ((1, width), f32, column)],
        [pltpu.VMEM(own.shape, bf16)],
        deps=deps,
    )


def local(
    devices, tokens, memory, target_lengths, memory_lengths, grad_output,
    gain_self, w_qkv, w_self_out, gain_cross, w_cross_query, w_cross_kv, w_cross_out,
    gain_ffn, w_expand, w_contract,
):
    seq_count, length, width = tokens.shape
    rows = seq_count * length
    gain_self, gain_cross, gain_ffn = gain_self[None], gain_cross[None], gain_ffn[None]
    flat_tokens = tokens.reshape(rows, width)
    me = lax.axis_index("dp")
    bits = jnp.stack([(me >> b) & 1 for b in range(devices.bit_length() - 1)]).astype(jnp.int32)
    raw = lax.all_to_all(
        memory.reshape(devices, -1, width), "dp", split_axis=0, concat_axis=0, tiled=True
    ).reshape(-1, width)
    mem_total = raw.shape[0] // seq_count
    act_one, triple, self_weights, attended, mid, queries = self_forward(
        bits, flat_tokens, target_lengths, gain_self, w_qkv, w_self_out, gain_cross, w_cross_query, length
    )
    arrived, pairs, cross_weights, cross, late, grad_low, late_near, grad_low_near, act = cross_forward(
        bits, target_lengths, memory_lengths, raw, queries, mid, grad_output.reshape(rows, width),
        w_cross_kv, w_cross_out, gain_ffn, length, mem_total,
    )
    output, grad_normed, send, keep = feed_forward(
        bits, act, grad_low_near, late_near, w_expand, w_contract
    )
    straight, turned = (1, 2), (2, 1)
    lanes = {"ffn": Lane(devices, (straight, turned), send, keep)}
    token, fresh, kept, found = send, {}, {}, {}
    for n, name in enumerate(PLAN):
        deps = [token]
        if PLAN[n - 1] == "self":
            deps.append(grad_memory)
        if name.startswith("end"):
            lane = lanes[name[4:]]
            while lane.state != "done":
                lane.advance(deps)
                deps = [lane.token]
        if name == "cross":
            gradient, grad_arrived, send, keep = cross_backward(
                bits, grad_normed, late, grad_low, cross, cross_weights, pairs, queries, mid, arrived,
                attended, w_cross_out, w_cross_query, w_cross_kv, gain_ffn, gain_cross, length, mem_total,
                deps=deps,
            )
            token = fresh["cross"] = send
            kept["cross"] = keep
        elif name == "self":
            grad_triple, send, keep = self_backward(
                bits, gradient, triple, self_weights, act_one, w_self_out, length, deps=deps
            )
            token = fresh["self"] = send
            kept["self"] = keep
        elif name == "tokens":
            token = grad_tokens = token_gradient(
                bits, gradient, grad_triple, flat_tokens, w_qkv, gain_self, deps=deps
            )
        elif name == "memory":
            grad_memory = lax.all_to_all(
                after((grad_arrived,), deps)[0].reshape(devices, -1, width),
                "dp", split_axis=0, concat_axis=0, tiled=True,
            ).reshape(memory.shape)
        elif name in ("start cross", "start self"):
            name = name[6:]
            order = turned if TURNED[name == "self"] else straight
            lanes[name] = Lane(devices, (order,), after((fresh[name],), deps)[0], kept[name])
        elif name == "end ffn":
            own, got = lanes["ffn"].result()
            found["ffn"] = ffn_final(bits, own, got, w_expand, gain_ffn, deps=deps)
            token = found["ffn"][2]
        elif name == "end cross":
            own, got = lanes["cross"].result()
            found["cross"] = cross_final(bits, own, got, w_cross_query, gain_cross, deps=deps)
            token = found["cross"][4]
        elif name == "end self":
            own, got = lanes["self"].result()
            found["self"] = self_final(bits, own, got, w_qkv, gain_self, deps=deps)
            token = found["self"][1]
        else:
            lane = lanes[name[3:]]
            if lane.state != "done":
                lane.advance(deps)
                token = lane.token
    grad_contract, grad_expand, grad_gain_ffn = found["ffn"]
    grad_cross_out, grad_cross_query, grad_cross_kv, grad_self_out, grad_gain_cross = found["cross"]
    grad_qkv, grad_gain_self = found["self"]
    return (
        output.reshape(tokens.shape),
        grad_tokens.reshape(tokens.shape),
        grad_memory,
        grad_gain_self[0],
        grad_qkv,
        grad_self_out,
        grad_gain_cross[0],
        grad_cross_query,
        grad_cross_kv,
        grad_cross_out,
        grad_gain_ffn[0],
        grad_expand,
        grad_contract,
    )


def solution(mesh):
    rows, columns, copied = P("dp", None, None), P(None, "dp", None), P()
    return jax.shard_map(
        functools.partial(local, mesh.shape["dp"]),
        mesh=mesh,
        in_specs=(rows, columns, P("dp"), P("dp"), rows) + (copied,) * 10,
        out_specs=(rows, rows, columns) + (copied,) * 10,
        check_vma=False,
    )
```

```python
import functools
import jax
import jax.numpy as jnp
from jax import lax
from jax.experimental import pallas as pl
from jax.experimental.pallas import tpu as pltpu
from jax.sharding import PartitionSpec as P

HEAD = 64
PAIR = 128
epsilon = 1e-05
big_negative = -1e30
f32 = jnp.float32
bf16 = jnp.bfloat16
VMEM_LIMIT = 24
HBM = pltpu.HBM
VMEM = pltpu.VMEM


def dot(left, right, left_dim=1, right_dim=0):
    return lax.dot_general(
        left, right, (((left_dim,), (right_dim,)), ((), ())), preferred_element_type=f32
    )


def normalize(hidden):
    centred = hidden - jnp.mean(hidden, axis=-1, keepdims=True)
    spread = lax.rsqrt(jnp.mean(centred * centred, axis=-1, keepdims=True) + epsilon)
    return centred * spread, spread


def norm_backward(gradient, gain, normalized, spread):
    scaled = gradient * gain
    first = jnp.mean(scaled, axis=-1, keepdims=True)
    second = jnp.mean(scaled * normalized, axis=-1, keepdims=True)
    return spread * (scaled - first - normalized * second)


def head_masks(rows):
    lane = lax.broadcasted_iota(jnp.int32, (rows, PAIR), 1)
    first = jnp.where(lane < HEAD, 1.0, 0.0).astype(bf16)
    second = jnp.where(lane >= HEAD, 1.0, 0.0).astype(bf16)
    return first, second


def spread_pair(block, first, second):
    return jnp.concatenate([block * first, block * second], axis=0)


def stack_pair(block):
    half = block.shape[1] // 2
    return jnp.concatenate([block[:, :half], block[:, half:]], axis=0)


def wide_mask(mem_total, width):
    lane = lax.broadcasted_iota(jnp.int32, (mem_total, width), 1)
    parts = [
        jnp.where((lane >= h * HEAD) & (lane < (h + 1) * HEAD), 1.0, 0.0)
        for h in range(width // HEAD)
    ]
    return parts


PARTS = 1
CROSS_GROUP = 4
FF_CHUNK = 512
FF_ROWS = 512
TOKEN_ROWS = 512
FF_LIMIT = 36
LAG = 1


def stagger(parts):
    waiting = [LAG * n for n in range(len(parts))]
    while parts:
        left = []
        for n, part in enumerate(parts):
            if waiting[n]:
                waiting[n] -= 1
                left.append(n)
            elif next(part, part) is not part:
                left.append(n)
        parts, waiting = [parts[n] for n in left], [waiting[n] for n in left]


def self_forward_kernel(
    seqs, length, width,
    bits, lengths, tokens, gain_self, w_qkv, w_out, gain_cross, w_query,
    act, triple, weights, attended, mid, queries,
):
    step = pl.program_id(0)
    first, second = head_masks(length)
    key_at = lax.broadcasted_iota(jnp.int32, (length, 2 * length), 0)
    query_at = lax.broadcasted_iota(jnp.int32, (length, 2 * length), 1)
    query_at = jnp.where(query_at >= length, query_at - length, query_at)
    causal = key_at <= query_at
    count = seqs // PARTS

    def part(n):
        span = slice(n * count * length, (n + 1) * count * length)
        residual = tokens[span, :].astype(f32)
        normal, _ = normalize(residual)
        low = (normal * gain_self[...]).astype(bf16)
        yield
        both = dot(low, w_qkv[...]).astype(bf16)
        yield
        heads = [(s, p) for s in range(count) for p in range(width // PAIR)]
        scores = []
        for s, p in heads:
            rows = slice(s * length, (s + 1) * length)
            q = both[rows, p * PAIR : (p + 1) * PAIR] * 0.125
            k = both[rows, width + p * PAIR : width + (p + 1) * PAIR]
            scores.append(dot(k, spread_pair(q, first, second), 1, 1))
        yield
        softs = []
        for (s, p), score in zip(heads, scores):
            allowed = causal & (key_at < lengths[step * seqs + n * count + s])
            score = jnp.where(allowed, score, big_negative)
            raised = jnp.exp(score - jnp.max(score, axis=0, keepdims=True))
            softs.append((raised * (1.0 / jnp.sum(raised, axis=0, keepdims=True))).astype(bf16))
        yield
        joined = {}
        for (s, p), soft in zip(heads, softs):
            rows = slice(s * length, (s + 1) * length)
            v = both[rows, 2 * width + p * PAIR : 2 * width + (p + 1) * PAIR]
            joined[s, p] = dot(stack_pair(soft), spread_pair(v, first, second), 0, 0).astype(bf16)
        yield
        out = jnp.concatenate(
            [
                jnp.concatenate([joined[s, p] for p in range(width // PAIR)], axis=1)
                for s in range(count)
            ],
            axis=0,
        )
        residual = residual + dot(out, w_out[...])
        yield
        normal, _ = normalize(residual)
        after = (normal * gain_cross[...]).astype(bf16)
        yield
        found = dot(after, w_query[...]).astype(bf16)
        yield
        act[span, :] = low
        triple[span, :] = both
        attended[span, :] = out
        mid[span, :] = residual.astype(bf16)
        queries[span, :] = found
        for (s, p), soft in zip(heads, softs):
            weights[n * count + s, p] = soft

    stagger([part(n) for n in range(PARTS)])


def cross_forward_kernel(
    seqs, length, width, mem_total,
    bits, lengths, memory_lengths, raw, queries, mid, grad_output, w_kv, w_out, gain_ffn,
    arrived, pairs, weights, cross, late, grad_low, late_near, grad_low_near, act,
):
    step = pl.program_id(0)
    total = raw.shape[0] // mem_total
    at = lax.broadcasted_iota(jnp.int32, (mem_total, raw.shape[0]), 0) * total
    column = lax.broadcasted_iota(jnp.int32, (mem_total, raw.shape[0]), 1)
    own_rows = jnp.concatenate(
        [jnp.where(column == at + (step * seqs + s), 1.0, 0.0).astype(bf16) for s in range(seqs)],
        axis=0,
    )
    own_rows = dot(own_rows, raw[...]).astype(bf16)
    arrived[...] = own_rows
    both = dot(own_rows, w_kv[...]).astype(bf16)
    pairs[...] = both
    mask = jnp.concatenate(wide_mask(mem_total, width), axis=0).astype(bf16)
    heads = width // HEAD
    key_at = lax.broadcasted_iota(jnp.int32, (mem_total, length), 0)
    row_at = lax.broadcasted_iota(jnp.int32, (length, width), 0)

    def spread(s, at):
        return jnp.concatenate([both[s * mem_total : (s + 1) * mem_total, at]] * heads, axis=0) * mask

    scores = []
    for s in range(seqs):
        q = queries[s * length : (s + 1) * length, :] * 0.125
        scores.append(dot(spread(s, slice(0, width)), q, 1, 1).reshape(heads, mem_total, length))
    softs = []
    for s in range(seqs):
        allowed = (key_at < memory_lengths[step * seqs + s])[None]
        score = jnp.where(allowed, scores[s], big_negative)
        raised = jnp.exp(score - jnp.max(score, axis=1, keepdims=True))
        soft = raised * (1.0 / jnp.sum(raised, axis=1, keepdims=True))
        softs.append(soft.reshape(heads * mem_total, length).astype(bf16))
    joined = [dot(softs[s], spread(s, slice(width, 2 * width)), 0, 0).astype(bf16) for s in range(seqs)]
    low = jnp.concatenate(joined, axis=0)
    cross[...] = low
    for s in range(seqs):
        rows = slice(s * length, (s + 1) * length)
        weights[s] = softs[s]
        live = row_at < lengths[step * seqs + s]
        masked = jnp.where(live, grad_output[rows, :].astype(f32), 0.0).astype(bf16)
        grad_low[rows, :] = masked
        grad_low_near[rows, :] = masked
    residual = mid[...].astype(f32) + dot(low, w_out[...])
    late[...] = residual.astype(bf16)
    late_near[...] = residual.astype(bf16)
    normal, _ = normalize(residual)
    act[...] = (normal * gain_ffn[...]).astype(bf16)


def gelu_parts(value):
    half = 0.5 + 0.5 * lax.erf(value * 0.7071067811865476)
    bell = value * jnp.exp2(value * value * (-0.5 * 1.4426950408889634))
    return value * half, half + 0.3989422804014327 * bell


def place(bits, n, turned=None):
    first, second = bits[1], bits[2]
    if turned is not None:
        first, second = jnp.where(turned, second, first), jnp.where(turned, first, second)
    mine = first * 4 + second * 2 + bits[3]
    return jnp.bitwise_xor(mine, 7 - n)


def ffn_kernel(
    row_block,
    bits, act, grad_low, start, w_expand, w_contract,
    result, grad_normed, send, keep,
    activated, grad_expanded, total, change,
):
    step = pl.program_id(0)
    rows = act.shape[0]
    chunk = w_expand.shape[1]

    @pl.when(step == 0)
    def _():
        total[...] = start[...].astype(f32)
        change[...] = jnp.zeros_like(change)

    for b in range(rows // row_block):
        r = slice(b * row_block, (b + 1) * row_block)
        expanded = dot(act[r, :], w_expand[...])
        grad_activated = dot(grad_low[r, :], w_contract[...], 1, 1)
        value, slope = gelu_parts(expanded)
        value = value.astype(bf16)
        slope = (grad_activated * slope).astype(bf16)
        activated[r, :] = value
        grad_expanded[r, :] = slope
        total[r, :] += dot(value, w_contract[...])
        change[r, :] += dot(slope, w_expand[...], 1, 1)

    def fill(grads):
        unit = grad_low.shape[1]
        size = unit // 4
        contract = dot(activated[...], grad_low[...], 0, 0)
        expand = dot(act[...], grad_expanded[...], 0, 0)
        for k in range(chunk // unit):
            found = [contract[k * unit : (k + 1) * unit, :], expand[:, k * unit : (k + 1) * unit]]
            turned = lax.rem(step * (chunk // unit) + k, 2) == 1
            for n in range(8):
                at = k * 2 * unit + place(bits, n, turned) * size
                at = pl.ds(pl.multiple_of(at, size), size)
                grads[at, :] = found[n // 4][n % 4 * size : (n % 4 + 1) * size, :].astype(bf16)

    @pl.when(step < pl.num_programs(0) // 2)
    def _():
        fill(send)

    @pl.when(step >= pl.num_programs(0) // 2)
    def _():
        fill(keep)

    @pl.when(step == pl.num_programs(0) - 1)
    def _():
        result[...] = total[...].astype(bf16)
        grad_normed[...] = change[...].astype(bf16)


def give_rows(bits, start, low, high, send, keep, size, turned):
    first = bits[0] == 0
    for side, one, other in ((keep, low, high), (send, high, low)):
        rows = jnp.where(first, one, other)
        at, end = start, start + low.shape[0]
        while at < end:
            part = at // size
            stop = min(end, (part + 1) * size)
            to = place(bits, part, turned) * size + (at - part * size)
            to = pl.ds(pl.multiple_of(to, 32), stop - at)
            side[to, :] = rows[at - start : stop - start, :]
            at = stop


def cross_backward_kernel(
    length, mem_total,
    bits, grad_normed_far, late_far, grad_low_far, cross_far, weights_far, pairs_far, queries_far, mid_far,
    arrived_far, attended_far, w_out_far, w_query_far, w_kv_far, gain_ffn, gain_cross,
    gradient, grad_arrived, send, keep,
    grad_normed, late, grad_low, cross, weights, pairs, queries, mid,
    arrived, attended, w_out, w_query, w_kv,
    running, low_queries, out, low_pairs, arrival,
):
    rows, width = grad_normed.shape
    seqs = rows // length
    heads = width // HEAD
    blocks = [slice(n * rows // 4, (n + 1) * rows // 4) for n in range(4)]
    copies = []

    def fetch(far, near):
        copy = pltpu.make_async_copy(far, near, arrival.at[len(copies)])
        copies.append(copy)
        copy.start()
        return copy

    def fetch_rows(n):
        return [
            fetch(far.at[blocks[n], :], near.at[blocks[n], :])
            for far, near in ((grad_normed_far, grad_normed), (late_far, late), (grad_low_far, grad_low))
        ]

    waiting = [fetch_rows(0), fetch_rows(1)]
    copy_out = fetch(w_out_far, w_out)
    masks = wide_mask(mem_total, width)
    mask = jnp.concatenate(masks, axis=0).astype(bf16)
    grad_cross = []
    for n in range(4):
        for copy in waiting[n]:
            copy.wait()
        if n < 2:
            waiting.append(fetch_rows(n + 2))
        if n == 1:
            early = [fetch(weights_far, weights), fetch(pairs_far, pairs), fetch(queries_far, queries)]
        if n == 2:
            later = [fetch(w_query_far, w_query), fetch(mid_far, mid)]
        if n == 3:
            last = [
                fetch(cross_far, cross), fetch(arrived_far, arrived), fetch(w_kv_far, w_kv),
                fetch(attended_far, attended),
            ]
        normal, spread = normalize(late[blocks[n], :].astype(f32))
        change = norm_backward(grad_normed[blocks[n], :].astype(f32), gain_ffn[...], normal, spread)
        change = grad_low[blocks[n], :].astype(f32) + change
        running[blocks[n], :] = change
        low = change.astype(bf16)
        grad_normed[blocks[n], :] = low
        if n == 0:
            copy_out.wait()
        grad_cross.append(dot(low, w_out[...], 1, 1).astype(bf16))
    grad_cross = jnp.concatenate(grad_cross, axis=0)

    def widen(s, at):
        return jnp.concatenate([pairs[s * mem_total : (s + 1) * mem_total, at]] * heads, axis=0) * mask

    def narrow(block):
        return sum(block[h * mem_total : (h + 1) * mem_total, :] * masks[h] for h in range(heads))

    for copy in early:
        copy.wait()
    for start in range(0, seqs, CROSS_GROUP):
        group = range(start, start + CROSS_GROUP)
        softs = [weights[s] for s in group]
        grads = [grad_cross[s * length : (s + 1) * length, :] for s in group]
        changes = [
            dot(widen(s, slice(width, 2 * width)), grad, 1, 1).reshape(heads, mem_total, length)
            for s, grad in zip(group, grads)
        ]
        values = [dot(soft, grad) for soft, grad in zip(softs, grads)]
        scores = []
        for soft, change in zip(softs, changes):
            soft = soft.astype(f32).reshape(heads, mem_total, length)
            product = soft * change
            score = product - soft * jnp.sum(product, axis=1, keepdims=True)
            scores.append(score.reshape(heads * mem_total, length).astype(bf16))
        for s, score in zip(group, scores):
            low_queries[s * length : (s + 1) * length, :] = (
                dot(score, widen(s, slice(0, width)), 0, 0) * 0.125
            ).astype(bf16)
        keys = [
            dot(score, queries[s * length : (s + 1) * length, :]) for s, score in zip(group, scores)
        ]
        for s, key, value in zip(group, keys, values):
            at = slice(s * mem_total, (s + 1) * mem_total)
            low_pairs[at, :width] = (narrow(key) * 0.125).astype(bf16)
            low_pairs[at, width:] = narrow(value).astype(bf16)
    for copy in later + last:
        copy.wait()
    half = width // 2

    def give(n, left, right):
        found = dot(left[...], right, 0, 0).astype(bf16)
        size = send.shape[0] // 8
        give_rows(bits, n * half, found[:half], found[half:], send, keep, size, TURNED[0])

    give(0, cross, grad_normed[...])
    sent = []
    for n in range(4):
        back = dot(low_queries[blocks[n], :], w_query[...], 1, 1)
        normal, spread = normalize(mid[blocks[n], :].astype(f32))
        mid[blocks[n], :] = (normal * gain_cross[...]).astype(bf16)
        low = (running[blocks[n], :] + norm_backward(back, gain_cross[...], normal, spread)).astype(bf16)
        out[blocks[n], :] = low
        copy = pltpu.make_async_copy(
            out.at[blocks[n], :], gradient.at[blocks[n], :], arrival.at[len(copies) + n]
        )
        copy.start()
        sent.append(copy)
    give(1, mid, low_queries[...])
    give(2, arrived, low_pairs[:, :width])
    give(3, arrived, low_pairs[:, width:])
    give(4, attended, out[...])
    grad_rows = dot(low_pairs[...], w_kv[...], 1, 1).astype(bf16)
    count = seqs
    total = grad_rows.shape[0]
    block = min(total, 512)
    for start in range(0, total, block):
        row = lax.broadcasted_iota(jnp.int32, (block, total), 0) + start
        column = lax.broadcasted_iota(jnp.int32, (block, total), 1)
        shift = count.bit_length() - 1
        source = (row & (count - 1)) * mem_total + (row >> shift)
        order = jnp.where(column == source, 1.0, 0.0).astype(bf16)
        grad_arrived[start : start + block, :] = dot(order, grad_rows).astype(bf16)
    for copy in sent:
        copy.wait()


def self_backward_kernel(
    length,
    bits, gradient_far, triple_far, weights_far, act_far, w_out_far,
    grad_triple_far, send, keep,
    gradient, triple, weights, act, w_out, grad_triple, arrival,
):
    rows, width = gradient.shape
    seqs = rows // length // 4
    blocks = [slice(n * rows // 4, (n + 1) * rows // 4) for n in range(4)]
    copies = []

    def move(source, target):
        copy = pltpu.make_async_copy(source, target, arrival.at[len(copies)])
        copies.append(copy)
        copy.start()
        return copy

    def fetch(n):
        own = slice(n * seqs, (n + 1) * seqs)
        return [
            move(gradient_far.at[blocks[n], :], gradient.at[blocks[n], :]),
            move(triple_far.at[blocks[n], :], triple.at[blocks[n], :]),
            move(weights_far.at[own], weights.at[own]),
        ]

    ready = [move(w_out_far, w_out)]
    waiting = [fetch(0), fetch(1)]
    first, second = head_masks(length)
    sent = []
    for n in range(4):
        for copy in waiting[n] + ready:
            copy.wait()
        ready = []
        if n < 2:
            waiting.append(fetch(n + 2))
        if n == 2:
            late = move(act_far, act)
        low = dot(gradient[blocks[n], :], w_out[...], 1, 1).astype(bf16)
        group = []
        for s in range(n * seqs, (n + 1) * seqs):
            for p in range(width // PAIR):
                at = [slice(j * width + p * PAIR, j * width + (p + 1) * PAIR) for j in range(3)]
                group.append((s, p, slice(s * length, (s + 1) * length), at))
        grads = [
            spread_pair(low[(s - n * seqs) * length : (s + 1 - n * seqs) * length, at[0]], first, second)
            for s, p, span, at in group
        ]
        softs = [weights[s, p] for s, p, span, at in group]
        changes = [dot(triple[span, at[2]], grad, 1, 1) for (s, p, span, at), grad in zip(group, grads)]
        values = [dot(soft, grad).astype(bf16) for soft, grad in zip(softs, grads)]
        scores = []
        for soft, change in zip(softs, changes):
            soft = soft.astype(f32)
            product = soft * change
            scores.append((product - soft * jnp.sum(product, axis=0, keepdims=True)).astype(bf16))
        keys = [
            dot(score, spread_pair(triple[span, at[0]] * 0.125, first, second)).astype(bf16)
            for (s, p, span, at), score in zip(group, scores)
        ]
        queries = [
            (dot(stack_pair(score), spread_pair(triple[span, at[1]], first, second), 0, 0) * 0.125).astype(bf16)
            for (s, p, span, at), score in zip(group, scores)
        ]
        for k, (s, p, span, at) in enumerate(group):
            grad_triple[span, at[0]] = queries[k]
            grad_triple[span, at[1]] = keys[k]
            grad_triple[span, at[2]] = values[k]
        sent.append(move(grad_triple.at[blocks[n], :], grad_triple_far.at[blocks[n], :]))
    late.wait()
    half = width // 2
    for j in range(3):
        found = dot(act[...], grad_triple[:, j * width : (j + 1) * width], 0, 0).astype(bf16)
        give_rows(bits, j * half, found[:half], found[half:], send, keep, send.shape[0] // 8, TURNED[1])
    for copy in sent:
        copy.wait()


def grad_tokens_kernel(bits, gradient, grad_triple, tokens, w_qkv, gain_self, grad_tokens):
    normal, spread = normalize(tokens[...].astype(f32))
    change = norm_backward(dot(grad_triple[...], w_qkv[...], 1, 1), gain_self[...], normal, spread)
    grad_tokens[...] = (gradient[...].astype(f32) + change).astype(bf16)


def row_sums(weight, grad, gain):
    product = weight.astype(f32) * grad
    columns = sum(product[:, n : n + PAIR] for n in range(0, product.shape[1], PAIR))
    return jnp.sum(columns.T, axis=0, keepdims=True) / gain


def in_order(bits, mine, own, got, ordered, turned):
    size = ordered.shape[0] // 8

    def fill(source):
        for n in range(8):
            at = pl.ds(pl.multiple_of(place(bits, n, turned) * size, size), size)
            ordered[n * size : (n + 1) * size, :] = source[at, :]

    @pl.when(mine)
    def _():
        fill(own)

    @pl.when(jnp.logical_not(mine))
    def _():
        fill(got)


def ffn_final_kernel(bits, own, got, w_expand, gain, contract, expand, gain_grad, ordered):
    step = pl.program_id(0)
    chunk = expand.shape[1]
    half = pl.num_programs(0) // 2
    in_order(bits, (step >= half) == (bits[0] == 1), own, got, ordered, lax.rem(step, half) == 1)
    contract[...] = ordered[:chunk, :].astype(f32)
    grad = ordered[chunk:, :].astype(f32)
    expand[...] = grad
    sums = row_sums(w_expand[...], grad, gain[...])

    @pl.when(step == 0)
    def _():
        gain_grad[...] = sums

    @pl.when(step > 0)
    def _():
        gain_grad[...] += sums


def cross_final_kernel(bits, own, got, w_query, gain, cross_out, query, pair, self_out, gain_grad, ordered):
    half, width = query.shape
    in_order(bits, pl.program_id(0) == bits[0], own, got, ordered, TURNED[0])
    cross_out[...] = ordered[:half, :].astype(f32)
    grad = ordered[half : 2 * half, :].astype(f32)
    query[...] = grad
    pair[:, :width] = ordered[2 * half : 3 * half, :].astype(f32)
    pair[:, width:] = ordered[3 * half : 4 * half, :].astype(f32)
    self_out[...] = ordered[4 * half :, :].astype(f32)
    gain_grad[...] = row_sums(w_query[...], grad, gain[...])


def self_final_kernel(bits, own, got, w_qkv, gain, qkv, gain_grad, ordered):
    half = qkv.shape[0]
    width = own.shape[1]
    in_order(bits, pl.program_id(0) == bits[0], own, got, ordered, TURNED[1])
    for j in range(3):
        qkv[:, j * width : (j + 1) * width] = ordered[j * half : (j + 1) * half, :].astype(f32)
    gain_grad[...] = row_sums(w_qkv[...], qkv[...], gain[...])


def call(kernel, grid, bits, ins, outs, scratch=(), flops=0, deps=(), limit=VMEM_LIMIT):
    moved = sum(a.size * a.dtype.itemsize for a, *_ in ins)
    shapes = []
    for shape, dtype, _, *space in outs:
        size = 1
        for n in shape:
            size *= n
        moved += size * jnp.dtype(dtype).itemsize
        shapes.append(space[0](shape, dtype) if space else jax.ShapeDtypeStruct(shape, dtype))
    count = len(ins)
    arrays = [
        pltpu.with_memory_space_constraint(a, space[0]) if space else a for a, _, *space in ins
    ]

    def body(bits_ref, *refs):
        kernel(bits_ref, *refs[:count], *refs[count + len(deps) :])

    return pl.pallas_call(
        body,
        grid_spec=pltpu.PrefetchScalarGridSpec(
            num_scalar_prefetch=1,
            grid=grid,
            in_specs=[spec for _, spec, *_ in ins] + [pl.BlockSpec(memory_space=pl.ANY)] * len(deps),
            out_specs=[spec for _, _, spec, *_ in outs],
            scratch_shapes=list(scratch),
        ),
        out_shape=shapes,
        compiler_params=pltpu.CompilerParams(vmem_limit_bytes=limit * 1024 * 1024),
        cost_estimate=pl.CostEstimate(flops=flops, bytes_accessed=moved, transcendentals=0),
    )(bits, *arrays, *deps)


def by_step(*shape):
    return pl.BlockSpec(shape, lambda i, bits: (i,) + (0,) * (len(shape) - 1))


def whole(*shape):
    return pl.BlockSpec(shape, lambda i, bits: (0,) * len(shape))


def scalars():
    return pl.BlockSpec(memory_space=pltpu.SMEM)


SEQS = 4
GROUP = 16
TURNED = (True, None)
PLAN = (
    "do ffn",
    "cross",
    "do ffn",
    "start cross",
    "do cross",
    "do ffn",
    "memory",
    "self",
    "do ffn",
    "do cross",
    "start self",
    "do self",
    "do cross",
    "do ffn",
    "do cross",
    "do self",
    "do ffn",
    "do self",
    "do cross",
    "do ffn",
    "do self",
    "do cross",
    "do self",
    "do self",
    "do ffn",
    "do cross",
    "do self",
    "tokens",
    "do self",
    "do cross",
    "end ffn",
    "end self",
    "end cross",
)


def self_forward(bits, tokens, lengths, gain_self, w_qkv, w_out, gain_cross, w_query, length):
    rows, width = tokens.shape
    n = rows // length
    block = SEQS * length
    row = by_step(block, width)
    return call(
        functools.partial(self_forward_kernel, SEQS, length, width),
        (n // SEQS,), bits,
        [
            (lengths, scalars()), (tokens, row, HBM),
            (gain_self, whole(1, width)), (w_qkv, whole(width, 3 * width), HBM),
            (w_out, whole(width, width), HBM), (gain_cross, whole(1, width)),
            (w_query, whole(width, width), HBM),
        ],
        [
            ((rows, width), bf16, row, HBM),
            ((rows, 3 * width), bf16, by_step(block, 3 * width), HBM),
            ((n, width // PAIR, length, 2 * length), bf16, by_step(SEQS, width // PAIR, length, 2 * length), HBM),
            ((rows, width), bf16, row, HBM),
            ((rows, width), bf16, row, HBM),
            ((rows, width), bf16, row, HBM),
        ],
        flops=12 * rows * width * width,
        limit=36,
    )


def cross_forward(bits, lengths, memory_lengths, raw, queries, mid, grad_output, w_kv, w_out, gain_ffn, length, mem_total):
    rows, width = queries.shape
    n = rows // length
    block = SEQS * length
    mem = SEQS * mem_total
    heads = width // HEAD
    row = by_step(block, width)
    return call(
        functools.partial(cross_forward_kernel, SEQS, length, width, mem_total),
        (n // SEQS,), bits,
        [
            (lengths, scalars()), (memory_lengths, scalars()),
            (raw, whole(*raw.shape)), (queries, row, HBM),
            (mid, row, HBM), (grad_output, row, HBM),
            (w_kv, whole(width, 2 * width)), (w_out, whole(width, width)),
            (gain_ffn, whole(1, width)),
        ],
        [
            ((n * mem_total, width), bf16, by_step(mem, width), HBM),
            ((n * mem_total, 2 * width), bf16, by_step(mem, 2 * width), HBM),
            ((n, heads * mem_total, length), bf16, by_step(SEQS, heads * mem_total, length), HBM),
            ((rows, width), bf16, row, HBM),
            ((rows, width), bf16, row, HBM),
            ((rows, width), bf16, row, HBM),
            ((rows, width), bf16, row, VMEM),
            ((rows, width), bf16, row, VMEM),
            ((rows, width), bf16, row, VMEM),
        ],
        flops=6 * rows * width * width,
        limit=VMEM_LIMIT if mem_total <= 32 else 2 * VMEM_LIMIT,
    )


def feed_forward(bits, act, grad_low, start, w_expand, w_contract, chunk=FF_CHUNK):
    rows, width = act.shape
    hidden = w_expand.shape[1]
    steps = hidden // chunk
    half = steps // 2

    def at(i, bits):
        return lax.rem(i + half * (1 - bits[0]), steps)

    def block(place):
        return pl.BlockSpec((2 * chunk, width), lambda i, bits: (place(i), 0))

    return call(
        functools.partial(ffn_kernel, min(rows, FF_ROWS)),
        (steps,), bits,
        [
            (act, whole(rows, width)), (grad_low, whole(rows, width)), (start, whole(rows, width)),
            (w_expand, pl.BlockSpec((width, chunk), lambda i, bits: (0, at(i, bits)))),
            (w_contract, pl.BlockSpec((chunk, width), lambda i, bits: (at(i, bits), 0))),
        ],
        [
            ((rows, width), bf16, whole(rows, width), HBM),
            ((rows, width), bf16, whole(rows, width), HBM),
            ((hidden, width), bf16, block(lambda i: jnp.minimum(i, half - 1)), HBM),
            ((hidden, width), bf16, block(lambda i: jnp.maximum(i - half, 0)), HBM),
        ],
        [
            pltpu.VMEM((rows, chunk), bf16),
            pltpu.VMEM((rows, chunk), bf16),
            pltpu.VMEM((rows, width), f32),
            pltpu.VMEM((rows, width), f32),
        ],
        flops=12 * rows * width * hidden,
        limit=FF_LIMIT,
    )


def cross_backward(bits, grad_normed, late, grad_low, cross, weights, pairs, queries, mid, arrived, attended, w_out, w_query, w_kv, gain_ffn, gain_cross, length, mem_total, deps=()):
    rows, width = queries.shape
    far = [
        grad_normed, late, grad_low, cross, weights, pairs, queries, mid, arrived, attended,
        w_out, w_query, w_kv,
    ]
    anywhere = pl.BlockSpec(memory_space=pl.ANY)
    return call(
        functools.partial(cross_backward_kernel, length, mem_total),
        (1,), bits,
        [(a, anywhere, HBM) for a in far]
        + [(gain_ffn, whole(1, width)), (gain_cross, whole(1, width))],
        [
            ((rows, width), bf16, anywhere, HBM),
            (arrived.shape, bf16, whole(*arrived.shape), HBM),
            ((5 * width // 2, width), bf16, whole(5 * width // 2, width), HBM),
            ((5 * width // 2, width), bf16, whole(5 * width // 2, width), HBM),
        ],
        [pltpu.VMEM(a.shape, bf16) for a in far]
        + [
            pltpu.VMEM((rows, width), f32),
            pltpu.VMEM((rows, width), bf16),
            pltpu.VMEM((rows, width), bf16),
            pltpu.VMEM(pairs.shape, bf16),
            pltpu.SemaphoreType.DMA((32,)),
        ],
        flops=14 * rows * width * width,
        deps=deps,
        limit=48 if mem_total <= 32 else 62,
    )


def self_backward(bits, gradient, triple, weights, act, w_out, length, deps=()):
    rows, width = gradient.shape
    far = [gradient, triple, weights, act, w_out]
    anywhere = pl.BlockSpec(memory_space=pl.ANY)
    return call(
        functools.partial(self_backward_kernel, length),
        (1,), bits,
        [(a, anywhere, HBM) for a in far],
        [
            (triple.shape, bf16, anywhere, HBM),
            ((3 * width // 2, width), bf16, whole(3 * width // 2, width), HBM),
            ((3 * width // 2, width), bf16, whole(3 * width // 2, width), HBM),
        ],
        [pltpu.VMEM(a.shape, bf16) for a in far]
        + [pltpu.VMEM(triple.shape, bf16), pltpu.SemaphoreType.DMA((24,))],
        flops=14 * rows * width * width,
        deps=deps,
        limit=44,
    )


def token_gradient(bits, gradient, grad_triple, tokens, w_qkv, gain_self, deps=()):
    rows, width = tokens.shape
    block = TOKEN_ROWS
    row = by_step(block, width)
    return call(
        grad_tokens_kernel, (rows // block,), bits,
        [
            (gradient, row, HBM), (grad_triple, by_step(block, 3 * width), HBM), (tokens, row, HBM),
            (w_qkv, whole(width, 3 * width), HBM), (gain_self, whole(1, width)),
        ],
        [((rows, width), bf16, row)],
        flops=6 * rows * width * width,
        deps=deps,
    )[0]


def after(arrays, deps):
    if not deps:
        return arrays
    return lax.optimization_barrier((*arrays, *deps))[: len(arrays)]


def added(left, right):
    return (left.astype(f32) + right.astype(f32)).astype(bf16)


def exchange(block, bit, devices):
    return lax.ppermute(block, "dp", [(i, i ^ (1 << bit)) for i in range(devices)])


class Lane:
    def __init__(self, devices, orders, send, keep):
        self.devices, self.orders, self.count = devices, orders, len(orders)
        self.rest = list(range(4, devices.bit_length() - 1))
        self.level, self.state = 0, "halve"
        self.own = self.parted(keep)
        self.got = self.parted(exchange(send, 0, devices))
        self.token = send

    def parted(self, block):
        size = block.shape[0] // self.count
        return [block[n * size : (n + 1) * size] for n in range(self.count)]

    def send(self, blocks):
        self.token = blocks[0]
        if self.level in (1, 2):
            bits = [order[self.level - 1] for order in self.orders]
            self.got = [exchange(b, bit, self.devices) for b, bit in zip(blocks, bits)]
        else:
            bit = {0: 0, 3: 3}.get(self.level, self.level)
            whole_block = jnp.concatenate(blocks) if len(blocks) > 1 else blocks[0]
            self.token = whole_block
            self.got = self.parted(exchange(whole_block, bit, self.devices))

    def advance(self, deps=()):
        both = after((*self.own, *self.got), deps)
        own, got = both[: self.count], both[self.count :]
        if self.state == "halve":
            half = own[0].shape[0] // 2
            self.own = [added(a[half:], b[half:]) for a, b in zip(own, got)]
            self.level += 1
            self.send([added(a[:half], b[:half]) for a, b in zip(own, got)])
            if self.level == 3:
                self.state = "whole"
        elif self.state == "whole":
            self.own = [added(a, b) for a, b in zip(own, got)]
            if self.rest:
                self.level = self.rest.pop(0)
            else:
                self.level, self.state = 3, "join"
            self.send(self.own)
        else:
            self.own = [jnp.concatenate([b, a]) for a, b in zip(own, got)]
            self.level -= 1
            self.send(self.own)
            if self.level == 0:
                self.state = "done"

    def result(self):
        return [blocks[0] if self.count == 1 else jnp.concatenate(blocks) for blocks in (self.own, self.got)]


def ffn_final(bits, own, got, w_expand, gain, deps=(), chunk=512):
    width, hidden = w_expand.shape
    steps = hidden // chunk

    def source(mine):
        def at(i, bits):
            first = (bits[0] == 0) == mine
            return (jnp.where(first, jnp.minimum(i, steps // 2 - 1), jnp.maximum(i - steps // 2, 0)), 0)

        return pl.BlockSpec((2 * chunk, width), at)

    return call(
        ffn_final_kernel, (steps,), bits,
        [
            (own, source(True)), (got, source(False)),
            (w_expand, pl.BlockSpec((width, chunk), lambda i, bits: (0, i))),
            (gain, whole(1, width)),
        ],
        [
            ((hidden, width), f32, by_step(chunk, width)),
            ((width, hidden), f32, pl.BlockSpec((width, chunk), lambda i, bits: (0, i))),
            ((1, width), f32, whole(1, width)),
        ],
        [pltpu.VMEM((2 * chunk, width), bf16)],
        deps=deps,
    )


def cross_final(bits, own, got, w_query, gain, deps=()):
    width = w_query.shape[0]
    half = width // 2
    part = by_step(half, width)
    column = pl.BlockSpec((1, half), lambda i, bits: (0, i))
    return call(
        cross_final_kernel, (2,), bits,
        [
            (own, whole(*own.shape)), (got, whole(*own.shape)), (w_query, part), (gain, column),
        ],
        [
            ((width, width), f32, part), ((width, width), f32, part),
            ((width, 2 * width), f32, by_step(half, 2 * width)), ((width, width), f32, part),
            ((1, width), f32, column),
        ],
        [pltpu.VMEM(own.shape, bf16)],
        deps=deps,
    )


def self_final(bits, own, got, w_qkv, gain, deps=()):
    width = w_qkv.shape[0]
    half = width // 2
    column = pl.BlockSpec((1, half), lambda i, bits: (0, i))
    return call(
        self_final_kernel, (2,), bits,
        [
            (own, whole(*own.shape)), (got, whole(*own.shape)),
            (w_qkv, by_step(half, 3 * width)), (gain, column),
        ],
        [((width, 3 * width), f32, by_step(half, 3 * width)), ((1, width), f32, column)],
        [pltpu.VMEM(own.shape, bf16)],
        deps=deps,
    )


def local(
    devices, tokens, memory, target_lengths, memory_lengths, grad_output,
    gain_self, w_qkv, w_self_out, gain_cross, w_cross_query, w_cross_kv, w_cross_out,
    gain_ffn, w_expand, w_contract,
):
    seq_count, length, width = tokens.shape
    rows = seq_count * length
    gain_self, gain_cross, gain_ffn = gain_self[None], gain_cross[None], gain_ffn[None]
    flat_tokens = tokens.reshape(rows, width)
    me = lax.axis_index("dp")
    bits = jnp.stack([(me >> b) & 1 for b in range(devices.bit_length() - 1)]).astype(jnp.int32)
    raw = lax.all_to_all(
        memory.reshape(devices, -1, width), "dp", split_axis=0, concat_axis=0, tiled=True
    ).reshape(-1, width)
    mem_total = raw.shape[0] // seq_count
    act_one, triple, self_weights, attended, mid, queries = self_forward(
        bits, flat_tokens, target_lengths, gain_self, w_qkv, w_self_out, gain_cross, w_cross_query, length
    )
    arrived, pairs, cross_weights, cross, late, grad_low, late_near, grad_low_near, act = cross_forward(
        bits, target_lengths, memory_lengths, raw, queries, mid, grad_output.reshape(rows, width),
        w_cross_kv, w_cross_out, gain_ffn, length, mem_total,
    )
    output, grad_normed, send, keep = feed_forward(
        bits, act, grad_low_near, late_near, w_expand, w_contract
    )
    straight, turned = (1, 2), (2, 1)
    lanes = {"ffn": Lane(devices, (straight, turned), send, keep)}
    token, fresh, kept, found = send, {}, {}, {}
    for n, name in enumerate(PLAN):
        deps = [token]
        if PLAN[n - 1] == "self":
            deps.append(grad_memory)
        if name.startswith("end"):
            lane = lanes[name[4:]]
            while lane.state != "done":
                lane.advance(deps)
                deps = [lane.token]
        if name == "cross":
            gradient, grad_arrived, send, keep = cross_backward(
                bits, grad_normed, late, grad_low, cross, cross_weights, pairs, queries, mid, arrived,
                attended, w_cross_out, w_cross_query, w_cross_kv, gain_ffn, gain_cross, length, mem_total,
                deps=deps,
            )
            token = fresh["cross"] = send
            kept["cross"] = keep
        elif name == "self":
            grad_triple, send, keep = self_backward(
                bits, gradient, triple, self_weights, act_one, w_self_out, length, deps=deps
            )
            token = fresh["self"] = send
            kept["self"] = keep
        elif name == "tokens":
            token = grad_tokens = token_gradient(
                bits, gradient, grad_triple, flat_tokens, w_qkv, gain_self, deps=deps
            )
        elif name == "memory":
            grad_memory = lax.all_to_all(
                after((grad_arrived,), deps)[0].reshape(devices, -1, width),
                "dp", split_axis=0, concat_axis=0, tiled=True,
            ).reshape(memory.shape)
        elif name in ("start cross", "start self"):
            name = name[6:]
            order = turned if TURNED[name == "self"] else straight
            lanes[name] = Lane(devices, (order,), after((fresh[name],), deps)[0], kept[name])
        elif name == "end ffn":
            own, got = lanes["ffn"].result()
            found["ffn"] = ffn_final(bits, own, got, w_expand, gain_ffn, deps=deps)
            token = found["ffn"][2]
        elif name == "end cross":
            own, got = lanes["cross"].result()
            found["cross"] = cross_final(bits, own, got, w_cross_query, gain_cross, deps=deps)
            token = found["cross"][4]
        elif name == "end self":
            own, got = lanes["self"].result()
            found["self"] = self_final(bits, own, got, w_qkv, gain_self, deps=deps)
            token = found["self"][1]
        else:
            lane = lanes[name[3:]]
            if lane.state != "done":
                lane.advance(deps)
                token = lane.token
    grad_contract, grad_expand, grad_gain_ffn = found["ffn"]
    grad_cross_out, grad_cross_query, grad_cross_kv, grad_self_out, grad_gain_cross = found["cross"]
    grad_qkv, grad_gain_self = found["self"]
    return (
        output.reshape(tokens.shape),
        grad_tokens.reshape(tokens.shape),
        grad_memory,
        grad_gain_self[0],
        grad_qkv,
        grad_self_out,
        grad_gain_cross[0],
        grad_cross_query,
        grad_cross_kv,
        grad_cross_out,
        grad_gain_ffn[0],
        grad_expand,
        grad_contract,
    )


def solution(mesh):
    rows, columns, copied = P("dp", None, None), P(None, "dp", None), P()
    return jax.shard_map(
        functools.partial(local, mesh.shape["dp"]),
        mesh=mesh,
        in_specs=(rows, columns, P("dp"), P("dp"), rows) + (copied,) * 10,
        out_specs=(rows, rows, columns) + (copied,) * 10,
        check_vma=False,
    )
```

```python
import functools
import jax
import jax.numpy as jnp
from jax import lax
from jax.experimental import pallas as pl
from jax.experimental.pallas import tpu as pltpu
from jax.sharding import PartitionSpec as P

HEAD = 64
PAIR = 128
epsilon = 1e-05
big_negative = -1e30
f32 = jnp.float32
bf16 = jnp.bfloat16
VMEM_LIMIT = 24
HBM = pltpu.HBM
VMEM = pltpu.VMEM


def dot(left, right, left_dim=1, right_dim=0):
    return lax.dot_general(
        left, right, (((left_dim,), (right_dim,)), ((), ())), preferred_element_type=f32
    )


def normalize(hidden):
    centred = hidden - jnp.mean(hidden, axis=-1, keepdims=True)
    spread = lax.rsqrt(jnp.mean(centred * centred, axis=-1, keepdims=True) + epsilon)
    return centred * spread, spread


def norm_backward(gradient, gain, normalized, spread):
    scaled = gradient * gain
    first = jnp.mean(scaled, axis=-1, keepdims=True)
    second = jnp.mean(scaled * normalized, axis=-1, keepdims=True)
    return spread * (scaled - first - normalized * second)


def head_masks(rows):
    lane = lax.broadcasted_iota(jnp.int32, (rows, PAIR), 1)
    first = jnp.where(lane < HEAD, 1.0, 0.0).astype(bf16)
    second = jnp.where(lane >= HEAD, 1.0, 0.0).astype(bf16)
    return first, second


def spread_pair(block, first, second):
    return jnp.concatenate([block * first, block * second], axis=0)


def stack_pair(block):
    half = block.shape[1] // 2
    return jnp.concatenate([block[:, :half], block[:, half:]], axis=0)


def wide_mask(mem_total, width):
    lane = lax.broadcasted_iota(jnp.int32, (mem_total, width), 1)
    parts = [
        jnp.where((lane >= h * HEAD) & (lane < (h + 1) * HEAD), 1.0, 0.0)
        for h in range(width // HEAD)
    ]
    return parts


PARTS = 1
CROSS_GROUP = 4
FF_CHUNK = 512
FF_ROWS = 512
TOKEN_ROWS = 512
FF_LIMIT = 36
LAG = 1


def stagger(parts):
    waiting = [LAG * n for n in range(len(parts))]
    while parts:
        left = []
        for n, part in enumerate(parts):
            if waiting[n]:
                waiting[n] -= 1
                left.append(n)
            elif next(part, part) is not part:
                left.append(n)
        parts, waiting = [parts[n] for n in left], [waiting[n] for n in left]


def self_forward_kernel(
    seqs, length, width,
    bits, lengths, tokens, gain_self, w_qkv, w_out, gain_cross, w_query,
    act, triple, weights, attended, mid, queries,
):
    step = pl.program_id(0)
    first, second = head_masks(length)
    key_at = lax.broadcasted_iota(jnp.int32, (length, 2 * length), 0)
    query_at = lax.broadcasted_iota(jnp.int32, (length, 2 * length), 1)
    query_at = jnp.where(query_at >= length, query_at - length, query_at)
    causal = key_at <= query_at
    count = seqs // PARTS

    def part(n):
        span = slice(n * count * length, (n + 1) * count * length)
        residual = tokens[span, :].astype(f32)
        normal, _ = normalize(residual)
        low = (normal * gain_self[...]).astype(bf16)
        yield
        both = dot(low, w_qkv[...]).astype(bf16)
        yield
        heads = [(s, p) for s in range(count) for p in range(width // PAIR)]
        scores = []
        for s, p in heads:
            rows = slice(s * length, (s + 1) * length)
            q = both[rows, p * PAIR : (p + 1) * PAIR] * 0.125
            k = both[rows, width + p * PAIR : width + (p + 1) * PAIR]
            scores.append(dot(k, spread_pair(q, first, second), 1, 1))
        yield
        softs = []
        for (s, p), score in zip(heads, scores):
            allowed = causal & (key_at < lengths[step * seqs + n * count + s])
            score = jnp.where(allowed, score, big_negative)
            raised = jnp.exp(score - jnp.max(score, axis=0, keepdims=True))
            softs.append((raised * (1.0 / jnp.sum(raised, axis=0, keepdims=True))).astype(bf16))
        yield
        joined = {}
        for (s, p), soft in zip(heads, softs):
            rows = slice(s * length, (s + 1) * length)
            v = both[rows, 2 * width + p * PAIR : 2 * width + (p + 1) * PAIR]
            joined[s, p] = dot(stack_pair(soft), spread_pair(v, first, second), 0, 0).astype(bf16)
        yield
        out = jnp.concatenate(
            [
                jnp.concatenate([joined[s, p] for p in range(width // PAIR)], axis=1)
                for s in range(count)
            ],
            axis=0,
        )
        residual = residual + dot(out, w_out[...])
        yield
        normal, _ = normalize(residual)
        after = (normal * gain_cross[...]).astype(bf16)
        yield
        found = dot(after, w_query[...]).astype(bf16)
        yield
        act[span, :] = low
        triple[span, :] = both
        attended[span, :] = out
        mid[span, :] = residual.astype(bf16)
        queries[span, :] = found
        for (s, p), soft in zip(heads, softs):
            weights[n * count + s, p] = soft

    stagger([part(n) for n in range(PARTS)])


def cross_forward_kernel(
    seqs, length, width, mem_total,
    bits, lengths, memory_lengths, raw, queries, mid, grad_output, w_kv, w_out, gain_ffn,
    arrived, pairs, weights, cross, late, grad_low, late_near, grad_low_near, act,
):
    step = pl.program_id(0)
    total = raw.shape[0] // mem_total
    at = lax.broadcasted_iota(jnp.int32, (mem_total, raw.shape[0]), 0) * total
    column = lax.broadcasted_iota(jnp.int32, (mem_total, raw.shape[0]), 1)
    own_rows = jnp.concatenate(
        [jnp.where(column == at + (step * seqs + s), 1.0, 0.0).astype(bf16) for s in range(seqs)],
        axis=0,
    )
    own_rows = dot(own_rows, raw[...]).astype(bf16)
    arrived[...] = own_rows
    both = dot(own_rows, w_kv[...]).astype(bf16)
    pairs[...] = both
    mask = jnp.concatenate(wide_mask(mem_total, width), axis=0).astype(bf16)
    heads = width // HEAD
    key_at = lax.broadcasted_iota(jnp.int32, (mem_total, length), 0)
    row_at = lax.broadcasted_iota(jnp.int32, (length, width), 0)

    def spread(s, at):
        return jnp.concatenate([both[s * mem_total : (s + 1) * mem_total, at]] * heads, axis=0) * mask

    scores = []
    for s in range(seqs):
        q = queries[s * length : (s + 1) * length, :] * 0.125
        scores.append(dot(spread(s, slice(0, width)), q, 1, 1).reshape(heads, mem_total, length))
    softs = []
    for s in range(seqs):
        allowed = (key_at < memory_lengths[step * seqs + s])[None]
        score = jnp.where(allowed, scores[s], big_negative)
        raised = jnp.exp(score - jnp.max(score, axis=1, keepdims=True))
        soft = raised * (1.0 / jnp.sum(raised, axis=1, keepdims=True))
        softs.append(soft.reshape(heads * mem_total, length).astype(bf16))
    joined = [dot(softs[s], spread(s, slice(width, 2 * width)), 0, 0).astype(bf16) for s in range(seqs)]
    low = jnp.concatenate(joined, axis=0)
    cross[...] = low
    for s in range(seqs):
        rows = slice(s * length, (s + 1) * length)
        weights[s] = softs[s]
        live = row_at < lengths[step * seqs + s]
        masked = jnp.where(live, grad_output[rows, :].astype(f32), 0.0).astype(bf16)
        grad_low[rows, :] = masked
        grad_low_near[rows, :] = masked
    residual = mid[...].astype(f32) + dot(low, w_out[...])
    late[...] = residual.astype(bf16)
    late_near[...] = residual.astype(bf16)
    normal, _ = normalize(residual)
    act[...] = (normal * gain_ffn[...]).astype(bf16)


def gelu_parts(value):
    half = 0.5 + 0.5 * lax.erf(value * 0.7071067811865476)
    bell = value * jnp.exp2(value * value * (-0.5 * 1.4426950408889634))
    return value * half, half + 0.3989422804014327 * bell


def place(bits, n, turned=None):
    first, second = bits[1], bits[2]
    if turned is not None:
        first, second = jnp.where(turned, second, first), jnp.where(turned, first, second)
    mine = first * 4 + second * 2 + bits[3]
    return jnp.bitwise_xor(mine, 7 - n)


def ffn_kernel(
    row_block,
    bits, act, grad_low, start, w_expand, w_contract,
    result, grad_normed, send, keep,
    activated, grad_expanded, total, change,
):
    step = pl.program_id(0)
    rows = act.shape[0]
    chunk = w_expand.shape[1]

    @pl.when(step == 0)
    def _():
        total[...] = start[...].astype(f32)
        change[...] = jnp.zeros_like(change)

    for b in range(rows // row_block):
        r = slice(b * row_block, (b + 1) * row_block)
        expanded = dot(act[r, :], w_expand[...])
        grad_activated = dot(grad_low[r, :], w_contract[...], 1, 1)
        value, slope = gelu_parts(expanded)
        value = value.astype(bf16)
        slope = (grad_activated * slope).astype(bf16)
        activated[r, :] = value
        grad_expanded[r, :] = slope
        total[r, :] += dot(value, w_contract[...])
        change[r, :] += dot(slope, w_expand[...], 1, 1)

    def fill(grads):
        unit = grad_low.shape[1]
        size = unit // 4
        contract = dot(activated[...], grad_low[...], 0, 0)
        expand = dot(act[...], grad_expanded[...], 0, 0)
        for k in range(chunk // unit):
            found = [contract[k * unit : (k + 1) * unit, :], expand[:, k * unit : (k + 1) * unit]]
            turned = lax.rem(step * (chunk // unit) + k, 2) == 1
            for n in range(8):
                at = k * 2 * unit + place(bits, n, turned) * size
                at = pl.ds(pl.multiple_of(at, size), size)
                grads[at, :] = found[n // 4][n % 4 * size : (n % 4 + 1) * size, :].astype(bf16)

    @pl.when(step < pl.num_programs(0) // 2)
    def _():
        fill(send)

    @pl.when(step >= pl.num_programs(0) // 2)
    def _():
        fill(keep)

    @pl.when(step == pl.num_programs(0) - 1)
    def _():
        result[...] = total[...].astype(bf16)
        grad_normed[...] = change[...].astype(bf16)


def give_rows(bits, start, low, high, send, keep, size, turned):
    first = bits[0] == 0
    for side, one, other in ((keep, low, high), (send, high, low)):
        rows = jnp.where(first, one, other)
        at, end = start, start + low.shape[0]
        while at < end:
            part = at // size
            stop = min(end, (part + 1) * size)
            to = place(bits, part, turned) * size + (at - part * size)
            to = pl.ds(pl.multiple_of(to, 32), stop - at)
            side[to, :] = rows[at - start : stop - start, :]
            at = stop


def cross_backward_kernel(
    length, mem_total,
    bits, grad_normed_far, late_far, grad_low_far, cross_far, weights_far, pairs_far, queries_far, mid_far,
    arrived_far, attended_far, w_out_far, w_query_far, w_kv_far, gain_ffn, gain_cross,
    gradient, grad_arrived, send, keep,
    grad_normed, late, grad_low, cross, weights, pairs, queries, mid,
    arrived, attended, w_out, w_query, w_kv,
    running, low_queries, out, low_pairs, arrival,
):
    rows, width = grad_normed.shape
    seqs = rows // length
    heads = width // HEAD
    blocks = [slice(n * rows // 4, (n + 1) * rows // 4) for n in range(4)]
    copies = []

    def fetch(far, near):
        copy = pltpu.make_async_copy(far, near, arrival.at[len(copies)])
        copies.append(copy)
        copy.start()
        return copy

    def fetch_rows(n):
        return [
            fetch(far.at[blocks[n], :], near.at[blocks[n], :])
            for far, near in ((grad_normed_far, grad_normed), (late_far, late), (grad_low_far, grad_low))
        ]

    waiting = [fetch_rows(0), fetch_rows(1)]
    copy_out = fetch(w_out_far, w_out)
    masks = wide_mask(mem_total, width)
    mask = jnp.concatenate(masks, axis=0).astype(bf16)
    grad_cross = []
    for n in range(4):
        for copy in waiting[n]:
            copy.wait()
        if n < 2:
            waiting.append(fetch_rows(n + 2))
        if n == 1:
            early = [fetch(weights_far, weights), fetch(pairs_far, pairs), fetch(queries_far, queries)]
        if n == 2:
            later = [fetch(w_query_far, w_query), fetch(mid_far, mid)]
        if n == 3:
            last = [
                fetch(cross_far, cross), fetch(arrived_far, arrived), fetch(w_kv_far, w_kv),
                fetch(attended_far, attended),
            ]
        normal, spread = normalize(late[blocks[n], :].astype(f32))
        change = norm_backward(grad_normed[blocks[n], :].astype(f32), gain_ffn[...], normal, spread)
        change = grad_low[blocks[n], :].astype(f32) + change
        running[blocks[n], :] = change
        low = change.astype(bf16)
        grad_normed[blocks[n], :] = low
        if n == 0:
            copy_out.wait()
        grad_cross.append(dot(low, w_out[...], 1, 1).astype(bf16))
    grad_cross = jnp.concatenate(grad_cross, axis=0)

    def widen(s, at):
        return jnp.concatenate([pairs[s * mem_total : (s + 1) * mem_total, at]] * heads, axis=0) * mask

    def narrow(block):
        return sum(block[h * mem_total : (h + 1) * mem_total, :] * masks[h] for h in range(heads))

    for copy in early:
        copy.wait()
    for start in range(0, seqs, CROSS_GROUP):
        group = range(start, start + CROSS_GROUP)
        softs = [weights[s] for s in group]
        grads = [grad_cross[s * length : (s + 1) * length, :] for s in group]
        changes = [
            dot(widen(s, slice(width, 2 * width)), grad, 1, 1).reshape(heads, mem_total, length)
            for s, grad in zip(group, grads)
        ]
        values = [dot(soft, grad) for soft, grad in zip(softs, grads)]
        scores = []
        for soft, change in zip(softs, changes):
            soft = soft.astype(f32).reshape(heads, mem_total, length)
            product = soft * change
            score = product - soft * jnp.sum(product, axis=1, keepdims=True)
            scores.append(score.reshape(heads * mem_total, length).astype(bf16))
        for s, score in zip(group, scores):
            low_queries[s * length : (s + 1) * length, :] = (
                dot(score, widen(s, slice(0, width)), 0, 0) * 0.125
            ).astype(bf16)
        keys = [
            dot(score, queries[s * length : (s + 1) * length, :]) for s, score in zip(group, scores)
        ]
        for s, key, value in zip(group, keys, values):
            at = slice(s * mem_total, (s + 1) * mem_total)
            low_pairs[at, :width] = (narrow(key) * 0.125).astype(bf16)
            low_pairs[at, width:] = narrow(value).astype(bf16)
    for copy in later + last:
        copy.wait()
    half = width // 2

    def give(n, left, right):
        found = dot(left[...], right, 0, 0).astype(bf16)
        size = send.shape[0] // 8
        give_rows(bits, n * half, found[:half], found[half:], send, keep, size, TURNED[0])

    give(0, cross, grad_normed[...])
    sent = []
    for n in range(4):
        back = dot(low_queries[blocks[n], :], w_query[...], 1, 1)
        normal, spread = normalize(mid[blocks[n], :].astype(f32))
        mid[blocks[n], :] = (normal * gain_cross[...]).astype(bf16)
        low = (running[blocks[n], :] + norm_backward(back, gain_cross[...], normal, spread)).astype(bf16)
        out[blocks[n], :] = low
        copy = pltpu.make_async_copy(
            out.at[blocks[n], :], gradient.at[blocks[n], :], arrival.at[len(copies) + n]
        )
        copy.start()
        sent.append(copy)
    give(1, mid, low_queries[...])
    give(2, arrived, low_pairs[:, :width])
    give(3, arrived, low_pairs[:, width:])
    give(4, attended, out[...])
    grad_rows = dot(low_pairs[...], w_kv[...], 1, 1).astype(bf16)
    count = seqs
    total = grad_rows.shape[0]
    block = min(total, 512)
    for start in range(0, total, block):
        row = lax.broadcasted_iota(jnp.int32, (block, total), 0) + start
        column = lax.broadcasted_iota(jnp.int32, (block, total), 1)
        shift = count.bit_length() - 1
        source = (row & (count - 1)) * mem_total + (row >> shift)
        order = jnp.where(column == source, 1.0, 0.0).astype(bf16)
        grad_arrived[start : start + block, :] = dot(order, grad_rows).astype(bf16)
    for copy in sent:
        copy.wait()


def self_backward_kernel(
    length,
    bits, gradient_far, triple_far, weights_far, act_far, w_out_far,
    grad_triple_far, send, keep,
    gradient, triple, weights, act, w_out, grad_triple, arrival,
):
    rows, width = gradient.shape
    seqs = rows // length // 4
    blocks = [slice(n * rows // 4, (n + 1) * rows // 4) for n in range(4)]
    copies = []

    def move(source, target):
        copy = pltpu.make_async_copy(source, target, arrival.at[len(copies)])
        copies.append(copy)
        copy.start()
        return copy

    def fetch(n):
        own = slice(n * seqs, (n + 1) * seqs)
        return [
            move(gradient_far.at[blocks[n], :], gradient.at[blocks[n], :]),
            move(triple_far.at[blocks[n], :], triple.at[blocks[n], :]),
            move(weights_far.at[own], weights.at[own]),
        ]

    ready = [move(w_out_far, w_out)]
    waiting = [fetch(0), fetch(1)]
    first, second = head_masks(length)
    sent = []
    for n in range(4):
        for copy in waiting[n] + ready:
            copy.wait()
        ready = []
        if n < 2:
            waiting.append(fetch(n + 2))
        if n == 2:
            late = move(act_far, act)
        low = dot(gradient[blocks[n], :], w_out[...], 1, 1).astype(bf16)
        group = []
        for s in range(n * seqs, (n + 1) * seqs):
            for p in range(width // PAIR):
                at = [slice(j * width + p * PAIR, j * width + (p + 1) * PAIR) for j in range(3)]
                group.append((s, p, slice(s * length, (s + 1) * length), at))
        grads = [
            spread_pair(low[(s - n * seqs) * length : (s + 1 - n * seqs) * length, at[0]], first, second)
            for s, p, span, at in group
        ]
        softs = [weights[s, p] for s, p, span, at in group]
        changes = [dot(triple[span, at[2]], grad, 1, 1) for (s, p, span, at), grad in zip(group, grads)]
        values = [dot(soft, grad).astype(bf16) for soft, grad in zip(softs, grads)]
        scores = []
        for soft, change in zip(softs, changes):
            soft = soft.astype(f32)
            product = soft * change
            scores.append((product - soft * jnp.sum(product, axis=0, keepdims=True)).astype(bf16))
        keys = [
            dot(score, spread_pair(triple[span, at[0]] * 0.125, first, second)).astype(bf16)
            for (s, p, span, at), score in zip(group, scores)
        ]
        queries = [
            (dot(stack_pair(score), spread_pair(triple[span, at[1]], first, second), 0, 0) * 0.125).astype(bf16)
            for (s, p, span, at), score in zip(group, scores)
        ]
        for k, (s, p, span, at) in enumerate(group):
            grad_triple[span, at[0]] = queries[k]
            grad_triple[span, at[1]] = keys[k]
            grad_triple[span, at[2]] = values[k]
        sent.append(move(grad_triple.at[blocks[n], :], grad_triple_far.at[blocks[n], :]))
    late.wait()
    half = width // 2
    for j in range(3):
        found = dot(act[...], grad_triple[:, j * width : (j + 1) * width], 0, 0).astype(bf16)
        give_rows(bits, j * half, found[:half], found[half:], send, keep, send.shape[0] // 8, TURNED[1])
    for copy in sent:
        copy.wait()


def grad_tokens_kernel(bits, gradient, grad_triple, tokens, w_qkv, gain_self, grad_tokens):
    normal, spread = normalize(tokens[...].astype(f32))
    change = norm_backward(dot(grad_triple[...], w_qkv[...], 1, 1), gain_self[...], normal, spread)
    grad_tokens[...] = (gradient[...].astype(f32) + change).astype(bf16)


def row_sums(weight, grad, gain):
    product = weight.astype(f32) * grad
    columns = sum(product[:, n : n + PAIR] for n in range(0, product.shape[1], PAIR))
    return jnp.sum(columns.T, axis=0, keepdims=True) / gain


def in_order(bits, mine, own, got, ordered, turned):
    size = ordered.shape[0] // 8

    def fill(source):
        for n in range(8):
            at = pl.ds(pl.multiple_of(place(bits, n, turned) * size, size), size)
            ordered[n * size : (n + 1) * size, :] = source[at, :]

    @pl.when(mine)
    def _():
        fill(own)

    @pl.when(jnp.logical_not(mine))
    def _():
        fill(got)


def ffn_final_kernel(bits, own, got, w_expand, gain, contract, expand, gain_grad, ordered):
    step = pl.program_id(0)
    chunk = expand.shape[1]
    half = pl.num_programs(0) // 2
    in_order(bits, (step >= half) == (bits[0] == 1), own, got, ordered, lax.rem(step, half) == 1)
    contract[...] = ordered[:chunk, :].astype(f32)
    grad = ordered[chunk:, :].astype(f32)
    expand[...] = grad
    sums = row_sums(w_expand[...], grad, gain[...])

    @pl.when(step == 0)
    def _():
        gain_grad[...] = sums

    @pl.when(step > 0)
    def _():
        gain_grad[...] += sums


def cross_final_kernel(bits, own, got, w_query, gain, cross_out, query, pair, self_out, gain_grad, ordered):
    half, width = query.shape
    in_order(bits, pl.program_id(0) == bits[0], own, got, ordered, TURNED[0])
    cross_out[...] = ordered[:half, :].astype(f32)
    grad = ordered[half : 2 * half, :].astype(f32)
    query[...] = grad
    pair[:, :width] = ordered[2 * half : 3 * half, :].astype(f32)
    pair[:, width:] = ordered[3 * half : 4 * half, :].astype(f32)
    self_out[...] = ordered[4 * half :, :].astype(f32)
    gain_grad[...] = row_sums(w_query[...], grad, gain[...])


def self_final_kernel(bits, own, got, w_qkv, gain, qkv, gain_grad, ordered):
    half = qkv.shape[0]
    width = own.shape[1]
    in_order(bits, pl.program_id(0) == bits[0], own, got, ordered, TURNED[1])
    for j in range(3):
        qkv[:, j * width : (j + 1) * width] = ordered[j * half : (j + 1) * half, :].astype(f32)
    gain_grad[...] = row_sums(w_qkv[...], qkv[...], gain[...])


def call(kernel, grid, bits, ins, outs, scratch=(), flops=0, deps=(), limit=VMEM_LIMIT):
    moved = sum(a.size * a.dtype.itemsize for a, *_ in ins)
    shapes = []
    for shape, dtype, _, *space in outs:
        size = 1
        for n in shape:
            size *= n
        moved += size * jnp.dtype(dtype).itemsize
        shapes.append(space[0](shape, dtype) if space else jax.ShapeDtypeStruct(shape, dtype))
    count = len(ins)
    arrays = [
        pltpu.with_memory_space_constraint(a, space[0]) if space else a for a, _, *space in ins
    ]

    def body(bits_ref, *refs):
        kernel(bits_ref, *refs[:count], *refs[count + len(deps) :])

    return pl.pallas_call(
        body,
        grid_spec=pltpu.PrefetchScalarGridSpec(
            num_scalar_prefetch=1,
            grid=grid,
            in_specs=[spec for _, spec, *_ in ins] + [pl.BlockSpec(memory_space=pl.ANY)] * len(deps),
            out_specs=[spec for _, _, spec, *_ in outs],
            scratch_shapes=list(scratch),
        ),
        out_shape=shapes,
        compiler_params=pltpu.CompilerParams(vmem_limit_bytes=limit * 1024 * 1024),
        cost_estimate=pl.CostEstimate(flops=flops, bytes_accessed=moved, transcendentals=0),
    )(bits, *arrays, *deps)


def by_step(*shape):
    return pl.BlockSpec(shape, lambda i, bits: (i,) + (0,) * (len(shape) - 1))


def whole(*shape):
    return pl.BlockSpec(shape, lambda i, bits: (0,) * len(shape))


def scalars():
    return pl.BlockSpec(memory_space=pltpu.SMEM)


SEQS = 4
GROUP = 16
TURNED = (True, None)
PLAN = (
    "do ffn",
    "cross",
    "do ffn",
    "start cross",
    "do cross",
    "do ffn",
    "memory",
    "self",
    "start self",
    "do ffn",
    "do cross",
    "do self",
    "do cross",
    "do ffn",
    "do cross",
    "do self",
    "do ffn",
    "do self",
    "do cross",
    "do ffn",
    "do self",
    "do cross",
    "do self",
    "do self",
    "do ffn",
    "do cross",
    "do self",
    "tokens",
    "do self",
    "do cross",
    "end ffn",
    "end self",
    "end cross",
)


def self_forward(bits, tokens, lengths, gain_self, w_qkv, w_out, gain_cross, w_query, length):
    rows, width = tokens.shape
    n = rows // length
    block = SEQS * length
    row = by_step(block, width)
    return call(
        functools.partial(self_forward_kernel, SEQS, length, width),
        (n // SEQS,), bits,
        [
            (lengths, scalars()), (tokens, row, HBM),
            (gain_self, whole(1, width)), (w_qkv, whole(width, 3 * width), HBM),
            (w_out, whole(width, width), HBM), (gain_cross, whole(1, width)),
            (w_query, whole(width, width), HBM),
        ],
        [
            ((rows, width), bf16, row, HBM),
            ((rows, 3 * width), bf16, by_step(block, 3 * width), HBM),
            ((n, width // PAIR, length, 2 * length), bf16, by_step(SEQS, width // PAIR, length, 2 * length), HBM),
            ((rows, width), bf16, row, HBM),
            ((rows, width), bf16, row, HBM),
            ((rows, width), bf16, row, HBM),
        ],
        flops=12 * rows * width * width,
        limit=36,
    )


def cross_forward(bits, lengths, memory_lengths, raw, queries, mid, grad_output, w_kv, w_out, gain_ffn, length, mem_total):
    rows, width = queries.shape
    n = rows // length
    block = SEQS * length
    mem = SEQS * mem_total
    heads = width // HEAD
    row = by_step(block, width)
    return call(
        functools.partial(cross_forward_kernel, SEQS, length, width, mem_total),
        (n // SEQS,), bits,
        [
            (lengths, scalars()), (memory_lengths, scalars()),
            (raw, whole(*raw.shape)), (queries, row, HBM),
            (mid, row, HBM), (grad_output, row, HBM),
            (w_kv, whole(width, 2 * width)), (w_out, whole(width, width)),
            (gain_ffn, whole(1, width)),
        ],
        [
            ((n * mem_total, width), bf16, by_step(mem, width), HBM),
            ((n * mem_total, 2 * width), bf16, by_step(mem, 2 * width), HBM),
            ((n, heads * mem_total, length), bf16, by_step(SEQS, heads * mem_total, length), HBM),
            ((rows, width), bf16, row, HBM),
            ((rows, width), bf16, row, HBM),
            ((rows, width), bf16, row, HBM),
            ((rows, width), bf16, row, VMEM),
            ((rows, width), bf16, row, VMEM),
            ((rows, width), bf16, row, VMEM),
        ],
        flops=6 * rows * width * width,
        limit=VMEM_LIMIT if mem_total <= 32 else 2 * VMEM_LIMIT,
    )


def feed_forward(bits, act, grad_low, start, w_expand, w_contract, chunk=FF_CHUNK):
    rows, width = act.shape
    hidden = w_expand.shape[1]
    steps = hidden // chunk
    half = steps // 2

    def at(i, bits):
        return lax.rem(i + half * (1 - bits[0]), steps)

    def block(place):
        return pl.BlockSpec((2 * chunk, width), lambda i, bits: (place(i), 0))

    return call(
        functools.partial(ffn_kernel, min(rows, FF_ROWS)),
        (steps,), bits,
        [
            (act, whole(rows, width)), (grad_low, whole(rows, width)), (start, whole(rows, width)),
            (w_expand, pl.BlockSpec((width, chunk), lambda i, bits: (0, at(i, bits)))),
            (w_contract, pl.BlockSpec((chunk, width), lambda i, bits: (at(i, bits), 0))),
        ],
        [
            ((rows, width), bf16, whole(rows, width), HBM),
            ((rows, width), bf16, whole(rows, width), HBM),
            ((hidden, width), bf16, block(lambda i: jnp.minimum(i, half - 1)), HBM),
            ((hidden, width), bf16, block(lambda i: jnp.maximum(i - half, 0)), HBM),
        ],
        [
            pltpu.VMEM((rows, chunk), bf16),
            pltpu.VMEM((rows, chunk), bf16),
            pltpu.VMEM((rows, width), f32),
            pltpu.VMEM((rows, width), f32),
        ],
        flops=12 * rows * width * hidden,
        limit=FF_LIMIT,
    )


def cross_backward(bits, grad_normed, late, grad_low, cross, weights, pairs, queries, mid, arrived, attended, w_out, w_query, w_kv, gain_ffn, gain_cross, length, mem_total, deps=()):
    rows, width = queries.shape
    far = [
        grad_normed, late, grad_low, cross, weights, pairs, queries, mid, arrived, attended,
        w_out, w_query, w_kv,
    ]
    anywhere = pl.BlockSpec(memory_space=pl.ANY)
    return call(
        functools.partial(cross_backward_kernel, length, mem_total),
        (1,), bits,
        [(a, anywhere, HBM) for a in far]
        + [(gain_ffn, whole(1, width)), (gain_cross, whole(1, width))],
        [
            ((rows, width), bf16, anywhere, HBM),
            (arrived.shape, bf16, whole(*arrived.shape), HBM),
            ((5 * width // 2, width), bf16, whole(5 * width // 2, width), HBM),
            ((5 * width // 2, width), bf16, whole(5 * width // 2, width), HBM),
        ],
        [pltpu.VMEM(a.shape, bf16) for a in far]
        + [
            pltpu.VMEM((rows, width), f32),
            pltpu.VMEM((rows, width), bf16),
            pltpu.VMEM((rows, width), bf16),
            pltpu.VMEM(pairs.shape, bf16),
            pltpu.SemaphoreType.DMA((32,)),
        ],
        flops=14 * rows * width * width,
        deps=deps,
        limit=48 if mem_total <= 32 else 62,
    )


def self_backward(bits, gradient, triple, weights, act, w_out, length, deps=()):
    rows, width = gradient.shape
    far = [gradient, triple, weights, act, w_out]
    anywhere = pl.BlockSpec(memory_space=pl.ANY)
    return call(
        functools.partial(self_backward_kernel, length),
        (1,), bits,
        [(a, anywhere, HBM) for a in far],
        [
            (triple.shape, bf16, anywhere, HBM),
            ((3 * width // 2, width), bf16, whole(3 * width // 2, width), HBM),
            ((3 * width // 2, width), bf16, whole(3 * width // 2, width), HBM),
        ],
        [pltpu.VMEM(a.shape, bf16) for a in far]
        + [pltpu.VMEM(triple.shape, bf16), pltpu.SemaphoreType.DMA((24,))],
        flops=14 * rows * width * width,
        deps=deps,
        limit=44,
    )


def token_gradient(bits, gradient, grad_triple, tokens, w_qkv, gain_self, deps=()):
    rows, width = tokens.shape
    block = TOKEN_ROWS
    row = by_step(block, width)
    return call(
        grad_tokens_kernel, (rows // block,), bits,
        [
            (gradient, row, HBM), (grad_triple, by_step(block, 3 * width), HBM), (tokens, row, HBM),
            (w_qkv, whole(width, 3 * width), HBM), (gain_self, whole(1, width)),
        ],
        [((rows, width), bf16, row)],
        flops=6 * rows * width * width,
        deps=deps,
    )[0]


def after(arrays, deps):
    if not deps:
        return arrays
    return lax.optimization_barrier((*arrays, *deps))[: len(arrays)]


def added(left, right):
    return (left.astype(f32) + right.astype(f32)).astype(bf16)


def exchange(block, bit, devices):
    return lax.ppermute(block, "dp", [(i, i ^ (1 << bit)) for i in range(devices)])


class Lane:
    def __init__(self, devices, orders, send, keep):
        self.devices, self.orders, self.count = devices, orders, len(orders)
        self.rest = list(range(4, devices.bit_length() - 1))
        self.level, self.state = 0, "halve"
        self.own = self.parted(keep)
        self.got = self.parted(exchange(send, 0, devices))
        self.token = send

    def parted(self, block):
        size = block.shape[0] // self.count
        return [block[n * size : (n + 1) * size] for n in range(self.count)]

    def send(self, blocks):
        self.token = blocks[0]
        if self.level in (1, 2):
            bits = [order[self.level - 1] for order in self.orders]
            self.got = [exchange(b, bit, self.devices) for b, bit in zip(blocks, bits)]
        else:
            bit = {0: 0, 3: 3}.get(self.level, self.level)
            whole_block = jnp.concatenate(blocks) if len(blocks) > 1 else blocks[0]
            self.token = whole_block
            self.got = self.parted(exchange(whole_block, bit, self.devices))

    def advance(self, deps=()):
        both = after((*self.own, *self.got), deps)
        own, got = both[: self.count], both[self.count :]
        if self.state == "halve":
            half = own[0].shape[0] // 2
            self.own = [added(a[half:], b[half:]) for a, b in zip(own, got)]
            self.level += 1
            self.send([added(a[:half], b[:half]) for a, b in zip(own, got)])
            if self.level == 3:
                self.state = "whole"
        elif self.state == "whole":
            self.own = [added(a, b) for a, b in zip(own, got)]
            if self.rest:
                self.level = self.rest.pop(0)
            else:
                self.level, self.state = 3, "join"
            self.send(self.own)
        else:
            self.own = [jnp.concatenate([b, a]) for a, b in zip(own, got)]
            self.level -= 1
            self.send(self.own)
            if self.level == 0:
                self.state = "done"

    def result(self):
        return [blocks[0] if self.count == 1 else jnp.concatenate(blocks) for blocks in (self.own, self.got)]


def ffn_final(bits, own, got, w_expand, gain, deps=(), chunk=512):
    width, hidden = w_expand.shape
    steps = hidden // chunk

    def source(mine):
        def at(i, bits):
            first = (bits[0] == 0) == mine
            return (jnp.where(first, jnp.minimum(i, steps // 2 - 1), jnp.maximum(i - steps // 2, 0)), 0)

        return pl.BlockSpec((2 * chunk, width), at)

    return call(
        ffn_final_kernel, (steps,), bits,
        [
            (own, source(True)), (got, source(False)),
            (w_expand, pl.BlockSpec((width, chunk), lambda i, bits: (0, i))),
            (gain, whole(1, width)),
        ],
        [
            ((hidden, width), f32, by_step(chunk, width)),
            ((width, hidden), f32, pl.BlockSpec((width, chunk), lambda i, bits: (0, i))),
            ((1, width), f32, whole(1, width)),
        ],
        [pltpu.VMEM((2 * chunk, width), bf16)],
        deps=deps,
    )


def cross_final(bits, own, got, w_query, gain, deps=()):
    width = w_query.shape[0]
    half = width // 2
    part = by_step(half, width)
    column = pl.BlockSpec((1, half), lambda i, bits: (0, i))
    return call(
        cross_final_kernel, (2,), bits,
        [
            (own, whole(*own.shape)), (got, whole(*own.shape)), (w_query, part), (gain, column),
        ],
        [
            ((width, width), f32, part), ((width, width), f32, part),
            ((width, 2 * width), f32, by_step(half, 2 * width)), ((width, width), f32, part),
            ((1, width), f32, column),
        ],
        [pltpu.VMEM(own.shape, bf16)],
        deps=deps,
    )


def self_final(bits, own, got, w_qkv, gain, deps=()):
    width = w_qkv.shape[0]
    half = width // 2
    column = pl.BlockSpec((1, half), lambda i, bits: (0, i))
    return call(
        self_final_kernel, (2,), bits,
        [
            (own, whole(*own.shape)), (got, whole(*own.shape)),
            (w_qkv, by_step(half, 3 * width)), (gain, column),
        ],
        [((width, 3 * width), f32, by_step(half, 3 * width)), ((1, width), f32, column)],
        [pltpu.VMEM(own.shape, bf16)],
        deps=deps,
    )


def local(
    devices, tokens, memory, target_lengths, memory_lengths, grad_output,
    gain_self, w_qkv, w_self_out, gain_cross, w_cross_query, w_cross_kv, w_cross_out,
    gain_ffn, w_expand, w_contract,
):
    seq_count, length, width = tokens.shape
    rows = seq_count * length
    gain_self, gain_cross, gain_ffn = gain_self[None], gain_cross[None], gain_ffn[None]
    flat_tokens = tokens.reshape(rows, width)
    me = lax.axis_index("dp")
    bits = jnp.stack([(me >> b) & 1 for b in range(devices.bit_length() - 1)]).astype(jnp.int32)
    raw = lax.all_to_all(
        memory.reshape(devices, -1, width), "dp", split_axis=0, concat_axis=0, tiled=True
    ).reshape(-1, width)
    mem_total = raw.shape[0] // seq_count
    act_one, triple, self_weights, attended, mid, queries = self_forward(
        bits, flat_tokens, target_lengths, gain_self, w_qkv, w_self_out, gain_cross, w_cross_query, length
    )
    arrived, pairs, cross_weights, cross, late, grad_low, late_near, grad_low_near, act = cross_forward(
        bits, target_lengths, memory_lengths, raw, queries, mid, grad_output.reshape(rows, width),
        w_cross_kv, w_cross_out, gain_ffn, length, mem_total,
    )
    output, grad_normed, send, keep = feed_forward(
        bits, act, grad_low_near, late_near, w_expand, w_contract
    )
    straight, turned = (1, 2), (2, 1)
    lanes = {"ffn": Lane(devices, (straight, turned), send, keep)}
    token, fresh, kept, found = send, {}, {}, {}
    for n, name in enumerate(PLAN):
        deps = [token]
        if PLAN[n - 1] == "self":
            deps.append(grad_memory)
        if name.startswith("end"):
            lane = lanes[name[4:]]
            while lane.state != "done":
                lane.advance(deps)
                deps = [lane.token]
        if name == "cross":
            gradient, grad_arrived, send, keep = cross_backward(
                bits, grad_normed, late, grad_low, cross, cross_weights, pairs, queries, mid, arrived,
                attended, w_cross_out, w_cross_query, w_cross_kv, gain_ffn, gain_cross, length, mem_total,
                deps=deps,
            )
            token = fresh["cross"] = send
            kept["cross"] = keep
        elif name == "self":
            grad_triple, send, keep = self_backward(
                bits, gradient, triple, self_weights, act_one, w_self_out, length, deps=deps
            )
            token = fresh["self"] = send
            kept["self"] = keep
        elif name == "tokens":
            token = grad_tokens = token_gradient(
                bits, gradient, grad_triple, flat_tokens, w_qkv, gain_self, deps=deps
            )
        elif name == "memory":
            grad_memory = lax.all_to_all(
                after((grad_arrived,), deps)[0].reshape(devices, -1, width),
                "dp", split_axis=0, concat_axis=0, tiled=True,
            ).reshape(memory.shape)
        elif name in ("start cross", "start self"):
            name = name[6:]
            order = turned if TURNED[name == "self"] else straight
            lanes[name] = Lane(devices, (order,), after((fresh[name],), deps)[0], kept[name])
        elif name == "end ffn":
            own, got = lanes["ffn"].result()
            found["ffn"] = ffn_final(bits, own, got, w_expand, gain_ffn, deps=deps)
            token = found["ffn"][2]
        elif name == "end cross":
            own, got = lanes["cross"].result()
            found["cross"] = cross_final(bits, own, got, w_cross_query, gain_cross, deps=deps)
            token = found["cross"][4]
        elif name == "end self":
            own, got = lanes["self"].result()
            found["self"] = self_final(bits, own, got, w_qkv, gain_self, deps=deps)
            token = found["self"][1]
        else:
            lane = lanes[name[3:]]
            if lane.state != "done":
                lane.advance(deps)
                token = lane.token
    grad_contract, grad_expand, grad_gain_ffn = found["ffn"]
    grad_cross_out, grad_cross_query, grad_cross_kv, grad_self_out, grad_gain_cross = found["cross"]
    grad_qkv, grad_gain_self = found["self"]
    return (
        output.reshape(tokens.shape),
        grad_tokens.reshape(tokens.shape),
        grad_memory,
        grad_gain_self[0],
        grad_qkv,
        grad_self_out,
        grad_gain_cross[0],
        grad_cross_query,
        grad_cross_kv,
        grad_cross_out,
        grad_gain_ffn[0],
        grad_expand,
        grad_contract,
    )


def solution(mesh):
    rows, columns, copied = P("dp", None, None), P(None, "dp", None), P()
    return jax.shard_map(
        functools.partial(local, mesh.shape["dp"]),
        mesh=mesh,
        in_specs=(rows, columns, P("dp"), P("dp"), rows) + (copied,) * 10,
        out_specs=(rows, rows, columns) + (copied,) * 10,
        check_vma=False,
    )
```

```python
import functools
import jax
import jax.numpy as jnp
from jax import lax
from jax.experimental import pallas as pl
from jax.experimental.pallas import tpu as pltpu
from jax.sharding import PartitionSpec as P

HEAD = 64
PAIR = 128
epsilon = 1e-05
big_negative = -1e30
f32 = jnp.float32
bf16 = jnp.bfloat16
VMEM_LIMIT = 24
HBM = pltpu.HBM
VMEM = pltpu.VMEM


def dot(left, right, left_dim=1, right_dim=0):
    return lax.dot_general(
        left, right, (((left_dim,), (right_dim,)), ((), ())), preferred_element_type=f32
    )


def normalize(hidden):
    centred = hidden - jnp.mean(hidden, axis=-1, keepdims=True)
    spread = lax.rsqrt(jnp.mean(centred * centred, axis=-1, keepdims=True) + epsilon)
    return centred * spread, spread


def norm_backward(gradient, gain, normalized, spread):
    scaled = gradient * gain
    first = jnp.mean(scaled, axis=-1, keepdims=True)
    second = jnp.mean(scaled * normalized, axis=-1, keepdims=True)
    return spread * (scaled - first - normalized * second)


def head_masks(rows):
    lane = lax.broadcasted_iota(jnp.int32, (rows, PAIR), 1)
    first = jnp.where(lane < HEAD, 1.0, 0.0).astype(bf16)
    second = jnp.where(lane >= HEAD, 1.0, 0.0).astype(bf16)
    return first, second


def spread_pair(block, first, second):
    return jnp.concatenate([block * first, block * second], axis=0)


def stack_pair(block):
    half = block.shape[1] // 2
    return jnp.concatenate([block[:, :half], block[:, half:]], axis=0)


def wide_mask(mem_total, width):
    lane = lax.broadcasted_iota(jnp.int32, (mem_total, width), 1)
    parts = [
        jnp.where((lane >= h * HEAD) & (lane < (h + 1) * HEAD), 1.0, 0.0)
        for h in range(width // HEAD)
    ]
    return parts


PARTS = 1
CROSS_GROUP = 4
FF_CHUNK = 512
FF_ROWS = 512
TOKEN_ROWS = 512
FF_LIMIT = 36
LAG = 1


def stagger(parts):
    waiting = [LAG * n for n in range(len(parts))]
    while parts:
        left = []
        for n, part in enumerate(parts):
            if waiting[n]:
                waiting[n] -= 1
                left.append(n)
            elif next(part, part) is not part:
                left.append(n)
        parts, waiting = [parts[n] for n in left], [waiting[n] for n in left]


def self_forward_kernel(
    seqs, length, width,
    bits, lengths, tokens, gain_self, w_qkv, w_out, gain_cross, w_query,
    act, triple, weights, attended, mid, queries,
):
    step = pl.program_id(0)
    first, second = head_masks(length)
    key_at = lax.broadcasted_iota(jnp.int32, (length, 2 * length), 0)
    query_at = lax.broadcasted_iota(jnp.int32, (length, 2 * length), 1)
    query_at = jnp.where(query_at >= length, query_at - length, query_at)
    causal = key_at <= query_at
    count = seqs // PARTS

    def part(n):
        span = slice(n * count * length, (n + 1) * count * length)
        residual = tokens[span, :].astype(f32)
        normal, _ = normalize(residual)
        low = (normal * gain_self[...]).astype(bf16)
        yield
        both = dot(low, w_qkv[...]).astype(bf16)
        yield
        heads = [(s, p) for s in range(count) for p in range(width // PAIR)]
        scores = []
        for s, p in heads:
            rows = slice(s * length, (s + 1) * length)
            q = both[rows, p * PAIR : (p + 1) * PAIR] * 0.125
            k = both[rows, width + p * PAIR : width + (p + 1) * PAIR]
            scores.append(dot(k, spread_pair(q, first, second), 1, 1))
        yield
        softs = []
        for (s, p), score in zip(heads, scores):
            allowed = causal & (key_at < lengths[step * seqs + n * count + s])
            score = jnp.where(allowed, score, big_negative)
            raised = jnp.exp(score - jnp.max(score, axis=0, keepdims=True))
            softs.append((raised * (1.0 / jnp.sum(raised, axis=0, keepdims=True))).astype(bf16))
        yield
        joined = {}
        for (s, p), soft in zip(heads, softs):
            rows = slice(s * length, (s + 1) * length)
            v = both[rows, 2 * width + p * PAIR : 2 * width + (p + 1) * PAIR]
            joined[s, p] = dot(stack_pair(soft), spread_pair(v, first, second), 0, 0).astype(bf16)
        yield
        out = jnp.concatenate(
            [
                jnp.concatenate([joined[s, p] for p in range(width // PAIR)], axis=1)
                for s in range(count)
            ],
            axis=0,
        )
        residual = residual + dot(out, w_out[...])
        yield
        normal, _ = normalize(residual)
        after = (normal * gain_cross[...]).astype(bf16)
        yield
        found = dot(after, w_query[...]).astype(bf16)
        yield
        act[span, :] = low
        triple[span, :] = both
        attended[span, :] = out
        mid[span, :] = residual.astype(bf16)
        queries[span, :] = found
        for (s, p), soft in zip(heads, softs):
            weights[n * count + s, p] = soft

    stagger([part(n) for n in range(PARTS)])


def cross_forward_kernel(
    seqs, length, width, mem_total,
    bits, lengths, memory_lengths, raw, queries, mid, grad_output, w_kv, w_out, gain_ffn,
    arrived, pairs, weights, cross, late, grad_low, late_near, grad_low_near, act,
):
    step = pl.program_id(0)
    total = raw.shape[0] // mem_total
    at = lax.broadcasted_iota(jnp.int32, (mem_total, raw.shape[0]), 0) * total
    column = lax.broadcasted_iota(jnp.int32, (mem_total, raw.shape[0]), 1)
    own_rows = jnp.concatenate(
        [jnp.where(column == at + (step * seqs + s), 1.0, 0.0).astype(bf16) for s in range(seqs)],
        axis=0,
    )
    own_rows = dot(own_rows, raw[...]).astype(bf16)
    arrived[...] = own_rows
    both = dot(own_rows, w_kv[...]).astype(bf16)
    pairs[...] = both
    mask = jnp.concatenate(wide_mask(mem_total, width), axis=0).astype(bf16)
    heads = width // HEAD
    key_at = lax.broadcasted_iota(jnp.int32, (mem_total, length), 0)
    row_at = lax.broadcasted_iota(jnp.int32, (length, width), 0)

    def spread(s, at):
        return jnp.concatenate([both[s * mem_total : (s + 1) * mem_total, at]] * heads, axis=0) * mask

    scores = []
    for s in range(seqs):
        q = queries[s * length : (s + 1) * length, :] * 0.125
        scores.append(dot(spread(s, slice(0, width)), q, 1, 1).reshape(heads, mem_total, length))
    softs = []
    for s in range(seqs):
        allowed = (key_at < memory_lengths[step * seqs + s])[None]
        score = jnp.where(allowed, scores[s], big_negative)
        raised = jnp.exp(score - jnp.max(score, axis=1, keepdims=True))
        soft = raised * (1.0 / jnp.sum(raised, axis=1, keepdims=True))
        softs.append(soft.reshape(heads * mem_total, length).astype(bf16))
    joined = [dot(softs[s], spread(s, slice(width, 2 * width)), 0, 0).astype(bf16) for s in range(seqs)]
    low = jnp.concatenate(joined, axis=0)
    cross[...] = low
    for s in range(seqs):
        rows = slice(s * length, (s + 1) * length)
        weights[s] = softs[s]
        live = row_at < lengths[step * seqs + s]
        masked = jnp.where(live, grad_output[rows, :].astype(f32), 0.0).astype(bf16)
        grad_low[rows, :] = masked
        grad_low_near[rows, :] = masked
    residual = mid[...].astype(f32) + dot(low, w_out[...])
    late[...] = residual.astype(bf16)
    late_near[...] = residual.astype(bf16)
    normal, _ = normalize(residual)
    act[...] = (normal * gain_ffn[...]).astype(bf16)


def gelu_parts(value):
    half = 0.5 + 0.5 * lax.erf(value * 0.7071067811865476)
    bell = value * jnp.exp2(value * value * (-0.5 * 1.4426950408889634))
    return value * half, half + 0.3989422804014327 * bell


def place(bits, n, turned=None):
    first, second = bits[1], bits[2]
    if turned is not None:
        first, second = jnp.where(turned, second, first), jnp.where(turned, first, second)
    mine = first * 4 + second * 2 + bits[3]
    return jnp.bitwise_xor(mine, 7 - n)


def ffn_kernel(
    row_block,
    bits, act, grad_low, start, w_expand, w_contract,
    result, grad_normed, send, keep,
    activated, grad_expanded, total, change,
):
    step = pl.program_id(0)
    rows = act.shape[0]
    chunk = w_expand.shape[1]

    @pl.when(step == 0)
    def _():
        total[...] = start[...].astype(f32)
        change[...] = jnp.zeros_like(change)

    for b in range(rows // row_block):
        r = slice(b * row_block, (b + 1) * row_block)
        expanded = dot(act[r, :], w_expand[...])
        grad_activated = dot(grad_low[r, :], w_contract[...], 1, 1)
        value, slope = gelu_parts(expanded)
        value = value.astype(bf16)
        slope = (grad_activated * slope).astype(bf16)
        activated[r, :] = value
        grad_expanded[r, :] = slope
        total[r, :] += dot(value, w_contract[...])
        change[r, :] += dot(slope, w_expand[...], 1, 1)

    def fill(grads):
        unit = grad_low.shape[1]
        size = unit // 4
        contract = dot(activated[...], grad_low[...], 0, 0)
        expand = dot(act[...], grad_expanded[...], 0, 0)
        for k in range(chunk // unit):
            found = [contract[k * unit : (k + 1) * unit, :], expand[:, k * unit : (k + 1) * unit]]
            turned = lax.rem(step * (chunk // unit) + k, 2) == 1
            for n in range(8):
                at = k * 2 * unit + place(bits, n, turned) * size
                at = pl.ds(pl.multiple_of(at, size), size)
                grads[at, :] = found[n // 4][n % 4 * size : (n % 4 + 1) * size, :].astype(bf16)

    @pl.when(step < pl.num_programs(0) // 2)
    def _():
        fill(send)

    @pl.when(step >= pl.num_programs(0) // 2)
    def _():
        fill(keep)

    @pl.when(step == pl.num_programs(0) - 1)
    def _():
        result[...] = total[...].astype(bf16)
        grad_normed[...] = change[...].astype(bf16)


def give_rows(bits, start, low, high, send, keep, size, turned):
    first = bits[0] == 0
    for side, one, other in ((keep, low, high), (send, high, low)):
        rows = jnp.where(first, one, other)
        at, end = start, start + low.shape[0]
        while at < end:
            part = at // size
            stop = min(end, (part + 1) * size)
            to = place(bits, part, turned) * size + (at - part * size)
            to = pl.ds(pl.multiple_of(to, 32), stop - at)
            side[to, :] = rows[at - start : stop - start, :]
            at = stop


def cross_backward_kernel(
    length, mem_total,
    bits, grad_normed_far, late_far, grad_low_far, cross_far, weights_far, pairs_far, queries_far, mid_far,
    arrived_far, attended_far, w_out_far, w_query_far, w_kv_far, gain_ffn, gain_cross,
    gradient, grad_arrived, send, keep,
    grad_normed, late, grad_low, cross, weights, pairs, queries, mid,
    arrived, attended, w_out, w_query, w_kv,
    running, low_queries, out, low_pairs, arrival,
):
    rows, width = grad_normed.shape
    seqs = rows // length
    heads = width // HEAD
    blocks = [slice(n * rows // 4, (n + 1) * rows // 4) for n in range(4)]
    copies = []

    def fetch(far, near):
        copy = pltpu.make_async_copy(far, near, arrival.at[len(copies)])
        copies.append(copy)
        copy.start()
        return copy

    def fetch_rows(n):
        return [
            fetch(far.at[blocks[n], :], near.at[blocks[n], :])
            for far, near in ((grad_normed_far, grad_normed), (late_far, late), (grad_low_far, grad_low))
        ]

    waiting = [fetch_rows(0), fetch_rows(1)]
    copy_out = fetch(w_out_far, w_out)
    masks = wide_mask(mem_total, width)
    mask = jnp.concatenate(masks, axis=0).astype(bf16)
    grad_cross = []
    for n in range(4):
        for copy in waiting[n]:
            copy.wait()
        if n < 2:
            waiting.append(fetch_rows(n + 2))
        if n == 1:
            early = [fetch(weights_far, weights), fetch(pairs_far, pairs), fetch(queries_far, queries)]
        if n == 2:
            later = [fetch(w_query_far, w_query), fetch(mid_far, mid)]
        if n == 3:
            last = [
                fetch(cross_far, cross), fetch(arrived_far, arrived), fetch(w_kv_far, w_kv),
                fetch(attended_far, attended),
            ]
        normal, spread = normalize(late[blocks[n], :].astype(f32))
        change = norm_backward(grad_normed[blocks[n], :].astype(f32), gain_ffn[...], normal, spread)
        change = grad_low[blocks[n], :].astype(f32) + change
        running[blocks[n], :] = change
        low = change.astype(bf16)
        grad_normed[blocks[n], :] = low
        if n == 0:
            copy_out.wait()
        grad_cross.append(dot(low, w_out[...], 1, 1).astype(bf16))
    grad_cross = jnp.concatenate(grad_cross, axis=0)

    def widen(s, at):
        return jnp.concatenate([pairs[s * mem_total : (s + 1) * mem_total, at]] * heads, axis=0) * mask

    def narrow(block):
        return sum(block[h * mem_total : (h + 1) * mem_total, :] * masks[h] for h in range(heads))

    for copy in early:
        copy.wait()
    for start in range(0, seqs, CROSS_GROUP):
        group = range(start, start + CROSS_GROUP)
        softs = [weights[s] for s in group]
        grads = [grad_cross[s * length : (s + 1) * length, :] for s in group]
        changes = [
            dot(widen(s, slice(width, 2 * width)), grad, 1, 1).reshape(heads, mem_total, length)
            for s, grad in zip(group, grads)
        ]
        values = [dot(soft, grad) for soft, grad in zip(softs, grads)]
        scores = []
        for soft, change in zip(softs, changes):
            soft = soft.astype(f32).reshape(heads, mem_total, length)
            product = soft * change
            score = product - soft * jnp.sum(product, axis=1, keepdims=True)
            scores.append(score.reshape(heads * mem_total, length).astype(bf16))
        for s, score in zip(group, scores):
            low_queries[s * length : (s + 1) * length, :] = (
                dot(score, widen(s, slice(0, width)), 0, 0) * 0.125
            ).astype(bf16)
        keys = [
            dot(score, queries[s * length : (s + 1) * length, :]) for s, score in zip(group, scores)
        ]
        for s, key, value in zip(group, keys, values):
            at = slice(s * mem_total, (s + 1) * mem_total)
            low_pairs[at, :width] = (narrow(key) * 0.125).astype(bf16)
            low_pairs[at, width:] = narrow(value).astype(bf16)
    for copy in later + last:
        copy.wait()
    half = width // 2

    def give(n, left, right):
        found = dot(left[...], right, 0, 0).astype(bf16)
        size = send.shape[0] // 8
        give_rows(bits, n * half, found[:half], found[half:], send, keep, size, TURNED[0])

    give(0, cross, grad_normed[...])
    sent = []
    for n in range(4):
        back = dot(low_queries[blocks[n], :], w_query[...], 1, 1)
        normal, spread = normalize(mid[blocks[n], :].astype(f32))
        mid[blocks[n], :] = (normal * gain_cross[...]).astype(bf16)
        low = (running[blocks[n], :] + norm_backward(back, gain_cross[...], normal, spread)).astype(bf16)
        out[blocks[n], :] = low
        copy = pltpu.make_async_copy(
            out.at[blocks[n], :], gradient.at[blocks[n], :], arrival.at[len(copies) + n]
        )
        copy.start()
        sent.append(copy)
    give(1, mid, low_queries[...])
    give(2, arrived, low_pairs[:, :width])
    give(3, arrived, low_pairs[:, width:])
    give(4, attended, out[...])
    grad_rows = dot(low_pairs[...], w_kv[...], 1, 1).astype(bf16)
    count = seqs
    total = grad_rows.shape[0]
    block = min(total, 512)
    for start in range(0, total, block):
        row = lax.broadcasted_iota(jnp.int32, (block, total), 0) + start
        column = lax.broadcasted_iota(jnp.int32, (block, total), 1)
        shift = count.bit_length() - 1
        source = (row & (count - 1)) * mem_total + (row >> shift)
        order = jnp.where(column == source, 1.0, 0.0).astype(bf16)
        grad_arrived[start : start + block, :] = dot(order, grad_rows).astype(bf16)
    for copy in sent:
        copy.wait()


def self_backward_kernel(
    length,
    bits, gradient_far, triple_far, weights_far, act_far, w_out_far,
    grad_triple_far, send, keep,
    gradient, triple, weights, act, w_out, grad_triple, arrival,
):
    rows, width = gradient.shape
    seqs = rows // length // 4
    blocks = [slice(n * rows // 4, (n + 1) * rows // 4) for n in range(4)]
    copies = []

    def move(source, target):
        copy = pltpu.make_async_copy(source, target, arrival.at[len(copies)])
        copies.append(copy)
        copy.start()
        return copy

    def fetch(n):
        own = slice(n * seqs, (n + 1) * seqs)
        return [
            move(gradient_far.at[blocks[n], :], gradient.at[blocks[n], :]),
            move(triple_far.at[blocks[n], :], triple.at[blocks[n], :]),
            move(weights_far.at[own], weights.at[own]),
        ]

    ready = [move(w_out_far, w_out)]
    waiting = [fetch(0), fetch(1)]
    first, second = head_masks(length)
    sent = []
    for n in range(4):
        for copy in waiting[n] + ready:
            copy.wait()
        ready = []
        if n < 2:
            waiting.append(fetch(n + 2))
        if n == 2:
            late = move(act_far, act)
        low = dot(gradient[blocks[n], :], w_out[...], 1, 1).astype(bf16)
        group = []
        for s in range(n * seqs, (n + 1) * seqs):
            for p in range(width // PAIR):
                at = [slice(j * width + p * PAIR, j * width + (p + 1) * PAIR) for j in range(3)]
                group.append((s, p, slice(s * length, (s + 1) * length), at))
        grads = [
            spread_pair(low[(s - n * seqs) * length : (s + 1 - n * seqs) * length, at[0]], first, second)
            for s, p, span, at in group
        ]
        softs = [weights[s, p] for s, p, span, at in group]
        changes = [dot(triple[span, at[2]], grad, 1, 1) for (s, p, span, at), grad in zip(group, grads)]
        values = [dot(soft, grad).astype(bf16) for soft, grad in zip(softs, grads)]
        scores = []
        for soft, change in zip(softs, changes):
            soft = soft.astype(f32)
            product = soft * change
            scores.append((product - soft * jnp.sum(product, axis=0, keepdims=True)).astype(bf16))
        keys = [
            dot(score, spread_pair(triple[span, at[0]] * 0.125, first, second)).astype(bf16)
            for (s, p, span, at), score in zip(group, scores)
        ]
        queries = [
            (dot(stack_pair(score), spread_pair(triple[span, at[1]], first, second), 0, 0) * 0.125).astype(bf16)
            for (s, p, span, at), score in zip(group, scores)
        ]
        for k, (s, p, span, at) in enumerate(group):
            grad_triple[span, at[0]] = queries[k]
            grad_triple[span, at[1]] = keys[k]
            grad_triple[span, at[2]] = values[k]
        sent.append(move(grad_triple.at[blocks[n], :], grad_triple_far.at[blocks[n], :]))
    late.wait()
    half = width // 2
    for j in range(3):
        found = dot(act[...], grad_triple[:, j * width : (j + 1) * width], 0, 0).astype(bf16)
        give_rows(bits, j * half, found[:half], found[half:], send, keep, send.shape[0] // 8, TURNED[1])
    for copy in sent:
        copy.wait()


def grad_tokens_kernel(bits, gradient, grad_triple, tokens, w_qkv, gain_self, grad_tokens):
    normal, spread = normalize(tokens[...].astype(f32))
    change = norm_backward(dot(grad_triple[...], w_qkv[...], 1, 1), gain_self[...], normal, spread)
    grad_tokens[...] = (gradient[...].astype(f32) + change).astype(bf16)


def row_sums(weight, grad, gain):
    product = weight.astype(f32) * grad
    columns = sum(product[:, n : n + PAIR] for n in range(0, product.shape[1], PAIR))
    return jnp.sum(columns.T, axis=0, keepdims=True) / gain


def in_order(bits, mine, own, got, ordered, turned):
    size = ordered.shape[0] // 8

    def fill(source):
        for n in range(8):
            at = pl.ds(pl.multiple_of(place(bits, n, turned) * size, size), size)
            ordered[n * size : (n + 1) * size, :] = source[at, :]

    @pl.when(mine)
    def _():
        fill(own)

    @pl.when(jnp.logical_not(mine))
    def _():
        fill(got)


def ffn_final_kernel(bits, own, got, w_expand, gain, contract, expand, gain_grad, ordered):
    step = pl.program_id(0)
    chunk = expand.shape[1]
    half = pl.num_programs(0) // 2
    in_order(bits, (step >= half) == (bits[0] == 1), own, got, ordered, lax.rem(step, half) == 1)
    contract[...] = ordered[:chunk, :].astype(f32)
    grad = ordered[chunk:, :].astype(f32)
    expand[...] = grad
    sums = row_sums(w_expand[...], grad, gain[...])

    @pl.when(step == 0)
    def _():
        gain_grad[...] = sums

    @pl.when(step > 0)
    def _():
        gain_grad[...] += sums


def cross_final_kernel(bits, own, got, w_query, gain, cross_out, query, pair, self_out, gain_grad, ordered):
    half, width = query.shape
    in_order(bits, pl.program_id(0) == bits[0], own, got, ordered, TURNED[0])
    cross_out[...] = ordered[:half, :].astype(f32)
    grad = ordered[half : 2 * half, :].astype(f32)
    query[...] = grad
    pair[:, :width] = ordered[2 * half : 3 * half, :].astype(f32)
    pair[:, width:] = ordered[3 * half : 4 * half, :].astype(f32)
    self_out[...] = ordered[4 * half :, :].astype(f32)
    gain_grad[...] = row_sums(w_query[...], grad, gain[...])


def self_final_kernel(bits, own, got, w_qkv, gain, qkv, gain_grad, ordered):
    half = qkv.shape[0]
    width = own.shape[1]
    in_order(bits, pl.program_id(0) == bits[0], own, got, ordered, TURNED[1])
    for j in range(3):
        qkv[:, j * width : (j + 1) * width] = ordered[j * half : (j + 1) * half, :].astype(f32)
    gain_grad[...] = row_sums(w_qkv[...], qkv[...], gain[...])


def call(kernel, grid, bits, ins, outs, scratch=(), flops=0, deps=(), limit=VMEM_LIMIT):
    moved = sum(a.size * a.dtype.itemsize for a, *_ in ins)
    shapes = []
    for shape, dtype, _, *space in outs:
        size = 1
        for n in shape:
            size *= n
        moved += size * jnp.dtype(dtype).itemsize
        shapes.append(space[0](shape, dtype) if space else jax.ShapeDtypeStruct(shape, dtype))
    count = len(ins)
    arrays = [
        pltpu.with_memory_space_constraint(a, space[0] if space else HBM)
        if space or a.size <= 4096 else a
        for a, _, *space in ins
    ]

    def body(bits_ref, *refs):
        kernel(bits_ref, *refs[:count], *refs[count + len(deps) :])

    return pl.pallas_call(
        body,
        grid_spec=pltpu.PrefetchScalarGridSpec(
            num_scalar_prefetch=1,
            grid=grid,
            in_specs=[spec for _, spec, *_ in ins] + [pl.BlockSpec(memory_space=pl.ANY)] * len(deps),
            out_specs=[spec for _, _, spec, *_ in outs],
            scratch_shapes=list(scratch),
        ),
        out_shape=shapes,
        compiler_params=pltpu.CompilerParams(vmem_limit_bytes=limit * 1024 * 1024),
        cost_estimate=pl.CostEstimate(flops=flops, bytes_accessed=moved, transcendentals=0),
    )(bits, *arrays, *deps)


def by_step(*shape):
    return pl.BlockSpec(shape, lambda i, bits: (i,) + (0,) * (len(shape) - 1))


def whole(*shape):
    return pl.BlockSpec(shape, lambda i, bits: (0,) * len(shape))


def scalars():
    return pl.BlockSpec(memory_space=pltpu.SMEM)


SEQS = 4
GROUP = 16
TURNED = (True, None)
PLAN = (
    "do ffn",
    "cross",
    "do ffn",
    "start cross",
    "do cross",
    "do ffn",
    "memory",
    "self",
    "start self",
    "do ffn",
    "do cross",
    "do self",
    "do cross",
    "do ffn",
    "do cross",
    "do self",
    "do ffn",
    "do self",
    "do cross",
    "do ffn",
    "do self",
    "do cross",
    "do self",
    "do self",
    "do ffn",
    "do cross",
    "do self",
    "tokens",
    "do self",
    "do cross",
    "end ffn",
    "end self",
    "end cross",
)


def self_forward(bits, tokens, lengths, gain_self, w_qkv, w_out, gain_cross, w_query, length):
    rows, width = tokens.shape
    n = rows // length
    block = SEQS * length
    row = by_step(block, width)
    return call(
        functools.partial(self_forward_kernel, SEQS, length, width),
        (n // SEQS,), bits,
        [
            (lengths, scalars()), (tokens, row, HBM),
            (gain_self, whole(1, width)), (w_qkv, whole(width, 3 * width), HBM),
            (w_out, whole(width, width), HBM), (gain_cross, whole(1, width)),
            (w_query, whole(width, width), HBM),
        ],
        [
            ((rows, width), bf16, row, HBM),
            ((rows, 3 * width), bf16, by_step(block, 3 * width), HBM),
            ((n, width // PAIR, length, 2 * length), bf16, by_step(SEQS, width // PAIR, length, 2 * length), HBM),
            ((rows, width), bf16, row, HBM),
            ((rows, width), bf16, row, HBM),
            ((rows, width), bf16, row, HBM),
        ],
        flops=12 * rows * width * width,
        limit=36,
    )


def cross_forward(bits, lengths, memory_lengths, raw, queries, mid, grad_output, w_kv, w_out, gain_ffn, length, mem_total):
    rows, width = queries.shape
    n = rows // length
    block = SEQS * length
    mem = SEQS * mem_total
    heads = width // HEAD
    row = by_step(block, width)
    return call(
        functools.partial(cross_forward_kernel, SEQS, length, width, mem_total),
        (n // SEQS,), bits,
        [
            (lengths, scalars()), (memory_lengths, scalars()),
            (raw, whole(*raw.shape)), (queries, row, HBM),
            (mid, row, HBM), (grad_output, row, HBM),
            (w_kv, whole(width, 2 * width), HBM), (w_out, whole(width, width), HBM),
            (gain_ffn, whole(1, width)),
        ],
        [
            ((n * mem_total, width), bf16, by_step(mem, width), HBM),
            ((n * mem_total, 2 * width), bf16, by_step(mem, 2 * width), HBM),
            ((n, heads * mem_total, length), bf16, by_step(SEQS, heads * mem_total, length), HBM),
            ((rows, width), bf16, row, HBM),
            ((rows, width), bf16, row, HBM),
            ((rows, width), bf16, row, HBM),
            ((rows, width), bf16, row, VMEM),
            ((rows, width), bf16, row, VMEM),
            ((rows, width), bf16, row, VMEM),
        ],
        flops=6 * rows * width * width,
        limit=VMEM_LIMIT if mem_total <= 32 else 2 * VMEM_LIMIT,
    )


def feed_forward(bits, act, grad_low, start, w_expand, w_contract, chunk=FF_CHUNK):
    rows, width = act.shape
    hidden = w_expand.shape[1]
    steps = hidden // chunk
    half = steps // 2

    def at(i, bits):
        return lax.rem(i + half * (1 - bits[0]), steps)

    def block(place):
        return pl.BlockSpec((2 * chunk, width), lambda i, bits: (place(i), 0))

    return call(
        functools.partial(ffn_kernel, min(rows, FF_ROWS)),
        (steps,), bits,
        [
            (act, whole(rows, width)), (grad_low, whole(rows, width)), (start, whole(rows, width)),
            (w_expand, pl.BlockSpec((width, chunk), lambda i, bits: (0, at(i, bits)))),
            (w_contract, pl.BlockSpec((chunk, width), lambda i, bits: (at(i, bits), 0))),
        ],
        [
            ((rows, width), bf16, whole(rows, width), HBM),
            ((rows, width), bf16, whole(rows, width), HBM),
            ((hidden, width), bf16, block(lambda i: jnp.minimum(i, half - 1)), HBM),
            ((hidden, width), bf16, block(lambda i: jnp.maximum(i - half, 0)), HBM),
        ],
        [
            pltpu.VMEM((rows, chunk), bf16),
            pltpu.VMEM((rows, chunk), bf16),
            pltpu.VMEM((rows, width), f32),
            pltpu.VMEM((rows, width), f32),
        ],
        flops=12 * rows * width * hidden,
        limit=FF_LIMIT,
    )


def cross_backward(bits, grad_normed, late, grad_low, cross, weights, pairs, queries, mid, arrived, attended, w_out, w_query, w_kv, gain_ffn, gain_cross, length, mem_total, deps=()):
    rows, width = queries.shape
    far = [
        grad_normed, late, grad_low, cross, weights, pairs, queries, mid, arrived, attended,
        w_out, w_query, w_kv,
    ]
    anywhere = pl.BlockSpec(memory_space=pl.ANY)
    return call(
        functools.partial(cross_backward_kernel, length, mem_total),
        (1,), bits,
        [(a, anywhere, HBM) for a in far]
        + [(gain_ffn, whole(1, width)), (gain_cross, whole(1, width))],
        [
            ((rows, width), bf16, anywhere, HBM),
            (arrived.shape, bf16, whole(*arrived.shape), HBM),
            ((5 * width // 2, width), bf16, whole(5 * width // 2, width), HBM),
            ((5 * width // 2, width), bf16, whole(5 * width // 2, width), HBM),
        ],
        [pltpu.VMEM(a.shape, bf16) for a in far]
        + [
            pltpu.VMEM((rows, width), f32),
            pltpu.VMEM((rows, width), bf16),
            pltpu.VMEM((rows, width), bf16),
            pltpu.VMEM(pairs.shape, bf16),
            pltpu.SemaphoreType.DMA((32,)),
        ],
        flops=14 * rows * width * width,
        deps=deps,
        limit=48 if mem_total <= 32 else 62,
    )


def self_backward(bits, gradient, triple, weights, act, w_out, length, deps=()):
    rows, width = gradient.shape
    far = [gradient, triple, weights, act, w_out]
    anywhere = pl.BlockSpec(memory_space=pl.ANY)
    return call(
        functools.partial(self_backward_kernel, length),
        (1,), bits,
        [(a, anywhere, HBM) for a in far],
        [
            (triple.shape, bf16, anywhere, HBM),
            ((3 * width // 2, width), bf16, whole(3 * width // 2, width), HBM),
            ((3 * width // 2, width), bf16, whole(3 * width // 2, width), HBM),
        ],
        [pltpu.VMEM(a.shape, bf16) for a in far]
        + [pltpu.VMEM(triple.shape, bf16), pltpu.SemaphoreType.DMA((24,))],
        flops=14 * rows * width * width,
        deps=deps,
        limit=44,
    )


def token_gradient(bits, gradient, grad_triple, tokens, w_qkv, gain_self, deps=()):
    rows, width = tokens.shape
    block = TOKEN_ROWS
    row = by_step(block, width)
    return call(
        grad_tokens_kernel, (rows // block,), bits,
        [
            (gradient, row, HBM), (grad_triple, by_step(block, 3 * width), HBM), (tokens, row, HBM),
            (w_qkv, whole(width, 3 * width), HBM), (gain_self, whole(1, width)),
        ],
        [((rows, width), bf16, row)],
        flops=6 * rows * width * width,
        deps=deps,
    )[0]


def after(arrays, deps):
    if not deps:
        return arrays
    return lax.optimization_barrier((*arrays, *deps))[: len(arrays)]


def added(left, right):
    return (left.astype(f32) + right.astype(f32)).astype(bf16)


def exchange(block, bit, devices):
    return lax.ppermute(block, "dp", [(i, i ^ (1 << bit)) for i in range(devices)])


class Lane:
    def __init__(self, devices, orders, send, keep):
        self.devices, self.orders, self.count = devices, orders, len(orders)
        self.rest = list(range(4, devices.bit_length() - 1))
        self.level, self.state = 0, "halve"
        self.own = self.parted(keep)
        self.got = self.parted(exchange(send, 0, devices))
        self.token = send

    def parted(self, block):
        size = block.shape[0] // self.count
        return [block[n * size : (n + 1) * size] for n in range(self.count)]

    def send(self, blocks):
        self.token = blocks[0]
        if self.level in (1, 2):
            bits = [order[self.level - 1] for order in self.orders]
            self.got = [exchange(b, bit, self.devices) for b, bit in zip(blocks, bits)]
        else:
            bit = {0: 0, 3: 3}.get(self.level, self.level)
            whole_block = jnp.concatenate(blocks) if len(blocks) > 1 else blocks[0]
            self.token = whole_block
            self.got = self.parted(exchange(whole_block, bit, self.devices))

    def advance(self, deps=()):
        both = after((*self.own, *self.got), deps)
        own, got = both[: self.count], both[self.count :]
        if self.state == "halve":
            half = own[0].shape[0] // 2
            self.own = [added(a[half:], b[half:]) for a, b in zip(own, got)]
            self.level += 1
            self.send([added(a[:half], b[:half]) for a, b in zip(own, got)])
            if self.level == 3:
                self.state = "whole"
        elif self.state == "whole":
            self.own = [added(a, b) for a, b in zip(own, got)]
            if self.rest:
                self.level = self.rest.pop(0)
            else:
                self.level, self.state = 3, "join"
            self.send(self.own)
        else:
            self.own = [jnp.concatenate([b, a]) for a, b in zip(own, got)]
            self.level -= 1
            self.send(self.own)
            if self.level == 0:
                self.state = "done"

    def result(self):
        return [blocks[0] if self.count == 1 else jnp.concatenate(blocks) for blocks in (self.own, self.got)]


def ffn_final(bits, own, got, w_expand, gain, deps=(), chunk=512):
    width, hidden = w_expand.shape
    steps = hidden // chunk

    def source(mine):
        def at(i, bits):
            first = (bits[0] == 0) == mine
            return (jnp.where(first, jnp.minimum(i, steps // 2 - 1), jnp.maximum(i - steps // 2, 0)), 0)

        return pl.BlockSpec((2 * chunk, width), at)

    return call(
        ffn_final_kernel, (steps,), bits,
        [
            (own, source(True)), (got, source(False)),
            (w_expand, pl.BlockSpec((width, chunk), lambda i, bits: (0, i)), HBM),
            (gain, whole(1, width)),
        ],
        [
            ((hidden, width), f32, by_step(chunk, width)),
            ((width, hidden), f32, pl.BlockSpec((width, chunk), lambda i, bits: (0, i))),
            ((1, width), f32, whole(1, width)),
        ],
        [pltpu.VMEM((2 * chunk, width), bf16)],
        deps=deps,
    )


def cross_final(bits, own, got, w_query, gain, deps=()):
    width = w_query.shape[0]
    half = width // 2
    part = by_step(half, width)
    column = pl.BlockSpec((1, half), lambda i, bits: (0, i))
    return call(
        cross_final_kernel, (2,), bits,
        [
            (own, whole(*own.shape)), (got, whole(*own.shape)), (w_query, part, HBM), (gain, column),
        ],
        [
            ((width, width), f32, part), ((width, width), f32, part),
            ((width, 2 * width), f32, by_step(half, 2 * width)), ((width, width), f32, part),
            ((1, width), f32, column),
        ],
        [pltpu.VMEM(own.shape, bf16)],
        deps=deps,
    )


def self_final(bits, own, got, w_qkv, gain, deps=()):
    width = w_qkv.shape[0]
    half = width // 2
    column = pl.BlockSpec((1, half), lambda i, bits: (0, i))
    return call(
        self_final_kernel, (2,), bits,
        [
            (own, whole(*own.shape)), (got, whole(*own.shape)),
            (w_qkv, by_step(half, 3 * width), HBM), (gain, column),
        ],
        [((width, 3 * width), f32, by_step(half, 3 * width)), ((1, width), f32, column)],
        [pltpu.VMEM(own.shape, bf16)],
        deps=deps,
    )


def local(
    devices, tokens, memory, target_lengths, memory_lengths, grad_output,
    gain_self, w_qkv, w_self_out, gain_cross, w_cross_query, w_cross_kv, w_cross_out,
    gain_ffn, w_expand, w_contract,
):
    seq_count, length, width = tokens.shape
    rows = seq_count * length
    gain_self, gain_cross, gain_ffn = gain_self[None], gain_cross[None], gain_ffn[None]
    flat_tokens = tokens.reshape(rows, width)
    me = lax.axis_index("dp")
    bits = jnp.stack([(me >> b) & 1 for b in range(devices.bit_length() - 1)]).astype(jnp.int32)
    raw = lax.all_to_all(
        memory.reshape(devices, -1, width), "dp", split_axis=0, concat_axis=0, tiled=True
    ).reshape(-1, width)
    mem_total = raw.shape[0] // seq_count
    act_one, triple, self_weights, attended, mid, queries = self_forward(
        bits, flat_tokens, target_lengths, gain_self, w_qkv, w_self_out, gain_cross, w_cross_query, length
    )
    arrived, pairs, cross_weights, cross, late, grad_low, late_near, grad_low_near, act = cross_forward(
        bits, target_lengths, memory_lengths, raw, queries, mid, grad_output.reshape(rows, width),
        w_cross_kv, w_cross_out, gain_ffn, length, mem_total,
    )
    output, grad_normed, send, keep = feed_forward(
        bits, act, grad_low_near, late_near, w_expand, w_contract
    )
    straight, turned = (1, 2), (2, 1)
    lanes = {"ffn": Lane(devices, (straight, turned), send, keep)}
    token, fresh, kept, found = send, {}, {}, {}
    for n, name in enumerate(PLAN):
        deps = [token]
        if PLAN[n - 1] == "self":
            deps.append(grad_memory)
        if name.startswith("end"):
            lane = lanes[name[4:]]
            while lane.state != "done":
                lane.advance(deps)
                deps = [lane.token]
        if name == "cross":
            gradient, grad_arrived, send, keep = cross_backward(
                bits, grad_normed, late, grad_low, cross, cross_weights, pairs, queries, mid, arrived,
                attended, w_cross_out, w_cross_query, w_cross_kv, gain_ffn, gain_cross, length, mem_total,
                deps=deps,
            )
            token = fresh["cross"] = send
            kept["cross"] = keep
        elif name == "self":
            grad_triple, send, keep = self_backward(
                bits, gradient, triple, self_weights, act_one, w_self_out, length, deps=deps
            )
            token = fresh["self"] = send
            kept["self"] = keep
        elif name == "tokens":
            token = grad_tokens = token_gradient(
                bits, gradient, grad_triple, flat_tokens, w_qkv, gain_self, deps=deps
            )
        elif name == "memory":
            grad_memory = lax.all_to_all(
                after((grad_arrived,), deps)[0].reshape(devices, -1, width),
                "dp", split_axis=0, concat_axis=0, tiled=True,
            ).reshape(memory.shape)
        elif name in ("start cross", "start self"):
            name = name[6:]
            order = turned if TURNED[name == "self"] else straight
            lanes[name] = Lane(devices, (order,), after((fresh[name],), deps)[0], kept[name])
        elif name == "end ffn":
            own, got = lanes["ffn"].result()
            found["ffn"] = ffn_final(bits, own, got, w_expand, gain_ffn, deps=deps)
            token = found["ffn"][2]
        elif name == "end cross":
            own, got = lanes["cross"].result()
            found["cross"] = cross_final(bits, own, got, w_cross_query, gain_cross, deps=deps)
            token = found["cross"][4]
        elif name == "end self":
            own, got = lanes["self"].result()
            found["self"] = self_final(bits, own, got, w_qkv, gain_self, deps=deps)
            token = found["self"][1]
        else:
            lane = lanes[name[3:]]
            if lane.state != "done":
                lane.advance(deps)
                token = lane.token
    grad_contract, grad_expand, grad_gain_ffn = found["ffn"]
    grad_cross_out, grad_cross_query, grad_cross_kv, grad_self_out, grad_gain_cross = found["cross"]
    grad_qkv, grad_gain_self = found["self"]
    return (
        output.reshape(tokens.shape),
        grad_tokens.reshape(tokens.shape),
        grad_memory,
        grad_gain_self[0],
        grad_qkv,
        grad_self_out,
        grad_gain_cross[0],
        grad_cross_query,
        grad_cross_kv,
        grad_cross_out,
        grad_gain_ffn[0],
        grad_expand,
        grad_contract,
    )


def solution(mesh):
    rows, columns, copied = P("dp", None, None), P(None, "dp", None), P()
    return jax.shard_map(
        functools.partial(local, mesh.shape["dp"]),
        mesh=mesh,
        in_specs=(rows, columns, P("dp"), P("dp"), rows) + (copied,) * 10,
        out_specs=(rows, rows, columns) + (copied,) * 10,
        check_vma=False,
    )
```

```python
import functools
import jax
import jax.numpy as jnp
from jax import lax
from jax.experimental import pallas as pl
from jax.experimental.pallas import tpu as pltpu
from jax.sharding import PartitionSpec as P

HEAD = 64
PAIR = 128
epsilon = 1e-05
big_negative = -1e30
f32 = jnp.float32
bf16 = jnp.bfloat16
VMEM_LIMIT = 24
HBM = pltpu.HBM
VMEM = pltpu.VMEM


def dot(left, right, left_dim=1, right_dim=0):
    return lax.dot_general(
        left, right, (((left_dim,), (right_dim,)), ((), ())), preferred_element_type=f32
    )


def normalize(hidden):
    centred = hidden - jnp.mean(hidden, axis=-1, keepdims=True)
    spread = lax.rsqrt(jnp.mean(centred * centred, axis=-1, keepdims=True) + epsilon)
    return centred * spread, spread


def norm_backward(gradient, gain, normalized, spread):
    scaled = gradient * gain
    first = jnp.mean(scaled, axis=-1, keepdims=True)
    second = jnp.mean(scaled * normalized, axis=-1, keepdims=True)
    return spread * (scaled - first - normalized * second)


def head_masks(rows):
    lane = lax.broadcasted_iota(jnp.int32, (rows, PAIR), 1)
    first = jnp.where(lane < HEAD, 1.0, 0.0).astype(bf16)
    second = jnp.where(lane >= HEAD, 1.0, 0.0).astype(bf16)
    return first, second


def spread_pair(block, first, second):
    return jnp.concatenate([block * first, block * second], axis=0)


def stack_pair(block):
    half = block.shape[1] // 2
    return jnp.concatenate([block[:, :half], block[:, half:]], axis=0)


def wide_mask(mem_total, width):
    lane = lax.broadcasted_iota(jnp.int32, (mem_total, width), 1)
    parts = [
        jnp.where((lane >= h * HEAD) & (lane < (h + 1) * HEAD), 1.0, 0.0)
        for h in range(width // HEAD)
    ]
    return parts


PARTS = 1
CROSS_GROUP = 4
FF_CHUNK = 512
FF_ROWS = 512
TOKEN_ROWS = 512
FF_LIMIT = 36
LAG = 1


def stagger(parts):
    waiting = [LAG * n for n in range(len(parts))]
    while parts:
        left = []
        for n, part in enumerate(parts):
            if waiting[n]:
                waiting[n] -= 1
                left.append(n)
            elif next(part, part) is not part:
                left.append(n)
        parts, waiting = [parts[n] for n in left], [waiting[n] for n in left]


def self_forward_kernel(
    seqs, length, width,
    bits, lengths, tokens, gain_self, w_qkv, w_out, gain_cross, w_query,
    act, triple, weights, attended, mid, queries,
):
    step = pl.program_id(0)
    first, second = head_masks(length)
    key_at = lax.broadcasted_iota(jnp.int32, (length, 2 * length), 0)
    query_at = lax.broadcasted_iota(jnp.int32, (length, 2 * length), 1)
    query_at = jnp.where(query_at >= length, query_at - length, query_at)
    causal = key_at <= query_at
    count = seqs // PARTS

    def part(n):
        span = slice(n * count * length, (n + 1) * count * length)
        residual = tokens[span, :].astype(f32)
        normal, _ = normalize(residual)
        low = (normal * gain_self[...]).astype(bf16)
        yield
        both = dot(low, w_qkv[...]).astype(bf16)
        yield
        heads = [(s, p) for s in range(count) for p in range(width // PAIR)]
        scores = []
        for s, p in heads:
            rows = slice(s * length, (s + 1) * length)
            q = both[rows, p * PAIR : (p + 1) * PAIR] * 0.125
            k = both[rows, width + p * PAIR : width + (p + 1) * PAIR]
            scores.append(dot(k, spread_pair(q, first, second), 1, 1))
        yield
        softs = []
        for (s, p), score in zip(heads, scores):
            allowed = causal & (key_at < lengths[step * seqs + n * count + s])
            score = jnp.where(allowed, score, big_negative)
            raised = jnp.exp(score - jnp.max(score, axis=0, keepdims=True))
            softs.append((raised * (1.0 / jnp.sum(raised, axis=0, keepdims=True))).astype(bf16))
        yield
        joined = {}
        for (s, p), soft in zip(heads, softs):
            rows = slice(s * length, (s + 1) * length)
            v = both[rows, 2 * width + p * PAIR : 2 * width + (p + 1) * PAIR]
            joined[s, p] = dot(stack_pair(soft), spread_pair(v, first, second), 0, 0).astype(bf16)
        yield
        out = jnp.concatenate(
            [
                jnp.concatenate([joined[s, p] for p in range(width // PAIR)], axis=1)
                for s in range(count)
            ],
            axis=0,
        )
        residual = residual + dot(out, w_out[...])
        yield
        normal, _ = normalize(residual)
        after = (normal * gain_cross[...]).astype(bf16)
        yield
        found = dot(after, w_query[...]).astype(bf16)
        yield
        act[span, :] = low
        triple[span, :] = both
        attended[span, :] = out
        mid[span, :] = residual.astype(bf16)
        queries[span, :] = found
        for (s, p), soft in zip(heads, softs):
            weights[n * count + s, p] = soft

    stagger([part(n) for n in range(PARTS)])


def cross_forward_kernel(
    seqs, length, width, mem_total,
    bits, lengths, memory_lengths, raw, queries, mid, grad_output, w_kv, w_out, gain_ffn,
    arrived, pairs, weights, cross, late, grad_low, late_near, grad_low_near, act,
):
    step = pl.program_id(0)
    total = raw.shape[0] // mem_total
    at = lax.broadcasted_iota(jnp.int32, (mem_total, raw.shape[0]), 0) * total
    column = lax.broadcasted_iota(jnp.int32, (mem_total, raw.shape[0]), 1)
    own_rows = jnp.concatenate(
        [jnp.where(column == at + (step * seqs + s), 1.0, 0.0).astype(bf16) for s in range(seqs)],
        axis=0,
    )
    own_rows = dot(own_rows, raw[...]).astype(bf16)
    arrived[...] = own_rows
    both = dot(own_rows, w_kv[...]).astype(bf16)
    pairs[...] = both
    mask = jnp.concatenate(wide_mask(mem_total, width), axis=0).astype(bf16)
    heads = width // HEAD
    key_at = lax.broadcasted_iota(jnp.int32, (mem_total, length), 0)
    row_at = lax.broadcasted_iota(jnp.int32, (length, width), 0)

    def spread(s, at):
        return jnp.concatenate([both[s * mem_total : (s + 1) * mem_total, at]] * heads, axis=0) * mask

    scores = []
    for s in range(seqs):
        q = queries[s * length : (s + 1) * length, :] * 0.125
        scores.append(dot(spread(s, slice(0, width)), q, 1, 1).reshape(heads, mem_total, length))
    softs = []
    for s in range(seqs):
        allowed = (key_at < memory_lengths[step * seqs + s])[None]
        score = jnp.where(allowed, scores[s], big_negative)
        raised = jnp.exp(score - jnp.max(score, axis=1, keepdims=True))
        soft = raised * (1.0 / jnp.sum(raised, axis=1, keepdims=True))
        softs.append(soft.reshape(heads * mem_total, length).astype(bf16))
    joined = [dot(softs[s], spread(s, slice(width, 2 * width)), 0, 0).astype(bf16) for s in range(seqs)]
    low = jnp.concatenate(joined, axis=0)
    cross[...] = low
    for s in range(seqs):
        rows = slice(s * length, (s + 1) * length)
        weights[s] = softs[s]
        live = row_at < lengths[step * seqs + s]
        masked = jnp.where(live, grad_output[rows, :].astype(f32), 0.0).astype(bf16)
        grad_low[rows, :] = masked
        grad_low_near[rows, :] = masked
    residual = mid[...].astype(f32) + dot(low, w_out[...])
    late[...] = residual.astype(bf16)
    late_near[...] = residual.astype(bf16)
    normal, _ = normalize(residual)
    act[...] = (normal * gain_ffn[...]).astype(bf16)


def gelu_parts(value):
    half = 0.5 + 0.5 * lax.erf(value * 0.7071067811865476)
    bell = value * jnp.exp2(value * value * (-0.5 * 1.4426950408889634))
    return value * half, half + 0.3989422804014327 * bell


def place(bits, n, turned=None):
    first, second = bits[1], bits[2]
    if turned is not None:
        first, second = jnp.where(turned, second, first), jnp.where(turned, first, second)
    mine = first * 4 + second * 2 + bits[3]
    return jnp.bitwise_xor(mine, 7 - n)


def ffn_kernel(
    row_block,
    bits, act, grad_low, start, w_expand, w_contract,
    result, grad_normed, send, keep,
    activated, grad_expanded, total, change,
):
    step = pl.program_id(0)
    rows = act.shape[0]
    chunk = w_expand.shape[1]

    @pl.when(step == 0)
    def _():
        total[...] = start[...].astype(f32)
        change[...] = jnp.zeros_like(change)

    for b in range(rows // row_block):
        r = slice(b * row_block, (b + 1) * row_block)
        expanded = dot(act[r, :], w_expand[...])
        grad_activated = dot(grad_low[r, :], w_contract[...], 1, 1)
        value, slope = gelu_parts(expanded)
        value = value.astype(bf16)
        slope = (grad_activated * slope).astype(bf16)
        activated[r, :] = value
        grad_expanded[r, :] = slope
        total[r, :] += dot(value, w_contract[...])
        change[r, :] += dot(slope, w_expand[...], 1, 1)

    def fill(grads):
        unit = grad_low.shape[1]
        size = unit // 4
        contract = dot(activated[...], grad_low[...], 0, 0)
        expand = dot(act[...], grad_expanded[...], 0, 0)
        for k in range(chunk // unit):
            found = [contract[k * unit : (k + 1) * unit, :], expand[:, k * unit : (k + 1) * unit]]
            turned = lax.rem(step * (chunk // unit) + k, 2) == 1
            for n in range(8):
                at = k * 2 * unit + place(bits, n, turned) * size
                at = pl.ds(pl.multiple_of(at, size), size)
                grads[at, :] = found[n // 4][n % 4 * size : (n % 4 + 1) * size, :].astype(bf16)

    @pl.when(step < pl.num_programs(0) // 2)
    def _():
        fill(send)

    @pl.when(step >= pl.num_programs(0) // 2)
    def _():
        fill(keep)

    @pl.when(step == pl.num_programs(0) - 1)
    def _():
        result[...] = total[...].astype(bf16)
        grad_normed[...] = change[...].astype(bf16)


def give_rows(bits, start, low, high, send, keep, size, turned):
    first = bits[0] == 0
    for side, one, other in ((keep, low, high), (send, high, low)):
        rows = jnp.where(first, one, other)
        at, end = start, start + low.shape[0]
        while at < end:
            part = at // size
            stop = min(end, (part + 1) * size)
            to = place(bits, part, turned) * size + (at - part * size)
            to = pl.ds(pl.multiple_of(to, 32), stop - at)
            side[to, :] = rows[at - start : stop - start, :]
            at = stop


def cross_backward_kernel(
    length, mem_total,
    bits, grad_normed_far, late_far, grad_low_far, cross_far, weights_far, pairs_far, queries_far, mid_far,
    arrived_far, attended_far, w_out_far, w_query_far, w_kv_far, gain_ffn, gain_cross,
    gradient, grad_arrived, send, keep,
    grad_normed, late, grad_low, cross, weights, pairs, queries, mid,
    arrived, attended, w_out, w_query, w_kv,
    running, low_queries, out, low_pairs, arrival,
):
    rows, width = grad_normed.shape
    seqs = rows // length
    heads = width // HEAD
    blocks = [slice(n * rows // 4, (n + 1) * rows // 4) for n in range(4)]
    copies = []

    def fetch(far, near):
        copy = pltpu.make_async_copy(far, near, arrival.at[len(copies)])
        copies.append(copy)
        copy.start()
        return copy

    def fetch_rows(n):
        return [
            fetch(far.at[blocks[n], :], near.at[blocks[n], :])
            for far, near in ((grad_normed_far, grad_normed), (late_far, late), (grad_low_far, grad_low))
        ]

    waiting = [fetch_rows(0), fetch_rows(1)]
    copy_out = fetch(w_out_far, w_out)
    masks = wide_mask(mem_total, width)
    mask = jnp.concatenate(masks, axis=0).astype(bf16)
    grad_cross = []
    for n in range(4):
        for copy in waiting[n]:
            copy.wait()
        if n < 2:
            waiting.append(fetch_rows(n + 2))
        if n == 1:
            early = [fetch(weights_far, weights), fetch(pairs_far, pairs), fetch(queries_far, queries)]
        if n == 2:
            later = [fetch(w_query_far, w_query), fetch(mid_far, mid)]
        if n == 3:
            last = [
                fetch(cross_far, cross), fetch(arrived_far, arrived), fetch(w_kv_far, w_kv),
                fetch(attended_far, attended),
            ]
        normal, spread = normalize(late[blocks[n], :].astype(f32))
        change = norm_backward(grad_normed[blocks[n], :].astype(f32), gain_ffn[...], normal, spread)
        change = grad_low[blocks[n], :].astype(f32) + change
        running[blocks[n], :] = change
        low = change.astype(bf16)
        grad_normed[blocks[n], :] = low
        if n == 0:
            copy_out.wait()
        grad_cross.append(dot(low, w_out[...], 1, 1).astype(bf16))
    grad_cross = jnp.concatenate(grad_cross, axis=0)

    def widen(s, at):
        return jnp.concatenate([pairs[s * mem_total : (s + 1) * mem_total, at]] * heads, axis=0) * mask

    def narrow(block):
        return sum(block[h * mem_total : (h + 1) * mem_total, :] * masks[h] for h in range(heads))

    for copy in early:
        copy.wait()
    for start in range(0, seqs, CROSS_GROUP):
        group = range(start, start + CROSS_GROUP)
        softs = [weights[s] for s in group]
        grads = [grad_cross[s * length : (s + 1) * length, :] for s in group]
        changes = [
            dot(widen(s, slice(width, 2 * width)), grad, 1, 1).reshape(heads, mem_total, length)
            for s, grad in zip(group, grads)
        ]
        values = [dot(soft, grad) for soft, grad in zip(softs, grads)]
        scores = []
        for soft, change in zip(softs, changes):
            soft = soft.astype(f32).reshape(heads, mem_total, length)
            product = soft * change
            score = product - soft * jnp.sum(product, axis=1, keepdims=True)
            scores.append(score.reshape(heads * mem_total, length).astype(bf16))
        for s, score in zip(group, scores):
            low_queries[s * length : (s + 1) * length, :] = (
                dot(score, widen(s, slice(0, width)), 0, 0) * 0.125
            ).astype(bf16)
        keys = [
            dot(score, queries[s * length : (s + 1) * length, :]) for s, score in zip(group, scores)
        ]
        for s, key, value in zip(group, keys, values):
            at = slice(s * mem_total, (s + 1) * mem_total)
            low_pairs[at, :width] = (narrow(key) * 0.125).astype(bf16)
            low_pairs[at, width:] = narrow(value).astype(bf16)
    for copy in later + last:
        copy.wait()
    half = width // 2

    def give(n, left, right):
        found = dot(left[...], right, 0, 0).astype(bf16)
        size = send.shape[0] // 8
        give_rows(bits, n * half, found[:half], found[half:], send, keep, size, TURNED[0])

    give(0, cross, grad_normed[...])
    sent = []
    for n in range(4):
        back = dot(low_queries[blocks[n], :], w_query[...], 1, 1)
        normal, spread = normalize(mid[blocks[n], :].astype(f32))
        mid[blocks[n], :] = (normal * gain_cross[...]).astype(bf16)
        low = (running[blocks[n], :] + norm_backward(back, gain_cross[...], normal, spread)).astype(bf16)
        out[blocks[n], :] = low
        copy = pltpu.make_async_copy(
            out.at[blocks[n], :], gradient.at[blocks[n], :], arrival.at[len(copies) + n]
        )
        copy.start()
        sent.append(copy)
    give(1, mid, low_queries[...])
    give(2, arrived, low_pairs[:, :width])
    give(3, arrived, low_pairs[:, width:])
    give(4, attended, out[...])
    grad_rows = dot(low_pairs[...], w_kv[...], 1, 1).astype(bf16)
    count = seqs
    total = grad_rows.shape[0]
    block = min(total, 512)
    for start in range(0, total, block):
        row = lax.broadcasted_iota(jnp.int32, (block, total), 0) + start
        column = lax.broadcasted_iota(jnp.int32, (block, total), 1)
        shift = count.bit_length() - 1
        source = (row & (count - 1)) * mem_total + (row >> shift)
        order = jnp.where(column == source, 1.0, 0.0).astype(bf16)
        grad_arrived[start : start + block, :] = dot(order, grad_rows).astype(bf16)
    for copy in sent:
        copy.wait()


def self_backward_kernel(
    length,
    bits, gradient_far, triple_far, weights_far, act_far, w_out_far,
    grad_triple_far, send, keep,
    gradient, triple, weights, act, w_out, grad_triple, arrival,
):
    rows, width = gradient.shape
    seqs = rows // length // 4
    blocks = [slice(n * rows // 4, (n + 1) * rows // 4) for n in range(4)]
    copies = []

    def move(source, target):
        copy = pltpu.make_async_copy(source, target, arrival.at[len(copies)])
        copies.append(copy)
        copy.start()
        return copy

    def fetch(n):
        own = slice(n * seqs, (n + 1) * seqs)
        return [
            move(gradient_far.at[blocks[n], :], gradient.at[blocks[n], :]),
            move(triple_far.at[blocks[n], :], triple.at[blocks[n], :]),
            move(weights_far.at[own], weights.at[own]),
        ]

    ready = [move(w_out_far, w_out)]
    waiting = [fetch(0), fetch(1)]
    first, second = head_masks(length)
    sent = []
    for n in range(4):
        for copy in waiting[n] + ready:
            copy.wait()
        ready = []
        if n < 2:
            waiting.append(fetch(n + 2))
        if n == 2:
            late = move(act_far, act)
        low = dot(gradient[blocks[n], :], w_out[...], 1, 1).astype(bf16)
        group = []
        for s in range(n * seqs, (n + 1) * seqs):
            for p in range(width // PAIR):
                at = [slice(j * width + p * PAIR, j * width + (p + 1) * PAIR) for j in range(3)]
                group.append((s, p, slice(s * length, (s + 1) * length), at))
        grads = [
            spread_pair(low[(s - n * seqs) * length : (s + 1 - n * seqs) * length, at[0]], first, second)
            for s, p, span, at in group
        ]
        softs = [weights[s, p] for s, p, span, at in group]
        changes = [dot(triple[span, at[2]], grad, 1, 1) for (s, p, span, at), grad in zip(group, grads)]
        values = [dot(soft, grad).astype(bf16) for soft, grad in zip(softs, grads)]
        scores = []
        for soft, change in zip(softs, changes):
            soft = soft.astype(f32)
            product = soft * change
            scores.append((product - soft * jnp.sum(product, axis=0, keepdims=True)).astype(bf16))
        keys = [
            dot(score, spread_pair(triple[span, at[0]] * 0.125, first, second)).astype(bf16)
            for (s, p, span, at), score in zip(group, scores)
        ]
        queries = [
            (dot(stack_pair(score), spread_pair(triple[span, at[1]], first, second), 0, 0) * 0.125).astype(bf16)
            for (s, p, span, at), score in zip(group, scores)
        ]
        for k, (s, p, span, at) in enumerate(group):
            grad_triple[span, at[0]] = queries[k]
            grad_triple[span, at[1]] = keys[k]
            grad_triple[span, at[2]] = values[k]
        sent.append(move(grad_triple.at[blocks[n], :], grad_triple_far.at[blocks[n], :]))
    late.wait()
    half = width // 2
    for j in range(3):
        found = dot(act[...], grad_triple[:, j * width : (j + 1) * width], 0, 0).astype(bf16)
        give_rows(bits, j * half, found[:half], found[half:], send, keep, send.shape[0] // 8, TURNED[1])
    for copy in sent:
        copy.wait()


def grad_tokens_kernel(bits, gradient, grad_triple, tokens, w_qkv, gain_self, grad_tokens):
    normal, spread = normalize(tokens[...].astype(f32))
    change = norm_backward(dot(grad_triple[...], w_qkv[...], 1, 1), gain_self[...], normal, spread)
    grad_tokens[...] = (gradient[...].astype(f32) + change).astype(bf16)


def row_sums(weight, grad, gain):
    product = weight.astype(f32) * grad
    columns = sum(product[:, n : n + PAIR] for n in range(0, product.shape[1], PAIR))
    return jnp.sum(columns.T, axis=0, keepdims=True) / gain


def in_order(bits, mine, own, got, ordered, turned):
    size = ordered.shape[0] // 8

    def fill(source):
        for n in range(8):
            at = pl.ds(pl.multiple_of(place(bits, n, turned) * size, size), size)
            ordered[n * size : (n + 1) * size, :] = source[at, :]

    @pl.when(mine)
    def _():
        fill(own)

    @pl.when(jnp.logical_not(mine))
    def _():
        fill(got)


def ffn_final_kernel(bits, own, got, w_expand, gain, brought, contract, expand, gain_grad, memory, ordered):
    step = pl.program_id(0)
    memory[...] = brought[...]
    chunk = expand.shape[1]
    half = pl.num_programs(0) // 2
    in_order(bits, (step >= half) == (bits[0] == 1), own, got, ordered, lax.rem(step, half) == 1)
    contract[...] = ordered[:chunk, :].astype(f32)
    grad = ordered[chunk:, :].astype(f32)
    expand[...] = grad
    sums = row_sums(w_expand[...], grad, gain[...])

    @pl.when(step == 0)
    def _():
        gain_grad[...] = sums

    @pl.when(step > 0)
    def _():
        gain_grad[...] += sums


def cross_final_kernel(bits, own, got, w_query, gain, cross_out, query, pair, self_out, gain_grad, ordered):
    half, width = query.shape
    in_order(bits, pl.program_id(0) == bits[0], own, got, ordered, TURNED[0])
    cross_out[...] = ordered[:half, :].astype(f32)
    grad = ordered[half : 2 * half, :].astype(f32)
    query[...] = grad
    pair[:, :width] = ordered[2 * half : 3 * half, :].astype(f32)
    pair[:, width:] = ordered[3 * half : 4 * half, :].astype(f32)
    self_out[...] = ordered[4 * half :, :].astype(f32)
    gain_grad[...] = row_sums(w_query[...], grad, gain[...])


def self_final_kernel(bits, own, got, w_qkv, gain, qkv, gain_grad, ordered):
    half = qkv.shape[0]
    width = own.shape[1]
    in_order(bits, pl.program_id(0) == bits[0], own, got, ordered, TURNED[1])
    for j in range(3):
        qkv[:, j * width : (j + 1) * width] = ordered[j * half : (j + 1) * half, :].astype(f32)
    gain_grad[...] = row_sums(w_qkv[...], qkv[...], gain[...])


def call(kernel, grid, bits, ins, outs, scratch=(), flops=0, deps=(), limit=VMEM_LIMIT):
    moved = sum(a.size * a.dtype.itemsize for a, *_ in ins)
    shapes = []
    for shape, dtype, _, *space in outs:
        size = 1
        for n in shape:
            size *= n
        moved += size * jnp.dtype(dtype).itemsize
        shapes.append(space[0](shape, dtype) if space else jax.ShapeDtypeStruct(shape, dtype))
    count = len(ins)
    arrays = [
        pltpu.with_memory_space_constraint(a, space[0]) if space else a for a, _, *space in ins
    ]

    def body(bits_ref, *refs):
        kernel(bits_ref, *refs[:count], *refs[count + len(deps) :])

    return pl.pallas_call(
        body,
        grid_spec=pltpu.PrefetchScalarGridSpec(
            num_scalar_prefetch=1,
            grid=grid,
            in_specs=[spec for _, spec, *_ in ins] + [pl.BlockSpec(memory_space=pl.ANY)] * len(deps),
            out_specs=[spec for _, _, spec, *_ in outs],
            scratch_shapes=list(scratch),
        ),
        out_shape=shapes,
        compiler_params=pltpu.CompilerParams(vmem_limit_bytes=limit * 1024 * 1024),
        cost_estimate=pl.CostEstimate(flops=flops, bytes_accessed=moved, transcendentals=0),
    )(bits, *arrays, *deps)


def by_step(*shape):
    return pl.BlockSpec(shape, lambda i, bits: (i,) + (0,) * (len(shape) - 1))


def whole(*shape):
    return pl.BlockSpec(shape, lambda i, bits: (0,) * len(shape))


def scalars():
    return pl.BlockSpec(memory_space=pltpu.SMEM)


SEQS = 4
GROUP = 16
TURNED = (True, None)
PLAN = (
    "do ffn",
    "cross",
    "do ffn",
    "start cross",
    "do cross",
    "do ffn",
    "memory",
    "self",
    "start self",
    "do ffn",
    "do cross",
    "do self",
    "do cross",
    "do ffn",
    "do cross",
    "do self",
    "do ffn",
    "do self",
    "do cross",
    "do ffn",
    "do self",
    "do cross",
    "do self",
    "do self",
    "do ffn",
    "do cross",
    "do self",
    "tokens",
    "do self",
    "do cross",
    "end ffn",
    "end self",
    "end cross",
)


def self_forward(bits, tokens, lengths, gain_self, w_qkv, w_out, gain_cross, w_query, length):
    rows, width = tokens.shape
    n = rows // length
    block = SEQS * length
    row = by_step(block, width)
    return call(
        functools.partial(self_forward_kernel, SEQS, length, width),
        (n // SEQS,), bits,
        [
            (lengths, scalars()), (tokens, row, HBM),
            (gain_self, whole(1, width)), (w_qkv, whole(width, 3 * width), HBM),
            (w_out, whole(width, width), HBM), (gain_cross, whole(1, width)),
            (w_query, whole(width, width), HBM),
        ],
        [
            ((rows, width), bf16, row, HBM),
            ((rows, 3 * width), bf16, by_step(block, 3 * width), HBM),
            ((n, width // PAIR, length, 2 * length), bf16, by_step(SEQS, width // PAIR, length, 2 * length), HBM),
            ((rows, width), bf16, row, HBM),
            ((rows, width), bf16, row, HBM),
            ((rows, width), bf16, row, HBM),
        ],
        flops=12 * rows * width * width,
        limit=36,
    )


def cross_forward(bits, lengths, memory_lengths, raw, queries, mid, grad_output, w_kv, w_out, gain_ffn, length, mem_total):
    rows, width = queries.shape
    n = rows // length
    block = SEQS * length
    mem = SEQS * mem_total
    heads = width // HEAD
    row = by_step(block, width)
    return call(
        functools.partial(cross_forward_kernel, SEQS, length, width, mem_total),
        (n // SEQS,), bits,
        [
            (lengths, scalars()), (memory_lengths, scalars()),
            (raw, whole(*raw.shape)), (queries, row, HBM),
            (mid, row, HBM), (grad_output, row, HBM),
            (w_kv, whole(width, 2 * width)), (w_out, whole(width, width)),
            (gain_ffn, whole(1, width)),
        ],
        [
            ((n * mem_total, width), bf16, by_step(mem, width), HBM),
            ((n * mem_total, 2 * width), bf16, by_step(mem, 2 * width), HBM),
            ((n, heads * mem_total, length), bf16, by_step(SEQS, heads * mem_total, length), HBM),
            ((rows, width), bf16, row, HBM),
            ((rows, width), bf16, row, HBM),
            ((rows, width), bf16, row, HBM),
            ((rows, width), bf16, row, VMEM),
            ((rows, width), bf16, row, VMEM),
            ((rows, width), bf16, row, VMEM),
        ],
        flops=6 * rows * width * width,
        limit=VMEM_LIMIT if mem_total <= 32 else 2 * VMEM_LIMIT,
    )


def feed_forward(bits, act, grad_low, start, w_expand, w_contract, chunk=FF_CHUNK):
    rows, width = act.shape
    hidden = w_expand.shape[1]
    steps = hidden // chunk
    half = steps // 2

    def at(i, bits):
        return lax.rem(i + half * (1 - bits[0]), steps)

    def block(place):
        return pl.BlockSpec((2 * chunk, width), lambda i, bits: (place(i), 0))

    return call(
        functools.partial(ffn_kernel, min(rows, FF_ROWS)),
        (steps,), bits,
        [
            (act, whole(rows, width)), (grad_low, whole(rows, width)), (start, whole(rows, width)),
            (w_expand, pl.BlockSpec((width, chunk), lambda i, bits: (0, at(i, bits)))),
            (w_contract, pl.BlockSpec((chunk, width), lambda i, bits: (at(i, bits), 0))),
        ],
        [
            ((rows, width), bf16, whole(rows, width), HBM),
            ((rows, width), bf16, whole(rows, width), HBM),
            ((hidden, width), bf16, block(lambda i: jnp.minimum(i, half - 1)), HBM),
            ((hidden, width), bf16, block(lambda i: jnp.maximum(i - half, 0)), HBM),
        ],
        [
            pltpu.VMEM((rows, chunk), bf16),
            pltpu.VMEM((rows, chunk), bf16),
            pltpu.VMEM((rows, width), f32),
            pltpu.VMEM((rows, width), f32),
        ],
        flops=12 * rows * width * hidden,
        limit=FF_LIMIT,
    )


def cross_backward(bits, grad_normed, late, grad_low, cross, weights, pairs, queries, mid, arrived, attended, w_out, w_query, w_kv, gain_ffn, gain_cross, length, mem_total, deps=()):
    rows, width = queries.shape
    far = [
        grad_normed, late, grad_low, cross, weights, pairs, queries, mid, arrived, attended,
        w_out, w_query, w_kv,
    ]
    anywhere = pl.BlockSpec(memory_space=pl.ANY)
    return call(
        functools.partial(cross_backward_kernel, length, mem_total),
        (1,), bits,
        [(a, anywhere, HBM) for a in far]
        + [(gain_ffn, whole(1, width)), (gain_cross, whole(1, width))],
        [
            ((rows, width), bf16, anywhere, HBM),
            (arrived.shape, bf16, whole(*arrived.shape), HBM),
            ((5 * width // 2, width), bf16, whole(5 * width // 2, width), HBM),
            ((5 * width // 2, width), bf16, whole(5 * width // 2, width), HBM),
        ],
        [pltpu.VMEM(a.shape, bf16) for a in far]
        + [
            pltpu.VMEM((rows, width), f32),
            pltpu.VMEM((rows, width), bf16),
            pltpu.VMEM((rows, width), bf16),
            pltpu.VMEM(pairs.shape, bf16),
            pltpu.SemaphoreType.DMA((32,)),
        ],
        flops=14 * rows * width * width,
        deps=deps,
        limit=48 if mem_total <= 32 else 62,
    )


def self_backward(bits, gradient, triple, weights, act, w_out, length, deps=()):
    rows, width = gradient.shape
    far = [gradient, triple, weights, act, w_out]
    anywhere = pl.BlockSpec(memory_space=pl.ANY)
    return call(
        functools.partial(self_backward_kernel, length),
        (1,), bits,
        [(a, anywhere, HBM) for a in far],
        [
            (triple.shape, bf16, anywhere, HBM),
            ((3 * width // 2, width), bf16, whole(3 * width // 2, width), HBM),
            ((3 * width // 2, width), bf16, whole(3 * width // 2, width), HBM),
        ],
        [pltpu.VMEM(a.shape, bf16) for a in far]
        + [pltpu.VMEM(triple.shape, bf16), pltpu.SemaphoreType.DMA((24,))],
        flops=14 * rows * width * width,
        deps=deps,
        limit=44,
    )


def token_gradient(bits, gradient, grad_triple, tokens, w_qkv, gain_self, deps=()):
    rows, width = tokens.shape
    block = TOKEN_ROWS
    row = by_step(block, width)
    return call(
        grad_tokens_kernel, (rows // block,), bits,
        [
            (gradient, row, HBM), (grad_triple, by_step(block, 3 * width), HBM), (tokens, row, HBM),
            (w_qkv, whole(width, 3 * width), HBM), (gain_self, whole(1, width)),
        ],
        [((rows, width), bf16, row)],
        flops=6 * rows * width * width,
        deps=deps,
    )[0]


def after(arrays, deps):
    if not deps:
        return arrays
    return lax.optimization_barrier((*arrays, *deps))[: len(arrays)]


def added(left, right):
    return (left.astype(f32) + right.astype(f32)).astype(bf16)


def exchange(block, bit, devices):
    return lax.ppermute(block, "dp", [(i, i ^ (1 << bit)) for i in range(devices)])


class Lane:
    def __init__(self, devices, orders, send, keep):
        self.devices, self.orders, self.count = devices, orders, len(orders)
        self.rest = list(range(4, devices.bit_length() - 1))
        self.level, self.state = 0, "halve"
        self.own = self.parted(keep)
        self.got = self.parted(exchange(send, 0, devices))
        self.token = send

    def parted(self, block):
        size = block.shape[0] // self.count
        return [block[n * size : (n + 1) * size] for n in range(self.count)]

    def send(self, blocks):
        self.token = blocks[0]
        if self.level in (1, 2):
            bits = [order[self.level - 1] for order in self.orders]
            self.got = [exchange(b, bit, self.devices) for b, bit in zip(blocks, bits)]
        else:
            bit = {0: 0, 3: 3}.get(self.level, self.level)
            whole_block = jnp.concatenate(blocks) if len(blocks) > 1 else blocks[0]
            self.token = whole_block
            self.got = self.parted(exchange(whole_block, bit, self.devices))

    def advance(self, deps=()):
        both = after((*self.own, *self.got), deps)
        own, got = both[: self.count], both[self.count :]
        if self.state == "halve":
            half = own[0].shape[0] // 2
            self.own = [added(a[half:], b[half:]) for a, b in zip(own, got)]
            self.level += 1
            self.send([added(a[:half], b[:half]) for a, b in zip(own, got)])
            if self.level == 3:
                self.state = "whole"
        elif self.state == "whole":
            self.own = [added(a, b) for a, b in zip(own, got)]
            if self.rest:
                self.level = self.rest.pop(0)
            else:
                self.level, self.state = 3, "join"
            self.send(self.own)
        else:
            self.own = [jnp.concatenate([b, a]) for a, b in zip(own, got)]
            self.level -= 1
            self.send(self.own)
            if self.level == 0:
                self.state = "done"

    def result(self):
        return [blocks[0] if self.count == 1 else jnp.concatenate(blocks) for blocks in (self.own, self.got)]


def ffn_final(bits, own, got, w_expand, gain, brought, deps=(), chunk=512):
    width, hidden = w_expand.shape
    steps = hidden // chunk
    part = by_step(brought.shape[0] // steps, width)

    def source(mine):
        def at(i, bits):
            first = (bits[0] == 0) == mine
            return (jnp.where(first, jnp.minimum(i, steps // 2 - 1), jnp.maximum(i - steps // 2, 0)), 0)

        return pl.BlockSpec((2 * chunk, width), at)

    return call(
        ffn_final_kernel, (steps,), bits,
        [
            (own, source(True)), (got, source(False)),
            (w_expand, pl.BlockSpec((width, chunk), lambda i, bits: (0, i))),
            (gain, whole(1, width)), (brought, part, HBM),
        ],
        [
            ((hidden, width), f32, by_step(chunk, width)),
            ((width, hidden), f32, pl.BlockSpec((width, chunk), lambda i, bits: (0, i))),
            ((1, width), f32, whole(1, width)),
            (brought.shape, bf16, part, HBM),
        ],
        [pltpu.VMEM((2 * chunk, width), bf16)],
        deps=deps,
    )


def cross_final(bits, own, got, w_query, gain, deps=()):
    width = w_query.shape[0]
    half = width // 2
    part = by_step(half, width)
    column = pl.BlockSpec((1, half), lambda i, bits: (0, i))
    return call(
        cross_final_kernel, (2,), bits,
        [
            (own, whole(*own.shape)), (got, whole(*own.shape)), (w_query, part), (gain, column),
        ],
        [
            ((width, width), f32, part), ((width, width), f32, part),
            ((width, 2 * width), f32, by_step(half, 2 * width)), ((width, width), f32, part),
            ((1, width), f32, column),
        ],
        [pltpu.VMEM(own.shape, bf16)],
        deps=deps,
    )


def self_final(bits, own, got, w_qkv, gain, deps=()):
    width = w_qkv.shape[0]
    half = width // 2
    column = pl.BlockSpec((1, half), lambda i, bits: (0, i))
    return call(
        self_final_kernel, (2,), bits,
        [
            (own, whole(*own.shape)), (got, whole(*own.shape)),
            (w_qkv, by_step(half, 3 * width)), (gain, column),
        ],
        [((width, 3 * width), f32, by_step(half, 3 * width)), ((1, width), f32, column)],
        [pltpu.VMEM(own.shape, bf16)],
        deps=deps,
    )


def local(
    devices, tokens, memory, target_lengths, memory_lengths, grad_output,
    gain_self, w_qkv, w_self_out, gain_cross, w_cross_query, w_cross_kv, w_cross_out,
    gain_ffn, w_expand, w_contract,
):
    seq_count, length, width = tokens.shape
    rows = seq_count * length
    gain_self, gain_cross, gain_ffn = gain_self[None], gain_cross[None], gain_ffn[None]
    flat_tokens = tokens.reshape(rows, width)
    me = lax.axis_index("dp")
    bits = jnp.stack([(me >> b) & 1 for b in range(devices.bit_length() - 1)]).astype(jnp.int32)
    raw = lax.all_to_all(
        memory.reshape(devices, -1, width), "dp", split_axis=0, concat_axis=0, tiled=True
    ).reshape(-1, width)
    mem_total = raw.shape[0] // seq_count
    act_one, triple, self_weights, attended, mid, queries = self_forward(
        bits, flat_tokens, target_lengths, gain_self, w_qkv, w_self_out, gain_cross, w_cross_query, length
    )
    arrived, pairs, cross_weights, cross, late, grad_low, late_near, grad_low_near, act = cross_forward(
        bits, target_lengths, memory_lengths, raw, queries, mid, grad_output.reshape(rows, width),
        w_cross_kv, w_cross_out, gain_ffn, length, mem_total,
    )
    output, grad_normed, send, keep = feed_forward(
        bits, act, grad_low_near, late_near, w_expand, w_contract
    )
    straight, turned = (1, 2), (2, 1)
    lanes = {"ffn": Lane(devices, (straight, turned), send, keep)}
    token, fresh, kept, found = send, {}, {}, {}
    for n, name in enumerate(PLAN):
        deps = [token]
        if PLAN[n - 1] == "self":
            deps.append(grad_memory)
        if name.startswith("end"):
            lane = lanes[name[4:]]
            while lane.state != "done":
                lane.advance(deps)
                deps = [lane.token]
        if name == "cross":
            gradient, grad_arrived, send, keep = cross_backward(
                bits, grad_normed, late, grad_low, cross, cross_weights, pairs, queries, mid, arrived,
                attended, w_cross_out, w_cross_query, w_cross_kv, gain_ffn, gain_cross, length, mem_total,
                deps=deps,
            )
            token = fresh["cross"] = send
            kept["cross"] = keep
        elif name == "self":
            grad_triple, send, keep = self_backward(
                bits, gradient, triple, self_weights, act_one, w_self_out, length, deps=deps
            )
            token = fresh["self"] = send
            kept["self"] = keep
        elif name == "tokens":
            token = grad_tokens = token_gradient(
                bits, gradient, grad_triple, flat_tokens, w_qkv, gain_self, deps=deps
            )
        elif name == "memory":
            grad_memory = lax.all_to_all(
                after((grad_arrived,), deps)[0].reshape(devices, -1, width),
                "dp", split_axis=0, concat_axis=0, tiled=True,
            ).reshape(-1, width)
        elif name in ("start cross", "start self"):
            name = name[6:]
            order = turned if TURNED[name == "self"] else straight
            lanes[name] = Lane(devices, (order,), after((fresh[name],), deps)[0], kept[name])
        elif name == "end ffn":
            own, got = lanes["ffn"].result()
            found["ffn"] = ffn_final(bits, own, got, w_expand, gain_ffn, grad_memory, deps=deps)
            token = found["ffn"][2]
        elif name == "end cross":
            own, got = lanes["cross"].result()
            found["cross"] = cross_final(bits, own, got, w_cross_query, gain_cross, deps=deps)
            token = found["cross"][4]
        elif name == "end self":
            own, got = lanes["self"].result()
            found["self"] = self_final(bits, own, got, w_qkv, gain_self, deps=deps)
            token = found["self"][1]
        else:
            lane = lanes[name[3:]]
            if lane.state != "done":
                lane.advance(deps)
                token = lane.token
    grad_contract, grad_expand, grad_gain_ffn, grad_memory = found["ffn"]
    grad_cross_out, grad_cross_query, grad_cross_kv, grad_self_out, grad_gain_cross = found["cross"]
    grad_qkv, grad_gain_self = found["self"]
    return (
        output.reshape(tokens.shape),
        grad_tokens.reshape(tokens.shape),
        grad_memory.reshape(memory.shape),
        grad_gain_self[0],
        grad_qkv,
        grad_self_out,
        grad_gain_cross[0],
        grad_cross_query,
        grad_cross_kv,
        grad_cross_out,
        grad_gain_ffn[0],
        grad_expand,
        grad_contract,
    )


def solution(mesh):
    rows, columns, copied = P("dp", None, None), P(None, "dp", None), P()
    return jax.shard_map(
        functools.partial(local, mesh.shape["dp"]),
        mesh=mesh,
        in_specs=(rows, columns, P("dp"), P("dp"), rows) + (copied,) * 10,
        out_specs=(rows, rows, columns) + (copied,) * 10,
        check_vma=False,
    )
```
